32 devices in a mesh: dp: 16 (over z, y, x), feat: 2 (over core).
Axes of the slice: x: 2, y: 2, z: 4, core: 2. Of those that a mesh axis runs over, the one named last changes fastest.
Arguments:
- teacher: bfloat16 [2048, 1024], P('dp'), may hold values from -6 to 6
- student: bfloat16 [2048, 768], P('dp'), may hold values from -6 to 6
- head: bfloat16 [768, 1024], P(None, 'feat'), may hold values from -0.21875 to 0.21875
- freqs: bfloat16 [1024, 2048], P(None, 'feat'), may hold values from -0.1875 to 0.1875
- labels: int32 [2048], P('dp'), may hold values from 0 to 5455, as said below
- class_slot: int32 [5456], replicated, may hold values from 0 to 5455, as said below
Outputs:
- head_grad: float32 [1024, 768], P(('dp', 'feat'))
- class_loss: float32 [5456], P('dp')
The draws below stay inside these ranges and needn't reach their ends.
Inputs may be any that keep to these rules, and one draw needn't show every extreme that they name: class_slot is a permutation of the classes. Of the 128 labels of one dp index, at most 16 have class_slot[label] // 341 equal to any one dp index; for one dp index that bound is reached from every dp index.
All inputs are finite; a program needn't handle non-finite values.
Results may differ from the reference program's by a relative error of at most 0.005.
Values may be sent and summed in bfloat16 or wider, within the bound.
No kernel may reach another device: no remote copies, remote signals or barrier semaphores. Data moves between devices by JAX's collectives and lax.ppermute only.
A program may use at most 64 MiB of HBM per device.

```python
import jax
import jax.numpy as jnp
from jax import lax

D_T = 1024
D_S = 768
FREQ = 2048
CLS_DEV = 341
IMG_DEV = 128
CAP = 16
IMAGES = 2048
CLASSES = 5456


def slot_table(key):
    return jax.random.permutation(jax.random.fold_in(key, 11), CLASSES).astype(jnp.int32)


def draw_class_slot(key, part):
    return slot_table(key)


def draw_labels(key, part):
    groups = IMAGES // IMG_DEV
    table = slot_table(key)
    inverse = jnp.zeros((CLASSES,), jnp.int32).at[table].set(jnp.arange(CLASSES, dtype=jnp.int32))
    hottest = jax.random.randint(jax.random.fold_in(key, 12), (), 0, groups).astype(jnp.int32)

    def one_group(group_key):
        keys = jax.random.split(group_key, 4)
        spare = jax.random.permutation(keys[0], (groups - 1) * CAP).astype(jnp.int32)[:IMG_DEV - CAP]
        others = spare // CAP
        others = jnp.where(others >= hottest, others + 1, others)
        owners = jnp.concatenate([jnp.full((CAP,), hottest, jnp.int32), others])
        order = jax.random.permutation(keys[1], IMG_DEV).astype(jnp.int32)
        owners = owners[order]
        first = jax.random.randint(keys[2], (IMG_DEV,), 0, CLS_DEV).astype(jnp.int32)
        second = jax.random.randint(keys[3], (IMG_DEV,), 0, CLS_DEV).astype(jnp.int32)
        local = first * second // CLS_DEV
        return inverse[owners * CLS_DEV + local]
    group_keys = jax.random.split(jax.random.fold_in(key, 13), groups)
    return jax.vmap(one_group)(group_keys).reshape(IMAGES)


def shard_levels(rng, extent, cuts, least, top_value):
    level = 1.0
    for position, parts in cuts:
        heights = jax.random.uniform(jax.random.fold_in(jax.random.fold_in(rng, 6), position), (parts,), jnp.float32, least / len(cuts), top_value / len(cuts))
        level = level * jnp.repeat(jnp.exp(heights), extent[position] // parts).reshape((-1,) + (1,) * (len(extent) - 1 - position))
    return level


def normal_values(own_key, dims, spread, most, cuts=(), kind=jnp.bfloat16):
    factor_of = shard_levels(own_key, dims, cuts, -0.22, 0.18) if cuts else 1.0
    drawn = jax.random.normal(own_key, dims, jnp.float32) * spread * factor_of
    return jnp.minimum(jnp.maximum(drawn, -most), most).astype(kind)


def setup_inputs(seed: int = 0) -> dict:
    seeds = jax.random.split(jax.random.key(seed), 7)
    return {
        "teacher": normal_values(seeds[0], (IMAGES, D_T), 1.0, 6.0, ((0, 16),)),
        "student": normal_values(seeds[1], (IMAGES, D_S), 1.0, 6.0, ((0, 16),)),
        "head": normal_values(seeds[2], (D_S, D_T), D_S ** -0.5, 0.21875, ((1, 2),)),
        "freqs": normal_values(seeds[3], (D_T, FREQ), D_T ** -0.5, 0.1875, ((1, 2),)),
        "labels": draw_labels(jax.random.fold_in(seeds[6], 71), 0),
        "class_slot": draw_class_slot(jax.random.fold_in(seeds[6], 71), 0),
    }


def reference(teacher, student, head, freqs, labels, class_slot):
    projected = jnp.dot(student, head, preferred_element_type=jnp.float32).astype(jnp.bfloat16)
    student_z = jnp.dot(projected, freqs, preferred_element_type=jnp.float32)
    teacher_z = jnp.dot(teacher, freqs, preferred_element_type=jnp.float32)
    delta = jnp.concatenate([jnp.cos(student_z) - jnp.cos(teacher_z), jnp.sin(student_z) - jnp.sin(teacher_z)], axis=1)
    sums = jax.ops.segment_sum(delta, labels, num_segments=CLASSES)
    counts = jax.ops.segment_sum(jnp.ones(labels.shape, jnp.float32), labels, num_segments=CLASSES)
    floor_counts = jnp.maximum(counts, 1.0)
    means = sums / floor_counts[:, None]
    per_class = lax.optimization_barrier(jnp.sum(sums * sums, axis=1)) / floor_counts / (2.0 * FREQ)
    class_loss = jnp.zeros((CLASSES,), jnp.float32).at[class_slot].set(per_class)
    picked = jnp.take(means, labels, axis=0)
    grad_z = (-jnp.sin(student_z) * picked[:, :FREQ] + jnp.cos(student_z) * picked[:, FREQ:]).astype(jnp.bfloat16)
    grad_u = jnp.dot(grad_z, freqs.T, preferred_element_type=jnp.float32)
    head_grad = jnp.dot(grad_u.T, student.astype(jnp.float32), precision=lax.Precision.HIGHEST)
    head_grad = head_grad / jnp.sqrt(jnp.float32(IMAGES))
    return (head_grad, class_loss)
```

```python
import functools
import math

import jax
import jax.numpy as jnp
from jax import lax
from jax.experimental import pallas as pl
from jax.experimental.pallas import tpu as pltpu
from jax.sharding import PartitionSpec as P

LANES = 128
TURN = 1.0 / (2.0 * math.pi)
ROUNDER = 1.5 * 2.0**23
SINE = (
    6.283185160088887,
    -41.34165503126523,
    81.60100406312206,
    -76.54978204660544,
    39.5367040910771,
)


def up_to(value, multiple):
    return -(-value // multiple) * multiple


def quarter_sine(turns):
    part = turns - ((turns + ROUNDER) - ROUNDER)
    angle = 0.25 - jnp.abs(part)
    square = angle * angle
    value = jnp.float32(SINE[4])
    for factor in SINE[3::-1]:
        value = value * square + factor
    return value * angle


def cos_sin(z):
    turns = z * TURN
    return quarter_sine(turns), quarter_sine(turns - 0.25)


def to_row(column, size):
    first = lax.broadcasted_iota(jnp.int32, (size, size), 0)
    second = lax.broadcasted_iota(jnp.int32, (size, size), 1)
    return jnp.sum(jnp.where(first == second, column, 0.0), axis=0, keepdims=True)


def to_column(row, size):
    first = lax.broadcasted_iota(jnp.int32, (size, size), 0)
    second = lax.broadcasted_iota(jnp.int32, (size, size), 1)
    return jnp.sum(jnp.where(first == second, row, 0.0), axis=1, keepdims=True)


def route_kernel(cls_dev, capacity, labels, table, teacher, student, out, rows):
    images = teacher.shape[0]
    slots, width = out.shape
    d_t, d_s = teacher.shape[1], student.shape[1]
    label = to_column(labels[...].astype(jnp.float32), images)
    lane = lax.broadcasted_iota(jnp.int32, (images, LANES), 1)
    lane_f = lane.astype(jnp.float32)
    label = jnp.broadcast_to(label, (images, LANES))
    found = jnp.zeros((images, LANES), jnp.float32)
    for chunk in range(table.shape[0]):
        entry = table[chunk : chunk + 1, :].astype(jnp.float32)
        found += jnp.where(lane_f + float(chunk * LANES) == label, entry, 0.0)
    position = jnp.sum(found, axis=1, keepdims=True)
    owner = jnp.floor((position + 0.5) * (1.0 / cls_dev))
    tag = position - owner * cls_dev + 1.0
    owner_row = to_row(owner, images)
    first = lax.broadcasted_iota(jnp.int32, (images, images), 0)
    second = lax.broadcasted_iota(jnp.int32, (images, images), 1)
    before = jnp.logical_and(first < second, owner == owner_row)
    rank = jnp.sum(jnp.where(before, 1.0, 0.0), axis=0, keepdims=True)
    slot = owner_row * float(capacity) + rank
    slot_id = lax.broadcasted_iota(jnp.int32, (slots, images), 0).astype(jnp.float32)
    pick = jnp.where(slot_id == slot, 1.0, 0.0).astype(jnp.bfloat16)
    high = jnp.floor(tag * (1.0 / 32.0))
    tags = jnp.where(lane == 0, high, jnp.where(lane == 1, tag - 32.0 * high, 0.0))
    rows[:, :d_t] = teacher[...]
    rows[:, d_t : d_t + d_s] = student[...]
    rows[:, d_t + d_s : d_t + d_s + LANES] = tags.astype(jnp.bfloat16)
    rows[:, d_t + d_s + LANES :] = jnp.zeros(
        (images, rows.shape[1] - d_t - d_s - LANES), jnp.bfloat16
    )
    start = pl.multiple_of(lax.axis_index("feat") * width, LANES)
    out[...] = jnp.dot(
        pick, rows[:, pl.ds(start, width)], preferred_element_type=jnp.float32
    ).astype(jnp.bfloat16)


def class_kernel(n_feat, n_dp, cls_pad, d_t, d_s, permuted, *refs):
    parts, heads = refs[:n_feat], refs[n_feat : 2 * n_feat]
    freqs, picked_rows = refs[2 * n_feat], refs[2 * n_feat + 1]
    grads, norms, student, rows, projected, grad_z, weight = refs[2 * n_feat + 2 :]
    feat = lax.axis_index("feat")
    slots, width = parts[0].shape
    half = freqs.shape[1]
    for offset in range(n_feat):
        index = lax.rem(feat + (n_feat - offset), n_feat)
        rows[:, pl.ds(pl.multiple_of(index * width, LANES), width)] = parts[offset][...]
    s_rows = rows[:, d_t : d_t + d_s]
    student[...] = s_rows
    part = d_t // n_feat
    for offset in range(n_feat):
        index = lax.rem(feat + (n_feat - offset), n_feat)
        projected[:, pl.ds(pl.multiple_of(index * part, LANES), part)] = jnp.dot(
            s_rows, heads[offset][...], preferred_element_type=jnp.float32
        ).astype(jnp.bfloat16)
    tags = rows[:, d_t + d_s : d_t + d_s + LANES].astype(jnp.float32)
    lane = lax.broadcasted_iota(jnp.int32, (slots, LANES), 1)
    tag = jnp.sum(
        tags * jnp.where(lane == 0, 32.0, jnp.where(lane == 1, 1.0, 0.0)), axis=1, keepdims=True
    )
    tag_row = to_row(tag, slots)
    same = jnp.where(jnp.logical_and(tag == tag_row, tag > 0.0), 1.0, 0.0)
    inverse = 1.0 / jnp.maximum(jnp.sum(same, axis=1, keepdims=True), 1.0)
    same = same.astype(jnp.bfloat16)
    step = min(half, 256)
    norm = jnp.zeros((slots, 1), jnp.float32)
    for column in range(0, half, step):
        block = slice(column, column + step)
        student_z = jnp.dot(
            projected[...], freqs[:, block], preferred_element_type=jnp.float32
        )
        teacher_z = jnp.dot(
            rows[:, :d_t], freqs[:, block], preferred_element_type=jnp.float32
        )
        cos_s, sin_s = cos_sin(student_z)
        cos_t, sin_t = cos_sin(teacher_z)
        mean_c = inverse * jnp.dot(
            same, (cos_s - cos_t).astype(jnp.bfloat16), preferred_element_type=jnp.float32
        )
        mean_s = inverse * jnp.dot(
            same, (sin_s - sin_t).astype(jnp.bfloat16), preferred_element_type=jnp.float32
        )
        norm += jnp.sum(mean_c * mean_c + mean_s * mean_s, axis=1, keepdims=True)
        grad_z[:, block] = (cos_s * mean_s - sin_s * mean_c).astype(jnp.bfloat16)
    cls = lax.broadcasted_iota(jnp.int32, (slots, cls_pad), 1).astype(jnp.float32) + 1.0
    norms[...] = jnp.sum(jnp.where(cls == tag, norm, 0.0), axis=0, keepdims=True)
    out_rows = d_t // (n_dp * n_feat)
    for offset in range(n_feat):
        index = lax.rem(feat + offset, n_feat)
        if permuted:
            source = picked_rows[index]
        else:
            for group in range(n_dp):
                start = pl.multiple_of((group * n_feat + index) * out_rows, out_rows)
                weight[group * out_rows : (group + 1) * out_rows, :] = freqs[
                    pl.ds(start, out_rows), :
                ]
            source = weight[...]
        grads[offset] = lax.dot_general(
            source, grad_z[...], (((1,), (1,)), ((), ())), preferred_element_type=jnp.float32
        ).astype(jnp.bfloat16)


def head_kernel(n_feat, divisor, *refs):
    grads, norms = refs[:n_feat], refs[n_feat : 2 * n_feat]
    student, head, loss = refs[2 * n_feat :]
    total, norm = grads[0][0].astype(jnp.float32), norms[0][...]
    for offset in range(1, n_feat):
        total += grads[offset][...].astype(jnp.float32)
        norm += norms[offset][...]
    head[...] = jnp.dot(
        total.astype(jnp.bfloat16), student[...], preferred_element_type=jnp.float32
    ).astype(jnp.bfloat16)
    loss[...] = (norm * (1.0 / divisor))[:, : loss.shape[1]]


def on_device(teacher, student, head, freqs, labels, class_slot):
    n_dp = lax.axis_size("dp")
    n_feat = lax.axis_size("feat")
    images, d_t = teacher.shape
    d_s = student.shape[1]
    half = freqs.shape[1]
    classes = class_slot.shape[0]
    cls_dev = classes // n_dp
    cls_pad = up_to(cls_dev, LANES)
    capacity = 2 * images // n_dp
    slots = n_dp * capacity
    width = up_to(d_t + d_s + LANES, LANES * n_feat) // n_feat
    out_rows = d_t // (n_dp * n_feat)
    permuted = out_rows % 16 != 0
    vmem = pltpu.CompilerParams(vmem_limit_bytes=32 * 2**20)

    def shifted(value, offset):
        return lax.ppermute(
            value, "feat", [(i, (i + offset) % n_feat) for i in range(n_feat)]
        )

    heads = [head] + [shifted(head, k) for k in range(1, n_feat)]
    table = jnp.pad(class_slot, (0, up_to(classes, 8 * LANES) - classes)).reshape(-1, LANES)
    sent = pl.pallas_call(
        functools.partial(route_kernel, cls_dev, capacity),
        out_shape=jax.ShapeDtypeStruct((slots, width), jnp.bfloat16),
        scratch_shapes=[pltpu.VMEM((images, width * n_feat), jnp.bfloat16)],
        compiler_params=vmem,
        name="route",
    )(labels.reshape(1, images), table, teacher, student)
    mine = lax.all_to_all(
        sent.reshape(n_dp, capacity, width), "dp", split_axis=0, concat_axis=0, tiled=True
    ).reshape(slots, width)
    parts = [mine] + [shifted(mine, k) for k in range(1, n_feat)]
    if permuted:
        picked = jnp.swapaxes(freqs.reshape(n_dp, n_feat, out_rows, half), 0, 1)
        picked = picked.reshape(n_feat, n_dp * out_rows, half)
    else:
        picked = jnp.zeros((8, LANES), jnp.bfloat16)
    grads, norms, s_rows = pl.pallas_call(
        functools.partial(class_kernel, n_feat, n_dp, cls_pad, d_t, d_s, permuted),
        out_shape=(
            jax.ShapeDtypeStruct((n_feat, n_dp * out_rows, slots), jnp.bfloat16),
            jax.ShapeDtypeStruct((1, cls_pad), jnp.float32),
            jax.ShapeDtypeStruct((slots, d_s), jnp.bfloat16),
        ),
        scratch_shapes=[
            pltpu.VMEM((slots, width * n_feat), jnp.bfloat16),
            pltpu.VMEM((slots, d_t), jnp.bfloat16),
            pltpu.VMEM((slots, half), jnp.bfloat16),
            pltpu.VMEM((n_dp * out_rows, half), jnp.bfloat16),
        ],
        compiler_params=vmem,
        name="classes",
    )(*parts, *heads, freqs, picked)
    all_grads = [grads] + [shifted(grads[k], k) for k in range(1, n_feat)]
    all_norms = [norms] + [shifted(norms, k) for k in range(1, n_feat)]
    partial_head, loss = pl.pallas_call(
        functools.partial(head_kernel, n_feat, 2.0 * half * n_feat),
        out_shape=(
            jax.ShapeDtypeStruct((n_dp * out_rows, d_s), jnp.bfloat16),
            jax.ShapeDtypeStruct((1, cls_dev), jnp.float32),
        ),
        compiler_params=vmem,
        name="head",
    )(*all_grads, *all_norms, s_rows)
    received = lax.all_to_all(
        partial_head.reshape(n_dp, out_rows, d_s), "dp", split_axis=0, concat_axis=0, tiled=True
    )
    scale = 1.0 / math.sqrt(images * n_dp)
    head_grad = jnp.sum(received.astype(jnp.float32), axis=0) * scale
    return (head_grad, loss.reshape(cls_dev))


def solution(mesh):
    in_specs = (P("dp", None), P("dp", None), P(None, "feat"), P(None, "feat"), P("dp"), P())
    out_specs = (P(("dp", "feat"), None), P("dp"))
    return jax.shard_map(
        on_device, mesh=mesh, in_specs=in_specs, out_specs=out_specs, check_vma=False
    )
```

```python
import functools
import math

import jax
import jax.numpy as jnp
from jax import lax
from jax.experimental import pallas as pl
from jax.experimental.pallas import tpu as pltpu
from jax.sharding import PartitionSpec as P

LANES = 128
TURN = 1.0 / (2.0 * math.pi)
ROUNDER = 1.5 * 2.0**23
SINE = (6.283164044217864, -41.337142357601536, 81.3407683703199, -70.9934277613874)


def up_to(value, multiple):
    return -(-value // multiple) * multiple


def quarter_sine(angle):
    square = angle * angle
    value = jnp.float32(SINE[-1])
    for factor in SINE[-2::-1]:
        value = value * square + factor
    return value * angle


def cos_sin(z):
    turns = z * TURN
    part = turns - ((turns + ROUNDER) - ROUNDER)
    wave = jnp.minimum(jnp.maximum(part, -0.5 - part), 0.5 - part)
    return quarter_sine(0.25 - jnp.abs(part)), quarter_sine(wave)


def to_row(column, size):
    first = lax.broadcasted_iota(jnp.int32, (size, size), 0)
    second = lax.broadcasted_iota(jnp.int32, (size, size), 1)
    return jnp.sum(jnp.where(first == second, column, 0.0), axis=0, keepdims=True)


def to_column(row, size):
    first = lax.broadcasted_iota(jnp.int32, (size, size), 0)
    second = lax.broadcasted_iota(jnp.int32, (size, size), 1)
    return jnp.sum(jnp.where(first == second, row, 0.0), axis=1, keepdims=True)


def table_entries(table, chunk):
    start = chunk * LANES
    size = min(LANES, table.shape[0] - start)
    entries = table[pl.ds(start, size)].astype(jnp.float32)
    if size < LANES:
        entries = jnp.concatenate([entries, jnp.zeros((LANES - size,), jnp.float32)])
    return entries.reshape(1, LANES)


def route_kernel(
    cls_dev, capacity, labels_in, table_in, teacher, student, out, token, labels, table, rows, sems
):
    images, d_t = teacher.shape
    d_s = student.shape[1]
    slots, width = out.shape
    copies = [
        pltpu.make_async_copy(labels_in, labels, sems.at[0]),
        pltpu.make_async_copy(table_in, table, sems.at[1]),
        pltpu.make_async_copy(teacher, rows.at[:, :d_t], sems.at[2]),
        pltpu.make_async_copy(student, rows.at[:, d_t : d_t + d_s], sems.at[3]),
    ]
    for copy in copies:
        copy.start()
    lane = lax.broadcasted_iota(jnp.int32, (images, LANES), 1)
    lane_f = lane.astype(jnp.float32)
    copies[0].wait()
    label = to_column(labels[...].astype(jnp.float32).reshape(1, images), images)
    label = jnp.broadcast_to(label, (images, LANES))
    copies[1].wait()
    found = jnp.zeros((images, LANES), jnp.float32)
    for chunk in range(pl.cdiv(table.shape[0], LANES)):
        entries = table_entries(table, chunk)
        found += jnp.where(lane_f + float(chunk * LANES) == label, entries, 0.0)
    position = jnp.sum(found, axis=1, keepdims=True)
    owner = jnp.floor((position + 0.5) * (1.0 / cls_dev))
    tag = position - owner * cls_dev + 1.0
    owner_row = to_row(owner, images)
    first = lax.broadcasted_iota(jnp.int32, (images, images), 0)
    second = lax.broadcasted_iota(jnp.int32, (images, images), 1)
    before = jnp.logical_and(first < second, owner == owner_row)
    rank = jnp.sum(jnp.where(before, 1.0, 0.0), axis=0, keepdims=True)
    slot = owner_row * float(capacity) + rank
    slot_id = lax.broadcasted_iota(jnp.int32, (slots, images), 0).astype(jnp.float32)
    pick = jnp.where(slot_id == slot, 1.0, 0.0).astype(jnp.bfloat16)
    high = jnp.floor(tag * (1.0 / 32.0))
    tags = jnp.where(lane == 0, high, jnp.where(lane == 1, tag - 32.0 * high, 0.0))
    rows[:, d_t + d_s : d_t + d_s + LANES] = tags.astype(jnp.bfloat16)
    rows[:, d_t + d_s + LANES :] = jnp.zeros(
        (images, rows.shape[1] - d_t - d_s - LANES), jnp.bfloat16
    )
    token[...] = jnp.zeros_like(token)
    copies[2].wait()
    copies[3].wait()
    start = pl.multiple_of(lax.axis_index("feat") * width, LANES)
    out[...] = jnp.dot(
        pick, rows[:, pl.ds(start, width)], preferred_element_type=jnp.float32
    ).astype(jnp.bfloat16)


def load_kernel(head_in, freqs_in, _, head, freqs, sems):
    copies = [
        pltpu.make_async_copy(head_in, head, sems.at[0]),
        pltpu.make_async_copy(freqs_in, freqs, sems.at[1]),
    ]
    for copy in copies:
        copy.start()
    for copy in copies:
        copy.wait()


def class_kernel(n_feat, n_dp, pair, cls_pad, d_t, d_s, permuted, *refs):
    parts, heads, refs = refs[:n_feat], refs[n_feat : 2 * n_feat], refs[2 * n_feat :]
    freqs, refs = refs[0], refs[1:]
    if permuted:
        weights, refs = refs[0], refs[1:]
    grads, refs = refs[:n_feat], refs[n_feat:]
    norms, student, rows, projected, grad_z, picked, near, sems = refs
    feat = lax.axis_index("feat")
    side = lax.rem(lax.axis_index("dp"), pair)
    copies = [
        pltpu.make_async_copy(heads[k], near.at[k - 1], sems.at[k - 1]) for k in range(1, n_feat)
    ]
    for copy in copies:
        copy.start()
    slots, width = parts[0].shape
    half = freqs.shape[1]
    for offset in range(n_feat):
        index = lax.rem(feat + (n_feat - offset), n_feat)
        rows[:, pl.ds(pl.multiple_of(index * width, LANES), width)] = parts[offset][...]
    s_rows = rows[:, d_t : d_t + d_s]
    student[...] = s_rows
    tags = rows[:, d_t + d_s : d_t + d_s + LANES].astype(jnp.float32)
    lane = lax.broadcasted_iota(jnp.int32, (slots, LANES), 1)
    tag = jnp.sum(
        tags * jnp.where(lane == 0, 32.0, jnp.where(lane == 1, 1.0, 0.0)), axis=1, keepdims=True
    )
    tag_row = to_row(tag, slots)
    same = jnp.where(jnp.logical_and(tag == tag_row, tag > 0.0), 1.0, 0.0)
    inverse = 1.0 / jnp.maximum(jnp.sum(same, axis=1, keepdims=True), 1.0)
    same = same.astype(jnp.bfloat16)
    part = d_t // n_feat
    for offset in range(n_feat):
        if offset:
            copies[offset - 1].wait()
        weight = near[offset - 1] if offset else heads[0][...]
        index = lax.rem(feat + (n_feat - offset), n_feat)
        projected[:, pl.ds(pl.multiple_of(index * part, LANES), part)] = jnp.dot(
            s_rows, weight, preferred_element_type=jnp.float32
        ).astype(jnp.bfloat16)
    step = min(half, 256)
    norm = jnp.zeros((slots, 1), jnp.float32)
    for column in range(0, half, step):
        block = slice(column, column + step)
        student_z = jnp.dot(
            projected[...], freqs[:, block], preferred_element_type=jnp.float32
        )
        teacher_z = jnp.dot(
            rows[:, :d_t], freqs[:, block], preferred_element_type=jnp.float32
        )
        cos_s, sin_s = cos_sin(student_z)
        cos_t, sin_t = cos_sin(teacher_z)
        mean_c = inverse * jnp.dot(
            same, (cos_s - cos_t).astype(jnp.bfloat16), preferred_element_type=jnp.float32
        )
        mean_s = inverse * jnp.dot(
            same, (sin_s - sin_t).astype(jnp.bfloat16), preferred_element_type=jnp.float32
        )
        norm += jnp.sum(mean_c * mean_c + mean_s * mean_s, axis=1, keepdims=True)
        grad_z[:, block] = (cos_s * mean_s - sin_s * mean_c).astype(jnp.bfloat16)
    cls = lax.broadcasted_iota(jnp.int32, (slots, cls_pad), 1).astype(jnp.float32) + 1.0
    norms[...] = jnp.sum(jnp.where(cls == tag, norm, 0.0), axis=0, keepdims=True)
    out_rows = d_t // (n_dp * n_feat)
    block = n_dp // pair * out_rows
    for offset in range(n_feat):
        for across in range(pair):
            index = lax.rem(side + across, pair) * n_feat + lax.rem(feat + offset, n_feat)
            target = slice(across * block, (across + 1) * block)
            if permuted:
                picked[target, :] = weights[index]
            else:
                for group in range(n_dp // pair):
                    start = pl.multiple_of((group * pair * n_feat + index) * out_rows, out_rows)
                    first = across * block + group * out_rows
                    picked[first : first + out_rows, :] = freqs[pl.ds(start, out_rows), :]
        out = grads[offset]
        out[...] = lax.dot_general(
            picked[...], grad_z[...], (((1,), (1,)), ((), ())), preferred_element_type=jnp.float32
        ).astype(out.dtype)


def summed(refs, start, size):
    total = refs[0][start : start + size, :].astype(jnp.float32)
    for ref in refs[1:]:
        total += ref[start : start + size, :].astype(jnp.float32)
    return total.astype(jnp.bfloat16)


def fold_kernel(*refs):
    size = refs[-1].shape[0]
    refs[-1][...] = summed(refs[:-1], size, size)


def own_kernel(n_feat, scale, divisor, d_t, d_s, *refs):
    grads, norms, student = refs[:n_feat], refs[n_feat : 2 * n_feat], refs[2 * n_feat]
    parts, refs = refs[2 * n_feat + 1 : -4], refs[-4:]
    head, loss, partner, rows = refs
    feat = lax.axis_index("feat")
    head[...] = scale * jnp.dot(
        summed(grads, 0, head.shape[0]), student[...], preferred_element_type=jnp.float32
    )
    norm = norms[0][...]
    for offset in range(1, n_feat):
        norm += norms[offset][...]
    loss[...] = (norm * (1.0 / divisor))[0, : loss.shape[0]]
    for offset, part in enumerate(parts):
        width = part.shape[1]
        index = lax.rem(feat + (n_feat - offset), n_feat)
        rows[:, pl.ds(pl.multiple_of(index * width, LANES), width)] = part[...]
    if parts:
        partner[...] = rows[:, d_t : d_t + d_s]


def head_kernel(scale, own, grads, partner, head):
    product = jnp.dot(grads[...], partner[...], preferred_element_type=jnp.float32)
    head[...] = (own[...] + product * scale).astype(jnp.bfloat16)


def on_device(teacher, student, head, freqs, labels, class_slot):
    n_dp = lax.axis_size("dp")
    n_feat = lax.axis_size("feat")
    images, d_t = teacher.shape
    d_s = student.shape[1]
    half = freqs.shape[1]
    classes = class_slot.shape[0]
    cls_dev = classes // n_dp
    cls_pad = up_to(cls_dev, LANES)
    capacity = 2 * images // n_dp
    slots = n_dp * capacity
    width = up_to(d_t + d_s + LANES, LANES * n_feat) // n_feat
    out_rows = d_t // (n_dp * n_feat)
    pair = 2 if n_dp % 2 == 0 else 1
    groups = n_dp // pair
    vmem = pltpu.CompilerParams(vmem_limit_bytes=20 * 2**20)
    hbm = pl.BlockSpec(memory_space=pltpu.HBM)
    near = pl.BlockSpec(memory_space=pltpu.VMEM)

    def moved(value, across, offset, feats=None):
        moves = [
            (d * n_feat + f, (d ^ across) * n_feat + (f + offset) % n_feat)
            for d in range(n_dp)
            for f in (range(n_feat) if feats is None else feats)
        ]
        return lax.ppermute(value, ("dp", "feat"), moves)

    def all_parts(value):
        return [value] + [moved(value, 0, k) for k in range(1, n_feat)]

    sent, token = pl.pallas_call(
        functools.partial(route_kernel, cls_dev, capacity),
        out_shape=(
            jax.ShapeDtypeStruct((slots, width), jnp.bfloat16),
            jax.ShapeDtypeStruct((8, LANES), jnp.float32),
        ),
        in_specs=[hbm] * 4,
        scratch_shapes=[
            pltpu.VMEM((images,), jnp.int32),
            pltpu.VMEM((classes,), jnp.int32),
            pltpu.VMEM((images, width * n_feat), jnp.bfloat16),
            pltpu.SemaphoreType.DMA((4,)),
        ],
        compiler_params=pltpu.CompilerParams(vmem_limit_bytes=60 * 2**20),
        name="route",
    )(labels, class_slot, teacher, student)
    permuted = out_rows % 16 != 0
    weights = []
    if permuted:
        weights = jnp.swapaxes(freqs.reshape(groups, pair * n_feat, out_rows, half), 0, 1)
        weights = [weights.reshape(pair * n_feat, groups * out_rows, half)]
    head_near, freqs_near = pl.pallas_call(
        load_kernel,
        out_shape=(
            jax.ShapeDtypeStruct(head.shape, jnp.bfloat16),
            jax.ShapeDtypeStruct(freqs.shape, jnp.bfloat16),
        ),
        in_specs=[hbm] * 3,
        scratch_shapes=[pltpu.SemaphoreType.DMA((2,))],
        compiler_params=vmem,
        name="load",
    )(head, freqs, token)
    heads = all_parts(head_near)
    mine = lax.all_to_all(
        sent.reshape(n_dp, capacity, width), "dp", split_axis=0, concat_axis=0, tiled=True
    ).reshape(slots, width)
    parts = all_parts(mine)
    block = groups * out_rows
    *grads, norms, s_rows = pl.pallas_call(
        functools.partial(class_kernel, n_feat, n_dp, pair, cls_pad, d_t, d_s, permuted),
        out_shape=tuple(
            jax.ShapeDtypeStruct((pair * block, slots), jnp.bfloat16 if k else jnp.float32)
            for k in range(n_feat)
        )
        + (
            jax.ShapeDtypeStruct((1, cls_pad), jnp.float32),
            jax.ShapeDtypeStruct((slots, d_s), jnp.bfloat16),
        ),
        scratch_shapes=[
            pltpu.VMEM((slots, width * n_feat), jnp.bfloat16),
            pltpu.VMEM((slots, d_t), jnp.bfloat16),
            pltpu.VMEM((slots, half), jnp.bfloat16),
            pltpu.VMEM((pair * block, half), jnp.bfloat16),
            pltpu.VMEM((n_feat - 1, *head.shape), jnp.bfloat16),
            pltpu.SemaphoreType.DMA((n_feat - 1,)),
        ],
        in_specs=[near] * (n_feat + 1) + [hbm] * (n_feat - 1) + [near] * (1 + len(weights)),
        compiler_params=vmem,
        name="classes",
    )(*parts, *heads, freqs_near, *weights)
    partner = []
    if pair > 1:
        holders = [
            f for f in range(n_feat) if f * width < d_t + d_s and (f + 1) * width > d_t
        ]
        across = moved(mine, 1, 0, holders)
    all_grads = [grads[0]] + [moved(grads[k], 0, k) for k in range(1, n_feat)]
    all_norms = all_parts(norms)
    if pair > 1:
        all_grads, all_norms, across = lax.optimization_barrier((all_grads, all_norms, across))
        partner = all_parts(across)
    scale = 1.0 / math.sqrt(images * n_dp)
    own, loss, partner_rows = pl.pallas_call(
        functools.partial(own_kernel, n_feat, scale, 2.0 * half * n_feat, d_t, d_s),
        out_shape=(
            jax.ShapeDtypeStruct((block, d_s), jnp.float32),
            jax.ShapeDtypeStruct((cls_dev,), jnp.float32),
            jax.ShapeDtypeStruct((slots, d_s), jnp.bfloat16),
        ),
        scratch_shapes=[pltpu.VMEM((slots, width * n_feat), jnp.bfloat16)],
        compiler_params=vmem,
        name="own",
    )(*all_grads, *all_norms, s_rows, *partner)
    if pair > 1:
        folded = pl.pallas_call(
            fold_kernel,
            out_shape=jax.ShapeDtypeStruct((block, slots), jnp.bfloat16),
            compiler_params=vmem,
            name="fold",
        )(*all_grads)
        partial_head = pl.pallas_call(
            functools.partial(head_kernel, scale),
            out_shape=jax.ShapeDtypeStruct((block, d_s), jnp.bfloat16),
            compiler_params=vmem,
            name="head",
        )(own, moved(folded, 1, 0), partner_rows)
    else:
        partial_head = own.astype(jnp.bfloat16)
    received = lax.all_to_all(
        partial_head.reshape(groups, out_rows, d_s),
        "dp",
        split_axis=0,
        concat_axis=0,
        tiled=True,
        axis_index_groups=[list(range(p, n_dp, pair)) for p in range(pair)],
    )
    head_grad = jnp.sum(received.astype(jnp.float32), axis=0)
    return (head_grad, loss)


def solution(mesh):
    in_specs = (P("dp", None), P("dp", None), P(None, "feat"), P(None, "feat"), P("dp"), P())
    out_specs = (P(("dp", "feat"), None), P("dp"))
    return jax.shard_map(
        on_device, mesh=mesh, in_specs=in_specs, out_specs=out_specs, check_vma=False
    )
```

```python
import functools
import math

import jax
import jax.numpy as jnp
from jax import lax
from jax.experimental import pallas as pl
from jax.experimental.pallas import tpu as pltpu
from jax.sharding import PartitionSpec as P

LANES = 128
CARRIED = 16
PIECES = 3
TURN = 1.0 / (2.0 * math.pi)
ROUNDER = 1.5 * 2.0**23
SINE = (6.283164044217864, -41.337142357601536, 81.3407683703199, -70.9934277613874)


def up_to(value, multiple):
    return -(-value // multiple) * multiple


def quarter_sine(angle):
    square = angle * angle
    value = jnp.float32(SINE[-1])
    for factor in SINE[-2::-1]:
        value = value * square + factor
    return value * angle


def cos_sin(z):
    turns = z * TURN
    part = turns - ((turns + ROUNDER) - ROUNDER)
    wave = jnp.minimum(jnp.maximum(part, -0.5 - part), 0.5 - part)
    return quarter_sine(0.25 - jnp.abs(part)), quarter_sine(wave)


def to_row(column, size):
    first = lax.broadcasted_iota(jnp.int32, (size, size), 0)
    second = lax.broadcasted_iota(jnp.int32, (size, size), 1)
    return jnp.sum(jnp.where(first == second, column, 0.0), axis=0, keepdims=True)


def to_column(row, size):
    first = lax.broadcasted_iota(jnp.int32, (size, size), 0)
    second = lax.broadcasted_iota(jnp.int32, (size, size), 1)
    return jnp.sum(jnp.where(first == second, row, 0.0), axis=1, keepdims=True)


def table_entries(table, chunk):
    start = chunk * LANES
    size = min(LANES, table.shape[0] - start)
    entries = table[pl.ds(start, size)].astype(jnp.float32)
    if size < LANES:
        entries = jnp.concatenate([entries, jnp.zeros((LANES - size,), jnp.float32)])
    return entries.reshape(1, LANES)


def route_kernel(
    cls_dev, capacity, labels_in, table_in, teacher, student, out, token, labels, table, rows, sems
):
    images, d_t = teacher.shape
    d_s = student.shape[1]
    slots, width = out.shape
    copies = [
        pltpu.make_async_copy(labels_in, labels, sems.at[0]),
        pltpu.make_async_copy(table_in, table, sems.at[1]),
        pltpu.make_async_copy(teacher, rows.at[:, :d_t], sems.at[2]),
        pltpu.make_async_copy(student, rows.at[:, d_t : d_t + d_s], sems.at[3]),
    ]
    for copy in copies:
        copy.start()
    lane = lax.broadcasted_iota(jnp.int32, (images, LANES), 1)
    lane_f = lane.astype(jnp.float32)
    copies[0].wait()
    label = to_column(labels[...].astype(jnp.float32).reshape(1, images), images)
    label = jnp.broadcast_to(label, (images, LANES))
    copies[1].wait()
    found = jnp.zeros((images, LANES), jnp.float32)
    for chunk in range(pl.cdiv(table.shape[0], LANES)):
        entries = table_entries(table, chunk)
        found += jnp.where(lane_f + float(chunk * LANES) == label, entries, 0.0)
    position = jnp.sum(found, axis=1, keepdims=True)
    owner = jnp.floor((position + 0.5) * (1.0 / cls_dev))
    tag = position - owner * cls_dev + 1.0
    owner_row = to_row(owner, images)
    first = lax.broadcasted_iota(jnp.int32, (images, images), 0)
    second = lax.broadcasted_iota(jnp.int32, (images, images), 1)
    before = jnp.logical_and(first < second, owner == owner_row)
    rank = jnp.sum(jnp.where(before, 1.0, 0.0), axis=0, keepdims=True)
    slot = owner_row * float(capacity) + rank
    slot_id = lax.broadcasted_iota(jnp.int32, (slots, images), 0).astype(jnp.float32)
    pick = jnp.where(slot_id == slot, 1.0, 0.0).astype(jnp.bfloat16)
    high = jnp.floor(tag * (1.0 / 32.0))
    tags = jnp.where(lane == 0, high, jnp.where(lane == 1, tag - 32.0 * high, 0.0))
    rows[:, d_t + d_s : d_t + d_s + LANES] = tags.astype(jnp.bfloat16)
    rows[:, d_t + d_s + LANES :] = jnp.zeros(
        (images, rows.shape[1] - d_t - d_s - LANES), jnp.bfloat16
    )
    token[...] = jnp.zeros_like(token)
    copies[2].wait()
    copies[3].wait()
    start = pl.multiple_of(lax.axis_index("feat") * width, LANES)
    out[...] = jnp.dot(
        pick, rows[:, pl.ds(start, width)], preferred_element_type=jnp.float32
    ).astype(jnp.bfloat16)


def load_kernel(head_in, freqs_in, _, head, freqs, sems):
    copies = [
        pltpu.make_async_copy(head_in, head, sems.at[0]),
        pltpu.make_async_copy(freqs_in, freqs, sems.at[1]),
    ]
    for copy in copies:
        copy.start()
    for copy in copies:
        copy.wait()


def carry(norm, lanes):
    row = lax.broadcasted_iota(jnp.int32, (CARRIED, lanes), 0)
    block, index = jnp.zeros((CARRIED, lanes), jnp.float32), 0
    for _ in range(PIECES):
        piece = norm.astype(jnp.bfloat16).astype(jnp.float32)
        norm = norm - piece
        for start in range(0, norm.shape[1], lanes):
            block = jnp.where(row == index, piece[:, start : start + lanes], block)
            index += 1
    return block.astype(jnp.bfloat16)


def carried_norm(block, size):
    lanes = block.shape[1]
    values = block.astype(jnp.float32)
    width = size // lanes
    found = []
    for part in range(width):
        rows = [values[p * width + part : p * width + part + 1, :] for p in range(PIECES)]
        found.append(sum(rows[1:], rows[0]))
    return jnp.concatenate(found, axis=1) if width > 1 else found[0]


def sort_kernel(mine, other, teacher, student, tags):
    d_s = student.shape[1]
    holds_student = lax.axis_index("feat") == 1

    def split(first, second):
        teacher[...] = first[...]
        student[...] = second[:, :d_s]
        tags[...] = second[:, d_s : d_s + LANES]

    pl.when(holds_student)(lambda: split(other, mine))
    pl.when(jnp.logical_not(holds_student))(lambda: split(mine, other))


def member_of(group, bit, side):
    low = group * 2 + side
    high = group // 2 * 4 + side * 2 + group % 2
    return jnp.where(bit == 0, low, high)


def class_kernel(n_feat, n_dp, bits, cls_pad, permuted, teacher, student, tags_in, *refs):
    heads, freqs, refs = refs[:n_feat], refs[n_feat], refs[n_feat + 1 :]
    if permuted:
        weights, refs = refs[0], refs[1:]
    grads, refs = refs[:n_feat], refs[n_feat:]
    norms, projected, grad_z, picked, near, sems = refs
    feat = lax.axis_index("feat")
    holder = lax.axis_index("dp")
    copies = [
        pltpu.make_async_copy(heads[k], near.at[k - 1], sems.at[k - 1]) for k in range(1, n_feat)
    ]
    for copy in copies:
        copy.start()
    slots, d_t = teacher.shape
    half = freqs.shape[1]
    tags = tags_in[...].astype(jnp.float32)
    lane = lax.broadcasted_iota(jnp.int32, (slots, LANES), 1)
    tag = jnp.sum(
        tags * jnp.where(lane == 0, 32.0, jnp.where(lane == 1, 1.0, 0.0)), axis=1, keepdims=True
    )
    tag_row = to_row(tag, slots)
    same = jnp.where(jnp.logical_and(tag == tag_row, tag > 0.0), 1.0, 0.0)
    inverse = 1.0 / jnp.maximum(jnp.sum(same, axis=1, keepdims=True), 1.0)
    same = same.astype(jnp.bfloat16)
    part = d_t // n_feat
    for offset in range(n_feat):
        if offset:
            copies[offset - 1].wait()
        weight = near[offset - 1] if offset else heads[0][...]
        index = lax.rem(feat + (n_feat - offset), n_feat)
        projected[:, pl.ds(pl.multiple_of(index * part, LANES), part)] = jnp.dot(
            student[...], weight, preferred_element_type=jnp.float32
        ).astype(jnp.bfloat16)
    step = min(half, 256)
    blocks = [slice(column, column + step) for column in range(0, half, step)]
    teacher_z = [
        jnp.dot(teacher[...], freqs[:, block], preferred_element_type=jnp.float32)
        for block in blocks
    ]
    student_z = [
        jnp.dot(projected[...], freqs[:, block], preferred_element_type=jnp.float32)
        for block in blocks
    ]
    norm = jnp.zeros((slots, 1), jnp.float32)
    for index, block in enumerate(blocks):
        cos_s, sin_s = cos_sin(student_z[index])
        cos_t, sin_t = cos_sin(teacher_z[index])
        mean_c = inverse * jnp.dot(
            same, (cos_s - cos_t).astype(jnp.bfloat16), preferred_element_type=jnp.float32
        )
        mean_s = inverse * jnp.dot(
            same, (sin_s - sin_t).astype(jnp.bfloat16), preferred_element_type=jnp.float32
        )
        norm += jnp.sum(mean_c * mean_c + mean_s * mean_s, axis=1, keepdims=True)
        grad_z[:, block] = (cos_s * mean_s - sin_s * mean_c).astype(jnp.bfloat16)
    cls = lax.broadcasted_iota(jnp.int32, (slots, cls_pad), 1).astype(jnp.float32) + 1.0
    total_norm = jnp.sum(jnp.where(cls == tag, norm, 0.0), axis=0, keepdims=True)
    norms[...] = total_norm
    carried = carry(total_norm, slots)
    out_rows = d_t // (n_dp * n_feat)
    block = n_dp // 2 * out_rows
    for offset in range(n_feat):
        target = lax.rem(feat + offset, n_feat)
        bit = lax.rem(target, bits)
        side = jnp.where(bit == 0, lax.rem(holder, 2), lax.rem(holder // 2, 2))
        if permuted:
            picked[...] = weights[offset]
        else:
            for index in range(n_dp):
                across, group = divmod(index, n_dp // 2)
                member = member_of(group, bit, 1 - side if across else side)
                start = pl.multiple_of((member * n_feat + target) * out_rows, out_rows)
                picked[index * out_rows : (index + 1) * out_rows, :] = freqs[
                    pl.ds(start, out_rows), :
                ]
        out = grads[offset]
        out[: 2 * block, :] = lax.dot_general(
            picked[...], grad_z[...], (((1,), (1,)), ((), ())), preferred_element_type=jnp.float32
        ).astype(out.dtype)
        if offset:
            out[2 * block :, :] = carried


def summed(refs, start, size):
    total = refs[0][start : start + size, :].astype(jnp.float32)
    for ref in refs[1:]:
        total += ref[start : start + size, :].astype(jnp.float32)
    return total.astype(jnp.bfloat16)


def fold_kernel(*refs):
    size = refs[-1].shape[0]
    refs[-1][...] = summed(refs[:-1], size, size)


def own_kernel(scale, divisor, *refs):
    grads, (norms, student, head, loss) = refs[:-4], refs[-4:]
    head[...] = scale * jnp.dot(
        summed(grads, 0, head.shape[0]), student[...], preferred_element_type=jnp.float32
    )
    norm = norms[...]
    for ref in grads[1:]:
        norm += carried_norm(ref[ref.shape[0] - CARRIED :, :], norm.shape[1])
    loss[...] = (norm * (1.0 / divisor))[0, : loss.shape[0]]


def head_kernel(scale, own, grads, student, head):
    product = jnp.dot(grads[...], student[...], preferred_element_type=jnp.float32)
    head[...] = (own[...] + product * scale).astype(jnp.bfloat16)


def on_device(teacher, student, head, freqs, labels, class_slot):
    n_dp = lax.axis_size("dp")
    n_feat = lax.axis_size("feat")
    images, d_t = teacher.shape
    d_s = student.shape[1]
    half = freqs.shape[1]
    classes = class_slot.shape[0]
    cls_dev = classes // n_dp
    capacity = 2 * images // n_dp
    slots = n_dp * capacity
    cls_pad = up_to(cls_dev, slots)
    width = up_to(d_t + d_s + LANES, LANES * n_feat) // n_feat
    out_rows = d_t // (n_dp * n_feat)
    bits = 2 if n_dp % 4 == 0 else 1
    block = n_dp // 2 * out_rows
    vmem = pltpu.CompilerParams(vmem_limit_bytes=20 * 2**20)
    hbm = pl.BlockSpec(memory_space=pltpu.HBM)
    near = pl.BlockSpec(memory_space=pltpu.VMEM)

    def across(value):
        moves = [
            (d * n_feat + f, (d ^ (1 << f % bits)) * n_feat + f)
            for d in range(n_dp)
            for f in range(n_feat)
        ]
        return lax.ppermute(value, ("dp", "feat"), moves)

    def shifted(value, offset):
        return lax.ppermute(
            value, "feat", [(f, (f + offset) % n_feat) for f in range(n_feat)]
        )

    sent, token = pl.pallas_call(
        functools.partial(route_kernel, cls_dev, capacity),
        out_shape=(
            jax.ShapeDtypeStruct((slots, width), jnp.bfloat16),
            jax.ShapeDtypeStruct((8, LANES), jnp.float32),
        ),
        in_specs=[hbm] * 4,
        scratch_shapes=[
            pltpu.VMEM((images,), jnp.int32),
            pltpu.VMEM((classes,), jnp.int32),
            pltpu.VMEM((images, width * n_feat), jnp.bfloat16),
            pltpu.SemaphoreType.DMA((4,)),
        ],
        compiler_params=pltpu.CompilerParams(vmem_limit_bytes=60 * 2**20),
        name="route",
    )(labels, class_slot, teacher, student)
    permuted = out_rows % 16 != 0
    weights = []
    if permuted:
        targets = (lax.axis_index("feat") + jnp.arange(n_feat)) % n_feat
        bit = (targets % bits)[:, None]
        group = jnp.tile(jnp.arange(n_dp // 2), 2)[None, :]
        side = (lax.axis_index("dp") >> bit) % 2
        side = jnp.where(jnp.arange(n_dp)[None, :] >= n_dp // 2, 1 - side, side)
        member = member_of(group, bit, side)
        lines = (member * n_feat + targets[:, None])[:, :, None] * out_rows + jnp.arange(out_rows)
        weights = [jnp.take(freqs, lines.reshape(n_feat, 2 * block), axis=0)]
    head_near, freqs_near = pl.pallas_call(
        load_kernel,
        out_shape=(
            jax.ShapeDtypeStruct(head.shape, jnp.bfloat16),
            jax.ShapeDtypeStruct(freqs.shape, jnp.bfloat16),
        ),
        in_specs=[hbm] * 3,
        scratch_shapes=[pltpu.SemaphoreType.DMA((2,))],
        compiler_params=vmem,
        name="load",
    )(head, freqs, token)
    heads = [head_near] + [shifted(head_near, k) for k in range(1, n_feat)]
    mine = lax.all_to_all(
        sent.reshape(n_dp, capacity, width), "dp", split_axis=0, concat_axis=0, tiled=True
    ).reshape(slots, width)
    if n_feat == 2 and width == d_t:
        teacher_in, student_in, tags_in = pl.pallas_call(
            sort_kernel,
            out_shape=(
                jax.ShapeDtypeStruct((slots, d_t), jnp.bfloat16),
                jax.ShapeDtypeStruct((slots, d_s), jnp.bfloat16),
                jax.ShapeDtypeStruct((slots, LANES), jnp.bfloat16),
            ),
            compiler_params=vmem,
            name="sort",
        )(mine, shifted(mine, 1))
    else:
        everything = lax.all_gather(mine, "feat", axis=1, tiled=True)
        teacher_in, student_in, tags_in = jnp.split(
            everything[:, : d_t + d_s + LANES], [d_t, d_t + d_s], axis=1
        )
    student_across = across(student_in)
    *grads, norms = pl.pallas_call(
        functools.partial(class_kernel, n_feat, n_dp, bits, cls_pad, permuted),
        out_shape=tuple(
            jax.ShapeDtypeStruct((2 * block + CARRIED, slots), jnp.bfloat16)
            if k
            else jax.ShapeDtypeStruct((2 * block, slots), jnp.float32)
            for k in range(n_feat)
        )
        + (jax.ShapeDtypeStruct((1, cls_pad), jnp.float32),),
        in_specs=[near] * 4 + [hbm] * (n_feat - 1) + [near] * (1 + len(weights)),
        scratch_shapes=[
            pltpu.VMEM((slots, d_t), jnp.bfloat16),
            pltpu.VMEM((slots, half), jnp.bfloat16),
            pltpu.VMEM((2 * block, half), jnp.bfloat16),
            pltpu.VMEM((n_feat - 1, *head.shape), jnp.bfloat16),
            pltpu.SemaphoreType.DMA((n_feat - 1,)),
        ],
        compiler_params=vmem,
        name="classes",
    )(teacher_in, student_in, tags_in, *heads, freqs_near, *weights)
    all_grads = [grads[0]] + [shifted(grads[k], k) for k in range(1, n_feat)]
    all_grads, student_across = lax.optimization_barrier((all_grads, student_across))
    scale = 1.0 / math.sqrt(images * n_dp)
    folded = pl.pallas_call(
        fold_kernel,
        out_shape=jax.ShapeDtypeStruct((block, slots), jnp.bfloat16),
        compiler_params=vmem,
        name="fold",
    )(*all_grads)
    folded, all_grads = lax.optimization_barrier((folded, all_grads))
    own, loss = pl.pallas_call(
        functools.partial(own_kernel, scale, 2.0 * half * n_feat),
        out_shape=(
            jax.ShapeDtypeStruct((block, d_s), jnp.float32),
            jax.ShapeDtypeStruct((cls_dev,), jnp.float32),
        ),
        compiler_params=vmem,
        name="own",
    )(*all_grads, norms, student_in)
    partial_head = pl.pallas_call(
        functools.partial(head_kernel, scale),
        out_shape=jax.ShapeDtypeStruct((block, d_s), jnp.bfloat16),
        compiler_params=vmem,
        name="head",
    )(own, across(folded), student_across)
    received = lax.all_to_all(
        partial_head.reshape(n_dp // 2, out_rows, d_s),
        ("dp", "feat"),
        split_axis=0,
        concat_axis=0,
        tiled=True,
        axis_index_groups=[
            [d * n_feat + f for d in range(n_dp) if (d >> f % bits) % 2 == side]
            for f in range(n_feat)
            for side in range(2)
        ],
    )
    head_grad = jnp.sum(received.astype(jnp.float32), axis=0)
    return (head_grad, loss)


def solution(mesh):
    in_specs = (P("dp", None), P("dp", None), P(None, "feat"), P(None, "feat"), P("dp"), P())
    out_specs = (P(("dp", "feat"), None), P("dp"))
    return jax.shard_map(
        on_device, mesh=mesh, in_specs=in_specs, out_specs=out_specs, check_vma=False
    )
```

```python
import functools
import math

import jax
import jax.numpy as jnp
from jax import lax
from jax.experimental import pallas as pl
from jax.experimental.pallas import tpu as pltpu
from jax.sharding import PartitionSpec as P

LANES = 128
CARRIED = 16
PIECES = 3
TURN = 1.0 / (2.0 * math.pi)
ROUNDER = 1.5 * 2.0**23
SINE = (6.283164044217864, -41.337142357601536, 81.3407683703199, -70.9934277613874)


def up_to(value, multiple):
    return -(-value // multiple) * multiple


def quarter_sine(angle):
    square = angle * angle
    value = jnp.float32(SINE[-1])
    for factor in SINE[-2::-1]:
        value = value * square + factor
    return value * angle


def cos_sin(z):
    turns = z * TURN
    part = turns - ((turns + ROUNDER) - ROUNDER)
    wave = jnp.minimum(jnp.maximum(part, -0.5 - part), 0.5 - part)
    return quarter_sine(0.25 - jnp.abs(part)), quarter_sine(wave)


def to_row(column, size):
    first = lax.broadcasted_iota(jnp.int32, (size, size), 0)
    second = lax.broadcasted_iota(jnp.int32, (size, size), 1)
    return jnp.sum(jnp.where(first == second, column, 0.0), axis=0, keepdims=True)


def to_column(row, size):
    first = lax.broadcasted_iota(jnp.int32, (size, size), 0)
    second = lax.broadcasted_iota(jnp.int32, (size, size), 1)
    return jnp.sum(jnp.where(first == second, row, 0.0), axis=1, keepdims=True)


def table_entries(table, chunk):
    start = chunk * LANES
    size = min(LANES, table.shape[0] - start)
    entries = table[pl.ds(start, size)].astype(jnp.float32)
    if size < LANES:
        entries = jnp.concatenate([entries, jnp.zeros((LANES - size,), jnp.float32)])
    return entries.reshape(1, LANES)


def route_kernel(
    cls_dev, capacity, labels_in, table_in, teacher, student, out, token, labels, table, rows, sems
):
    images, d_t = teacher.shape
    d_s = student.shape[1]
    slots, width = out.shape
    copies = [
        pltpu.make_async_copy(labels_in, labels, sems.at[0]),
        pltpu.make_async_copy(table_in, table, sems.at[1]),
        pltpu.make_async_copy(teacher, rows.at[:, :d_t], sems.at[2]),
        pltpu.make_async_copy(student, rows.at[:, d_t : d_t + d_s], sems.at[3]),
    ]
    for copy in copies:
        copy.start()
    lane = lax.broadcasted_iota(jnp.int32, (images, LANES), 1)
    lane_f = lane.astype(jnp.float32)
    copies[0].wait()
    label = to_column(labels[...].astype(jnp.float32).reshape(1, images), images)
    label = jnp.broadcast_to(label, (images, LANES))
    copies[1].wait()
    found = jnp.zeros((images, LANES), jnp.float32)
    for chunk in range(pl.cdiv(table.shape[0], LANES)):
        entries = table_entries(table, chunk)
        found += jnp.where(lane_f + float(chunk * LANES) == label, entries, 0.0)
    position = jnp.sum(found, axis=1, keepdims=True)
    owner = jnp.floor((position + 0.5) * (1.0 / cls_dev))
    tag = position - owner * cls_dev + 1.0
    owner_row = to_row(owner, images)
    first = lax.broadcasted_iota(jnp.int32, (images, images), 0)
    second = lax.broadcasted_iota(jnp.int32, (images, images), 1)
    before = jnp.logical_and(first < second, owner == owner_row)
    rank = jnp.sum(jnp.where(before, 1.0, 0.0), axis=0, keepdims=True)
    slot = owner_row * float(capacity) + rank
    slot_id = lax.broadcasted_iota(jnp.int32, (slots, images), 0).astype(jnp.float32)
    pick = jnp.where(slot_id == slot, 1.0, 0.0).astype(jnp.bfloat16)
    high = jnp.floor(tag * (1.0 / 32.0))
    tags = jnp.where(lane == 0, high, jnp.where(lane == 1, tag - 32.0 * high, 0.0))
    rows[:, d_t + d_s : d_t + d_s + LANES] = tags.astype(jnp.bfloat16)
    rows[:, d_t + d_s + LANES :] = jnp.zeros(
        (images, rows.shape[1] - d_t - d_s - LANES), jnp.bfloat16
    )
    token[...] = jnp.zeros_like(token)
    copies[2].wait()
    copies[3].wait()
    start = pl.multiple_of(lax.axis_index("feat") * width, LANES)
    out[...] = jnp.dot(
        pick, rows[:, pl.ds(start, width)], preferred_element_type=jnp.float32
    ).astype(jnp.bfloat16)


def load_kernel(head_in, freqs_in, _, head, freqs, sems):
    copies = [
        pltpu.make_async_copy(head_in, head, sems.at[0]),
        pltpu.make_async_copy(freqs_in, freqs, sems.at[1]),
    ]
    for copy in copies:
        copy.start()
    for copy in copies:
        copy.wait()


def carry(norm, lanes):
    row = lax.broadcasted_iota(jnp.int32, (CARRIED, lanes), 0)
    block, index = jnp.zeros((CARRIED, lanes), jnp.float32), 0
    for _ in range(PIECES):
        piece = norm.astype(jnp.bfloat16).astype(jnp.float32)
        norm = norm - piece
        for start in range(0, norm.shape[1], lanes):
            block = jnp.where(row == index, piece[:, start : start + lanes], block)
            index += 1
    return block.astype(jnp.bfloat16)


def carried_norm(block, size):
    lanes = block.shape[1]
    values = block.astype(jnp.float32)
    width = size // lanes
    found = []
    for part in range(width):
        rows = [values[p * width + part : p * width + part + 1, :] for p in range(PIECES)]
        found.append(sum(rows[1:], rows[0]))
    return jnp.concatenate(found, axis=1) if width > 1 else found[0]


def place_of(own, offset, count):
    return lax.rem(own + (count - offset), count)


def load_heads(heads, near, sems):
    return [
        pltpu.make_async_copy(heads[k], near.at[k - 1], sems.at[k - 1])
        for k in range(1, len(heads))
    ]


def project(student, heads, near, copies, projected):
    feat = lax.axis_index("feat")
    part = projected.shape[1] // len(heads)
    for offset in range(len(heads)):
        if offset:
            copies[offset - 1].wait()
        weight = near[offset - 1] if offset else heads[0][...]
        start = pl.multiple_of(place_of(feat, offset, len(heads)) * part, LANES)
        projected[:, pl.ds(start, part)] = jnp.dot(
            student, weight, preferred_element_type=jnp.float32
        ).astype(jnp.bfloat16)


def products(inputs, freqs, step):
    return [
        jnp.dot(
            inputs[...], freqs[:, column : column + step], preferred_element_type=jnp.float32
        )
        for column in range(0, freqs.shape[1], step)
    ]


def is_role(role, index):
    return (lax.axis_index("feat") if role is None else role) == index


def first_kernel(role, n_feat, d_s, rows, *refs):
    heads, (freqs, cos, sin, inputs, near, sems) = refs[:n_feat], refs[n_feat:]
    is_student = is_role(role, 1)
    copies = load_heads(heads, near, sems)
    part = freqs.shape[0] // n_feat
    own = pl.multiple_of(lax.axis_index("feat") * part, LANES)

    @pl.when(is_student)
    def _():
        for copy in copies:
            copy.start()
        inputs[:, pl.ds(own, part)] = jnp.dot(
            rows[:, :d_s], heads[0][...], preferred_element_type=jnp.float32
        ).astype(jnp.bfloat16)

    @pl.when(jnp.logical_not(is_student))
    def _():
        inputs[...] = rows[...]

    step = min(freqs.shape[1], 256)
    blocks = [slice(c, c + step) for c in range(0, freqs.shape[1], step)]
    found = [0.0] * len(blocks)
    for offset in range(n_feat):
        start = pl.multiple_of(place_of(lax.axis_index("feat"), offset, n_feat) * part, LANES)
        if offset:

            @pl.when(is_student)
            def _():
                copies[offset - 1].wait()
                inputs[:, pl.ds(start, part)] = jnp.dot(
                    rows[:, :d_s], near[offset - 1], preferred_element_type=jnp.float32
                ).astype(jnp.bfloat16)

        for index, block in enumerate(blocks):
            found[index] += jnp.dot(
                inputs[:, pl.ds(start, part)],
                freqs[pl.ds(start, part), block],
                preferred_element_type=jnp.float32,
            )
    for index, block in enumerate(blocks):
        cos[:, block], sin[:, block] = cos_sin(found[index])


def sort_kernel(mine, other, student, tags):
    d_s = student.shape[1]

    def split(rows):
        student[...] = rows[:, :d_s]
        tags[...] = rows[:, d_s : d_s + LANES]

    pl.when(is_role(None, 1))(lambda: split(mine))
    pl.when(is_role(None, 0))(lambda: split(other))


def member_of(group, bit, side):
    low = group * 2 + side
    high = group // 2 * 4 + side * 2 + group % 2
    return jnp.where(bit == 0, low, high)


def class_kernel(
    role, n_feat, n_dp, bits, cls_pad, permuted, other, student, tags_in, cos, sin, *refs
):
    heads, freqs, refs = refs[:n_feat], refs[n_feat], refs[n_feat + 1 :]
    if permuted:
        weights, refs = refs[0], refs[1:]
    grads, refs = refs[: 2 * n_feat], refs[2 * n_feat :]
    norms, inputs, grad_z, picked, near, sems = refs
    feat = lax.axis_index("feat")
    holder = lax.axis_index("dp")
    mine_student = is_role(role, 1)
    slots, d_t = inputs.shape
    half = freqs.shape[1]

    copies = load_heads(heads, near, sems)

    @pl.when(jnp.logical_not(mine_student))
    def _():
        for copy in copies:
            copy.start()

    tags = tags_in[...].astype(jnp.float32)
    lane = lax.broadcasted_iota(jnp.int32, (slots, LANES), 1)
    tag = jnp.sum(
        tags * jnp.where(lane == 0, 32.0, jnp.where(lane == 1, 1.0, 0.0)), axis=1, keepdims=True
    )
    tag_row = to_row(tag, slots)
    same = jnp.where(jnp.logical_and(tag == tag_row, tag > 0.0), 1.0, 0.0)
    inverse = 1.0 / jnp.maximum(jnp.sum(same, axis=1, keepdims=True), 1.0)
    inverse = jnp.where(mine_student, -inverse, inverse)
    same = same.astype(jnp.bfloat16)

    @pl.when(mine_student)
    def _():
        inputs[...] = other[...]

    @pl.when(jnp.logical_not(mine_student))
    def _():
        project(student[...], heads, near, copies, inputs)

    step = min(half, 256)
    norm = jnp.zeros((slots, 1), jnp.float32)
    for index, z in enumerate(products(inputs, freqs, step)):
        block = slice(index * step, (index + 1) * step)
        cos_mine, sin_mine = cos[:, block], sin[:, block]
        cos_other, sin_other = cos_sin(z)
        mean_c = inverse * jnp.dot(
            same, (cos_other - cos_mine).astype(jnp.bfloat16), preferred_element_type=jnp.float32
        )
        mean_s = inverse * jnp.dot(
            same, (sin_other - sin_mine).astype(jnp.bfloat16), preferred_element_type=jnp.float32
        )
        norm += jnp.sum(mean_c * mean_c + mean_s * mean_s, axis=1, keepdims=True)
        cos_s = jnp.where(mine_student, cos_mine, cos_other)
        sin_s = jnp.where(mine_student, sin_mine, sin_other)
        grad_z[:, block] = (cos_s * mean_s - sin_s * mean_c).astype(jnp.bfloat16)
    cls = lax.broadcasted_iota(jnp.int32, (slots, cls_pad), 1).astype(jnp.float32) + 1.0
    total_norm = jnp.sum(jnp.where(cls == tag, norm, 0.0), axis=0, keepdims=True)
    norms[...] = total_norm
    carried = carry(total_norm, slots)
    out_rows = d_t // (n_dp * n_feat)
    block = n_dp // 2 * out_rows
    for offset in range(n_feat):
        target = lax.rem(feat + offset, n_feat)
        bit = lax.rem(target, bits)
        side = jnp.where(bit == 0, lax.rem(holder, 2), lax.rem(holder // 2, 2))
        if permuted:
            picked[...] = weights[offset]
        else:
            for index in range(n_dp):
                across, group = divmod(index, n_dp // 2)
                member = member_of(group, bit, 1 - side if across else side)
                start = pl.multiple_of((member * n_feat + target) * out_rows, out_rows)
                picked[index * out_rows : (index + 1) * out_rows, :] = freqs[
                    pl.ds(start, out_rows), :
                ]
        product = lax.dot_general(
            picked[...], grad_z[...], (((1,), (1,)), ((), ())), preferred_element_type=jnp.float32
        )
        here, there = grads[offset], grads[n_feat + offset]
        here[:block, :] = product[:block].astype(here.dtype)
        there[...] = product[block:].astype(there.dtype)
        if offset:
            here[block:, :] = carried


def summed(refs, size):
    total = refs[0][:size, :].astype(jnp.float32)
    for ref in refs[1:]:
        total += ref[:size, :].astype(jnp.float32)
    return total.astype(jnp.bfloat16)


def own_kernel(scale, divisor, *refs):
    grads, (norms, student, head, loss) = refs[:-4], refs[-4:]
    head[...] = scale * jnp.dot(
        summed(grads, head.shape[0]), student[...], preferred_element_type=jnp.float32
    )
    norm = norms[...]
    for ref in grads[1:]:
        norm += carried_norm(ref[ref.shape[0] - CARRIED :, :], norm.shape[1])
    loss[...] = (norm * (1.0 / divisor))[0, : loss.shape[0]]


def head_kernel(scale, *refs):
    grads, (own, student, head) = refs[:-3], refs[-3:]
    product = jnp.dot(
        summed(grads, head.shape[0]), student[...], preferred_element_type=jnp.float32
    )
    head[...] = (own[...] + product * scale).astype(jnp.bfloat16)


def total_kernel(parts, out):
    out[...] = jnp.sum(parts[...].astype(jnp.float32), axis=0)


def on_device(teacher, student, head, freqs, labels, class_slot):
    n_dp = lax.axis_size("dp")
    n_feat = lax.axis_size("feat")
    images, d_t = teacher.shape
    d_s = student.shape[1]
    half = freqs.shape[1]
    classes = class_slot.shape[0]
    cls_dev = classes // n_dp
    capacity = 2 * images // n_dp
    slots = n_dp * capacity
    cls_pad = up_to(cls_dev, slots)
    width = up_to(d_t + d_s + LANES, LANES * n_feat) // n_feat
    out_rows = d_t // (n_dp * n_feat)
    bits = 2 if n_dp % 4 == 0 else 1
    block = n_dp // 2 * out_rows
    vmem = pltpu.CompilerParams(vmem_limit_bytes=20 * 2**20)
    hbm = pl.BlockSpec(memory_space=pltpu.HBM)
    near = pl.BlockSpec(memory_space=pltpu.VMEM)

    def across(value, offset=0):
        moves = [
            (d * n_feat + f, (d ^ (1 << (f + offset) % n_feat % bits)) * n_feat + (f + offset) % n_feat)
            for d in range(n_dp)
            for f in range(n_feat)
        ]
        return lax.ppermute(value, ("dp", "feat"), moves)

    def shifted(value, offset):
        return lax.ppermute(
            value, "feat", [(f, (f + offset) % n_feat) for f in range(n_feat)]
        )

    sent, token = pl.pallas_call(
        functools.partial(route_kernel, cls_dev, capacity),
        out_shape=(
            jax.ShapeDtypeStruct((slots, width), jnp.bfloat16),
            jax.ShapeDtypeStruct((8, LANES), jnp.float32),
        ),
        in_specs=[hbm] * 4,
        scratch_shapes=[
            pltpu.VMEM((images,), jnp.int32),
            pltpu.VMEM((classes,), jnp.int32),
            pltpu.VMEM((images, width * n_feat), jnp.bfloat16),
            pltpu.SemaphoreType.DMA((4,)),
        ],
        compiler_params=pltpu.CompilerParams(vmem_limit_bytes=60 * 2**20),
        name="route",
    )(labels, class_slot, teacher, student)
    permuted = out_rows % 16 != 0
    weights = []
    if permuted:
        targets = (lax.axis_index("feat") + jnp.arange(n_feat)) % n_feat
        bit = (targets % bits)[:, None]
        group = jnp.tile(jnp.arange(n_dp // 2), 2)[None, :]
        side = (lax.axis_index("dp") >> bit) % 2
        side = jnp.where(jnp.arange(n_dp)[None, :] >= n_dp // 2, 1 - side, side)
        member = member_of(group, bit, side)
        lines = (member * n_feat + targets[:, None])[:, :, None] * out_rows + jnp.arange(out_rows)
        weights = [jnp.take(freqs, lines.reshape(n_feat, 2 * block), axis=0)]
    head_near, freqs_near = pl.pallas_call(
        load_kernel,
        out_shape=(
            jax.ShapeDtypeStruct(head.shape, jnp.bfloat16),
            jax.ShapeDtypeStruct(freqs.shape, jnp.bfloat16),
        ),
        in_specs=[hbm] * 3,
        scratch_shapes=[pltpu.SemaphoreType.DMA((2,))],
        compiler_params=vmem,
        name="load",
    )(head, freqs, token)
    heads = [head_near] + [shifted(head_near, k) for k in range(1, n_feat)]
    mine = lax.all_to_all(
        sent.reshape(n_dp, capacity, width), "dp", split_axis=0, concat_axis=0, tiled=True
    ).reshape(slots, width)
    role = None
    if n_feat == 2 and width == d_t:
        other = shifted(mine, 1)
        student_in, tags_in = pl.pallas_call(
            sort_kernel,
            out_shape=(
                jax.ShapeDtypeStruct((slots, d_s), jnp.bfloat16),
                jax.ShapeDtypeStruct((slots, LANES), jnp.bfloat16),
            ),
            compiler_params=vmem,
            name="sort",
        )(mine, other)
    else:
        role = 0
        everything = lax.all_gather(mine, "feat", axis=1, tiled=True)
        mine, student_in, tags_in = jnp.split(
            everything[:, : d_t + d_s + LANES], [d_t, d_t + d_s], axis=1
        )
        other = mine
    head_specs = [near] + [hbm] * (n_feat - 1)
    head_scratch = [
        pltpu.VMEM((n_feat - 1, *head.shape), jnp.bfloat16),
        pltpu.SemaphoreType.DMA((n_feat - 1,)),
    ]
    cos, sin = pl.pallas_call(
        functools.partial(first_kernel, role, n_feat, d_s),
        out_shape=(jax.ShapeDtypeStruct((slots, half), jnp.float32),) * 2,
        in_specs=[near] + head_specs + [near],
        scratch_shapes=[pltpu.VMEM((slots, d_t), jnp.bfloat16), *head_scratch],
        compiler_params=vmem,
        name="first",
    )(mine, *heads, freqs_near)
    cos, student_out = lax.optimization_barrier((cos, student_in))
    student_across = across(student_out)
    *grads, norms = pl.pallas_call(
        functools.partial(class_kernel, role, n_feat, n_dp, bits, cls_pad, permuted),
        out_shape=tuple(
            jax.ShapeDtypeStruct((block + CARRIED, slots), jnp.bfloat16)
            if k
            else jax.ShapeDtypeStruct((block, slots), jnp.float32)
            for k in range(n_feat)
        )
        + (jax.ShapeDtypeStruct((block, slots), jnp.bfloat16),) * n_feat
        + (jax.ShapeDtypeStruct((1, cls_pad), jnp.float32),),
        in_specs=[near] * 5 + head_specs + [near] * (1 + len(weights)),
        scratch_shapes=[
            pltpu.VMEM((slots, d_t), jnp.bfloat16),
            pltpu.VMEM((slots, half), jnp.bfloat16),
            pltpu.VMEM((2 * block, half), jnp.bfloat16),
            *head_scratch,
        ],
        compiler_params=vmem,
        name="classes",
    )(other, student_in, tags_in, cos, sin, *heads, freqs_near, *weights)
    here = [grads[0]] + [shifted(grads[k], k) for k in range(1, n_feat)]
    there = [across(grads[n_feat + k], k) for k in range(n_feat)]
    here, student_across = lax.optimization_barrier((here, student_across))
    scale = 1.0 / math.sqrt(images * n_dp)
    own, loss = pl.pallas_call(
        functools.partial(own_kernel, scale, 2.0 * half * n_feat),
        out_shape=(
            jax.ShapeDtypeStruct((block, d_s), jnp.float32),
            jax.ShapeDtypeStruct((cls_dev,), jnp.float32),
        ),
        compiler_params=vmem,
        name="own",
    )(*here, norms, student_in)
    partial_head = pl.pallas_call(
        functools.partial(head_kernel, scale),
        out_shape=jax.ShapeDtypeStruct((block, d_s), jnp.bfloat16),
        compiler_params=vmem,
        name="head",
    )(*there, own, student_across)
    received = lax.all_to_all(
        partial_head.reshape(n_dp // 2, out_rows, d_s),
        ("dp", "feat"),
        split_axis=0,
        concat_axis=0,
        tiled=True,
        axis_index_groups=[
            [d * n_feat + f for d in range(n_dp) if (d >> f % bits) % 2 == side]
            for f in range(n_feat)
            for side in range(2)
        ],
    )
    head_grad = pl.pallas_call(
        total_kernel,
        out_shape=jax.ShapeDtypeStruct((out_rows, d_s), jnp.float32),
        compiler_params=vmem,
        name="total",
    )(received)
    return (head_grad, loss)


def solution(mesh):
    in_specs = (P("dp", None), P("dp", None), P(None, "feat"), P(None, "feat"), P("dp"), P())
    out_specs = (P(("dp", "feat"), None), P("dp"))
    return jax.shard_map(
        on_device, mesh=mesh, in_specs=in_specs, out_specs=out_specs, check_vma=False
    )
```

```python
import functools
import math

import jax
import jax.numpy as jnp
from jax import lax
from jax.experimental import pallas as pl
from jax.experimental.pallas import tpu as pltpu
from jax.sharding import PartitionSpec as P

LANES = 128
CARRIED = 16
PIECES = 3
TURN = 1.0 / (2.0 * math.pi)
ROUNDER = 1.5 * 2.0**23
SINE = (6.283164044217864, -41.337142357601536, 81.3407683703199, -70.9934277613874)


def up_to(value, multiple):
    return -(-value // multiple) * multiple


def quarter_sine(angle):
    square = angle * angle
    value = jnp.float32(SINE[-1])
    for factor in SINE[-2::-1]:
        value = value * square + factor
    return value * angle


def cos_sin(z):
    turns = z * TURN
    part = turns - ((turns + ROUNDER) - ROUNDER)
    wave = jnp.minimum(jnp.maximum(part, -0.5 - part), 0.5 - part)
    return quarter_sine(0.25 - jnp.abs(part)), quarter_sine(wave)


def to_row(column, size):
    first = lax.broadcasted_iota(jnp.int32, (size, size), 0)
    second = lax.broadcasted_iota(jnp.int32, (size, size), 1)
    return jnp.sum(jnp.where(first == second, column, 0.0), axis=0, keepdims=True)


def to_column(row, size):
    first = lax.broadcasted_iota(jnp.int32, (size, size), 0)
    second = lax.broadcasted_iota(jnp.int32, (size, size), 1)
    return jnp.sum(jnp.where(first == second, row, 0.0), axis=1, keepdims=True)


def table_entries(table, chunk):
    start = chunk * LANES
    size = min(LANES, table.shape[0] - start)
    entries = table[pl.ds(start, size)].astype(jnp.float32)
    if size < LANES:
        entries = jnp.concatenate([entries, jnp.zeros((LANES - size,), jnp.float32)])
    return entries.reshape(1, LANES)


def route_kernel(
    cls_dev, capacity, labels_in, table_in, teacher, student, out, token, labels, table, rows, sems
):
    images, d_t = teacher.shape
    d_s = student.shape[1]
    slots, width = out.shape
    copies = [
        pltpu.make_async_copy(labels_in, labels, sems.at[0]),
        pltpu.make_async_copy(table_in, table, sems.at[1]),
        pltpu.make_async_copy(teacher, rows.at[:, :d_t], sems.at[2]),
        pltpu.make_async_copy(student, rows.at[:, d_t : d_t + d_s], sems.at[3]),
    ]
    for copy in copies:
        copy.start()
    lane = lax.broadcasted_iota(jnp.int32, (images, LANES), 1)
    lane_f = lane.astype(jnp.float32)
    copies[0].wait()
    label = to_column(labels[...].astype(jnp.float32).reshape(1, images), images)
    label = jnp.broadcast_to(label, (images, LANES))
    copies[1].wait()
    found = jnp.zeros((images, LANES), jnp.float32)
    for chunk in range(pl.cdiv(table.shape[0], LANES)):
        entries = table_entries(table, chunk)
        found += jnp.where(lane_f + float(chunk * LANES) == label, entries, 0.0)
    position = jnp.sum(found, axis=1, keepdims=True)
    owner = jnp.floor((position + 0.5) * (1.0 / cls_dev))
    tag = position - owner * cls_dev + 1.0
    owner_row = to_row(owner, images)
    first = lax.broadcasted_iota(jnp.int32, (images, images), 0)
    second = lax.broadcasted_iota(jnp.int32, (images, images), 1)
    before = jnp.logical_and(first < second, owner == owner_row)
    rank = jnp.sum(jnp.where(before, 1.0, 0.0), axis=0, keepdims=True)
    slot = owner_row * float(capacity) + rank
    slot_id = lax.broadcasted_iota(jnp.int32, (slots, images), 0).astype(jnp.float32)
    pick = jnp.where(slot_id == slot, 1.0, 0.0).astype(jnp.bfloat16)
    high = jnp.floor(tag * (1.0 / 32.0))
    tags = jnp.where(lane == 0, high, jnp.where(lane == 1, tag - 32.0 * high, 0.0))
    rows[:, d_t + d_s : d_t + d_s + LANES] = tags.astype(jnp.bfloat16)
    rows[:, d_t + d_s + LANES :] = jnp.zeros(
        (images, rows.shape[1] - d_t - d_s - LANES), jnp.bfloat16
    )
    token[...] = jnp.zeros_like(token)
    copies[2].wait()
    copies[3].wait()
    start = pl.multiple_of(lax.axis_index("feat") * width, LANES)
    out[...] = jnp.dot(
        pick, rows[:, pl.ds(start, width)], preferred_element_type=jnp.float32
    ).astype(jnp.bfloat16)


def load_kernel(head_in, freqs_in, _, head, freqs, sems):
    copies = [
        pltpu.make_async_copy(head_in, head, sems.at[0]),
        pltpu.make_async_copy(freqs_in, freqs, sems.at[1]),
    ]
    for copy in copies:
        copy.start()
    for copy in copies:
        copy.wait()


def carry(norm, lanes):
    row = lax.broadcasted_iota(jnp.int32, (CARRIED, lanes), 0)
    block, index = jnp.zeros((CARRIED, lanes), jnp.float32), 0
    for _ in range(PIECES):
        piece = norm.astype(jnp.bfloat16).astype(jnp.float32)
        norm = norm - piece
        for start in range(0, norm.shape[1], lanes):
            block = jnp.where(row == index, piece[:, start : start + lanes], block)
            index += 1
    return block.astype(jnp.bfloat16)


def carried_norm(block, size):
    lanes = block.shape[1]
    values = block.astype(jnp.float32)
    width = size // lanes
    found = []
    for part in range(width):
        rows = [values[p * width + part : p * width + part + 1, :] for p in range(PIECES)]
        found.append(sum(rows[1:], rows[0]))
    return jnp.concatenate(found, axis=1) if width > 1 else found[0]


def place_of(own, offset, count):
    return lax.rem(own + (count - offset), count)


def project(student, head, others, projected):
    feat = lax.axis_index("feat")
    part = head.shape[1]
    count = projected.shape[1] // part
    for offset in range(count):
        weight = others[offset - 1] if offset else head[...]
        start = pl.multiple_of(place_of(feat, offset, count) * part, LANES)
        projected[:, pl.ds(start, part)] = jnp.dot(
            student, weight, preferred_element_type=jnp.float32
        ).astype(jnp.bfloat16)


def products(inputs, freqs, step):
    return [
        jnp.dot(
            inputs[...], freqs[:, column : column + step], preferred_element_type=jnp.float32
        )
        for column in range(0, freqs.shape[1], step)
    ]


def is_role(role, index):
    return (lax.axis_index("feat") if role is None else role) == index


def first_kernel(role, n_feat, d_s, rows, *refs):
    heads, (freqs, cos, sin, near, inputs, sems) = refs[:n_feat], refs[n_feat:]
    is_student = is_role(role, 1)
    copies = [
        pltpu.make_async_copy(heads[k], near.at[k - 1], sems.at[k - 1]) for k in range(1, n_feat)
    ]
    for copy in copies:
        copy.start()
    part = freqs.shape[0] // n_feat
    own = pl.multiple_of(lax.axis_index("feat") * part, LANES)

    @pl.when(is_student)
    def _():
        inputs[:, pl.ds(own, part)] = jnp.dot(
            rows[:, :d_s], heads[0][...], preferred_element_type=jnp.float32
        ).astype(jnp.bfloat16)

    @pl.when(jnp.logical_not(is_student))
    def _():
        inputs[...] = rows[...]

    step = min(freqs.shape[1], 256)
    blocks = [slice(c, c + step) for c in range(0, freqs.shape[1], step)]
    found = [0.0] * len(blocks)
    for offset in range(n_feat):
        start = pl.multiple_of(place_of(lax.axis_index("feat"), offset, n_feat) * part, LANES)
        if offset:

            @pl.when(is_student)
            def _():
                copies[offset - 1].wait()
                inputs[:, pl.ds(start, part)] = jnp.dot(
                    rows[:, :d_s], near[offset - 1], preferred_element_type=jnp.float32
                ).astype(jnp.bfloat16)

        for index, block in enumerate(blocks):
            found[index] += jnp.dot(
                inputs[:, pl.ds(start, part)],
                freqs[pl.ds(start, part), block],
                preferred_element_type=jnp.float32,
            )
    for index, block in enumerate(blocks):
        cos[:, block], sin[:, block] = cos_sin(found[index])

    @pl.when(jnp.logical_not(is_student))
    def _():
        for copy in copies:
            copy.wait()


def sort_kernel(mine, other, student, tags):
    d_s = student.shape[1]

    def split(rows):
        student[...] = rows[:, :d_s]
        tags[...] = rows[:, d_s : d_s + LANES]

    pl.when(is_role(None, 1))(lambda: split(mine))
    pl.when(is_role(None, 0))(lambda: split(other))


def member_of(group, bit, side):
    low = group * 2 + side
    high = group // 2 * 4 + side * 2 + group % 2
    return jnp.where(bit == 0, low, high)


def class_kernel(
    role, n_feat, n_dp, bits, cls_pad, permuted, other, student, tags_in, cos, sin, *refs
):
    head, others, freqs, refs = refs[0], refs[1], refs[2], refs[3:]
    if permuted:
        weights, refs = refs[0], refs[1:]
    grads, refs = refs[: 2 * n_feat], refs[2 * n_feat :]
    norms, inputs, grad_z, picked = refs
    feat = lax.axis_index("feat")
    holder = lax.axis_index("dp")
    mine_student = is_role(role, 1)
    slots, d_t = inputs.shape
    half = freqs.shape[1]

    tags = tags_in[...].astype(jnp.float32)
    lane = lax.broadcasted_iota(jnp.int32, (slots, LANES), 1)
    tag = jnp.sum(
        tags * jnp.where(lane == 0, 32.0, jnp.where(lane == 1, 1.0, 0.0)), axis=1, keepdims=True
    )
    tag_row = to_row(tag, slots)
    same = jnp.where(jnp.logical_and(tag == tag_row, tag > 0.0), 1.0, 0.0)
    inverse = 1.0 / jnp.maximum(jnp.sum(same, axis=1, keepdims=True), 1.0)
    inverse = jnp.where(mine_student, -inverse, inverse)
    same = same.astype(jnp.bfloat16)

    @pl.when(mine_student)
    def _():
        inputs[...] = other[...]

    @pl.when(jnp.logical_not(mine_student))
    def _():
        project(student[...], head, others, inputs)

    step = min(half, 256)
    norm = jnp.zeros((slots, 1), jnp.float32)
    for index, z in enumerate(products(inputs, freqs, step)):
        block = slice(index * step, (index + 1) * step)
        cos_mine, sin_mine = cos[:, block], sin[:, block]
        cos_other, sin_other = cos_sin(z)
        mean_c = inverse * jnp.dot(
            same, (cos_other - cos_mine).astype(jnp.bfloat16), preferred_element_type=jnp.float32
        )
        mean_s = inverse * jnp.dot(
            same, (sin_other - sin_mine).astype(jnp.bfloat16), preferred_element_type=jnp.float32
        )
        norm += jnp.sum(mean_c * mean_c + mean_s * mean_s, axis=1, keepdims=True)
        cos_s = jnp.where(mine_student, cos_mine, cos_other)
        sin_s = jnp.where(mine_student, sin_mine, sin_other)
        grad_z[:, block] = (cos_s * mean_s - sin_s * mean_c).astype(jnp.bfloat16)
    cls = lax.broadcasted_iota(jnp.int32, (slots, cls_pad), 1).astype(jnp.float32) + 1.0
    total_norm = jnp.sum(jnp.where(cls == tag, norm, 0.0), axis=0, keepdims=True)
    norms[...] = total_norm
    carried = carry(total_norm, slots)
    out_rows = d_t // (n_dp * n_feat)
    block = n_dp // 2 * out_rows
    for offset in range(n_feat):
        target = lax.rem(feat + offset, n_feat)
        bit = lax.rem(target, bits)
        side = jnp.where(bit == 0, lax.rem(holder, 2), lax.rem(holder // 2, 2))
        if permuted:
            picked[...] = weights[offset]
        else:
            for index in range(n_dp):
                across, group = divmod(index, n_dp // 2)
                member = member_of(group, bit, 1 - side if across else side)
                start = pl.multiple_of((member * n_feat + target) * out_rows, out_rows)
                picked[index * out_rows : (index + 1) * out_rows, :] = freqs[
                    pl.ds(start, out_rows), :
                ]
        product = lax.dot_general(
            picked[...], grad_z[...], (((1,), (1,)), ((), ())), preferred_element_type=jnp.float32
        )
        here, there = grads[offset], grads[n_feat + offset]
        here[:block, :] = product[:block].astype(here.dtype)
        there[...] = product[block:].astype(there.dtype)
        if offset:
            here[block:, :] = carried


def summed(refs, size):
    total = refs[0][:size, :].astype(jnp.float32)
    for ref in refs[1:]:
        total += ref[:size, :].astype(jnp.float32)
    return total.astype(jnp.bfloat16)


def fold_kernel(*refs):
    refs[-1][...] = summed(refs[:-1], refs[-1].shape[0])


def own_kernel(scale, divisor, *refs):
    grads, (norms, student, head, loss) = refs[:-4], refs[-4:]
    head[...] = scale * jnp.dot(
        summed(grads, head.shape[0]), student[...], preferred_element_type=jnp.float32
    )
    norm = norms[...]
    for ref in grads[1:]:
        norm += carried_norm(ref[ref.shape[0] - CARRIED :, :], norm.shape[1])
    loss[...] = (norm * (1.0 / divisor))[0, : loss.shape[0]]


def head_kernel(scale, *refs):
    grads, (own, student, head) = refs[:-3], refs[-3:]
    product = jnp.dot(
        summed(grads, head.shape[0]), student[...], preferred_element_type=jnp.float32
    )
    head[...] = (own[...] + product * scale).astype(jnp.bfloat16)


def total_kernel(parts, out):
    out[...] = jnp.sum(parts[...].astype(jnp.float32), axis=0)


def on_device(teacher, student, head, freqs, labels, class_slot):
    n_dp = lax.axis_size("dp")
    n_feat = lax.axis_size("feat")
    images, d_t = teacher.shape
    d_s = student.shape[1]
    half = freqs.shape[1]
    classes = class_slot.shape[0]
    cls_dev = classes // n_dp
    capacity = 2 * images // n_dp
    slots = n_dp * capacity
    cls_pad = up_to(cls_dev, slots)
    width = up_to(d_t + d_s + LANES, LANES * n_feat) // n_feat
    out_rows = d_t // (n_dp * n_feat)
    bits = 2 if n_dp % 4 == 0 else 1
    block = n_dp // 2 * out_rows
    vmem = pltpu.CompilerParams(vmem_limit_bytes=20 * 2**20)
    hbm = pl.BlockSpec(memory_space=pltpu.HBM)
    near = pl.BlockSpec(memory_space=pltpu.VMEM)

    def across(value, offset=0):
        moves = [
            (d * n_feat + f, (d ^ (1 << (f + offset) % n_feat % bits)) * n_feat + (f + offset) % n_feat)
            for d in range(n_dp)
            for f in range(n_feat)
        ]
        return lax.ppermute(value, ("dp", "feat"), moves)

    def shifted(value, offset):
        return lax.ppermute(
            value, "feat", [(f, (f + offset) % n_feat) for f in range(n_feat)]
        )

    sent, token = pl.pallas_call(
        functools.partial(route_kernel, cls_dev, capacity),
        out_shape=(
            jax.ShapeDtypeStruct((slots, width), jnp.bfloat16),
            jax.ShapeDtypeStruct((8, LANES), jnp.float32),
        ),
        in_specs=[hbm] * 4,
        scratch_shapes=[
            pltpu.VMEM((images,), jnp.int32),
            pltpu.VMEM((classes,), jnp.int32),
            pltpu.VMEM((images, width * n_feat), jnp.bfloat16),
            pltpu.SemaphoreType.DMA((4,)),
        ],
        compiler_params=pltpu.CompilerParams(vmem_limit_bytes=60 * 2**20),
        name="route",
    )(labels, class_slot, teacher, student)
    permuted = out_rows % 16 != 0
    weights = []
    if permuted:
        targets = (lax.axis_index("feat") + jnp.arange(n_feat)) % n_feat
        bit = (targets % bits)[:, None]
        group = jnp.tile(jnp.arange(n_dp // 2), 2)[None, :]
        side = (lax.axis_index("dp") >> bit) % 2
        side = jnp.where(jnp.arange(n_dp)[None, :] >= n_dp // 2, 1 - side, side)
        member = member_of(group, bit, side)
        lines = (member * n_feat + targets[:, None])[:, :, None] * out_rows + jnp.arange(out_rows)
        weights = [jnp.take(freqs, lines.reshape(n_feat, 2 * block), axis=0)]
    head_near, freqs_near = pl.pallas_call(
        load_kernel,
        out_shape=(
            jax.ShapeDtypeStruct(head.shape, jnp.bfloat16),
            jax.ShapeDtypeStruct(freqs.shape, jnp.bfloat16),
        ),
        in_specs=[hbm] * 3,
        scratch_shapes=[pltpu.SemaphoreType.DMA((2,))],
        compiler_params=vmem,
        name="load",
    )(head, freqs, token)
    heads = [head_near] + [shifted(head_near, k) for k in range(1, n_feat)]
    mine = lax.all_to_all(
        sent.reshape(n_dp, capacity, width), "dp", split_axis=0, concat_axis=0, tiled=True
    ).reshape(slots, width)
    role = None
    if n_feat == 2 and width == d_t:
        other = shifted(mine, 1)
        student_in, tags_in = pl.pallas_call(
            sort_kernel,
            out_shape=(
                jax.ShapeDtypeStruct((slots, d_s), jnp.bfloat16),
                jax.ShapeDtypeStruct((slots, LANES), jnp.bfloat16),
            ),
            compiler_params=vmem,
            name="sort",
        )(mine, other)
    else:
        role = 0
        everything = lax.all_gather(mine, "feat", axis=1, tiled=True)
        mine, student_in, tags_in = jnp.split(
            everything[:, : d_t + d_s + LANES], [d_t, d_t + d_s], axis=1
        )
        other = mine
    cos, sin, head_others = pl.pallas_call(
        functools.partial(first_kernel, role, n_feat, d_s),
        out_shape=(jax.ShapeDtypeStruct((slots, half), jnp.float32),) * 2
        + (jax.ShapeDtypeStruct((n_feat - 1, *head.shape), jnp.bfloat16),),
        in_specs=[near] * 2 + [hbm] * (n_feat - 1) + [near],
        scratch_shapes=[
            pltpu.VMEM((slots, d_t), jnp.bfloat16),
            pltpu.SemaphoreType.DMA((n_feat - 1,)),
        ],
        compiler_params=vmem,
        name="first",
    )(mine, *heads, freqs_near)
    cos, student_out = lax.optimization_barrier((cos, student_in))
    student_across = across(student_out)
    *grads, norms = pl.pallas_call(
        functools.partial(class_kernel, role, n_feat, n_dp, bits, cls_pad, permuted),
        out_shape=tuple(
            jax.ShapeDtypeStruct((block + CARRIED, slots), jnp.bfloat16)
            if k
            else jax.ShapeDtypeStruct((block, slots), jnp.float32)
            for k in range(n_feat)
        )
        + tuple(
            jax.ShapeDtypeStruct((block, slots), jnp.bfloat16 if k else jnp.float32)
            for k in range(n_feat)
        )
        + (jax.ShapeDtypeStruct((1, cls_pad), jnp.float32),),
        in_specs=[near] * (8 + len(weights)),
        scratch_shapes=[
            pltpu.VMEM((slots, d_t), jnp.bfloat16),
            pltpu.VMEM((slots, half), jnp.bfloat16),
            pltpu.VMEM((2 * block, half), jnp.bfloat16),
        ],
        compiler_params=vmem,
        name="classes",
    )(
        other, student_in, tags_in, cos, sin, heads[0], head_others, freqs_near, *weights
    )
    here = [grads[0]] + [shifted(grads[k], k) for k in range(1, n_feat)]
    there = [grads[n_feat]] + [shifted(grads[n_feat + k], k) for k in range(1, n_feat)]
    folded = pl.pallas_call(
        fold_kernel,
        out_shape=jax.ShapeDtypeStruct((block, slots), jnp.bfloat16),
        compiler_params=vmem,
        name="fold",
    )(*there)
    there = [across(folded)]
    here, student_across = lax.optimization_barrier((here, student_across))
    scale = 1.0 / math.sqrt(images * n_dp)
    own, loss = pl.pallas_call(
        functools.partial(own_kernel, scale, 2.0 * half * n_feat),
        out_shape=(
            jax.ShapeDtypeStruct((block, d_s), jnp.float32),
            jax.ShapeDtypeStruct((cls_dev,), jnp.float32),
        ),
        compiler_params=vmem,
        name="own",
    )(*here, norms, student_in)
    partial_head = pl.pallas_call(
        functools.partial(head_kernel, scale),
        out_shape=jax.ShapeDtypeStruct((block, d_s), jnp.bfloat16),
        compiler_params=vmem,
        name="head",
    )(*there, own, student_across)
    received = lax.all_to_all(
        partial_head.reshape(n_dp // 2, out_rows, d_s),
        ("dp", "feat"),
        split_axis=0,
        concat_axis=0,
        tiled=True,
        axis_index_groups=[
            [d * n_feat + f for d in range(n_dp) if (d >> f % bits) % 2 == side]
            for f in range(n_feat)
            for side in range(2)
        ],
    )
    head_grad = pl.pallas_call(
        total_kernel,
        out_shape=jax.ShapeDtypeStruct((out_rows, d_s), jnp.float32),
        compiler_params=vmem,
        name="total",
    )(received)
    return (head_grad, loss)


def solution(mesh):
    in_specs = (P("dp", None), P("dp", None), P(None, "feat"), P(None, "feat"), P("dp"), P())
    out_specs = (P(("dp", "feat"), None), P("dp"))
    return jax.shard_map(
        on_device, mesh=mesh, in_specs=in_specs, out_specs=out_specs, check_vma=False
    )
```

```python
import functools
import math

import jax
import jax.numpy as jnp
from jax import lax
from jax.experimental import pallas as pl
from jax.experimental.pallas import tpu as pltpu
from jax.sharding import PartitionSpec as P

LANES = 128
CARRIED = 16
PIECES = 3
TURN = 1.0 / (2.0 * math.pi)
SINE = (6.283164044217864, -41.337142357601536, 81.3407683703199, -70.9934277613874)


def up_to(value, multiple):
    return -(-value // multiple) * multiple


def quarter_sine(angle):
    square = angle * angle
    value = jnp.float32(SINE[-1])
    for factor in SINE[-2::-1]:
        value = value * square + factor
    return value * angle


def cos_sin(z):
    turns = z * TURN
    part = turns - lax.round(turns, lax.RoundingMethod.TO_NEAREST_EVEN)
    wave = jnp.minimum(jnp.maximum(part, -0.5 - part), 0.5 - part)
    return quarter_sine(0.25 - jnp.abs(part)), quarter_sine(wave)


def to_row(column, size):
    first = lax.broadcasted_iota(jnp.int32, (size, size), 0)
    second = lax.broadcasted_iota(jnp.int32, (size, size), 1)
    return jnp.sum(jnp.where(first == second, column, 0.0), axis=0, keepdims=True)


def to_column(row, size):
    first = lax.broadcasted_iota(jnp.int32, (size, size), 0)
    second = lax.broadcasted_iota(jnp.int32, (size, size), 1)
    return jnp.sum(jnp.where(first == second, row, 0.0), axis=1, keepdims=True)


def table_entries(table, chunk):
    start = chunk * LANES
    size = min(LANES, table.shape[0] - start)
    entries = table[pl.ds(start, size)].astype(jnp.float32)
    if size < LANES:
        entries = jnp.concatenate([entries, jnp.zeros((LANES - size,), jnp.float32)])
    return entries.reshape(1, LANES)


def route_kernel(
    cls_dev, capacity, labels_in, table_in, teacher, student, out, token, labels, table, rows, sems
):
    images, d_t = teacher.shape
    d_s = student.shape[1]
    slots, width = out.shape
    copies = [
        pltpu.make_async_copy(labels_in, labels, sems.at[0]),
        pltpu.make_async_copy(table_in, table, sems.at[1]),
        pltpu.make_async_copy(teacher, rows.at[:, :d_t], sems.at[2]),
        pltpu.make_async_copy(student, rows.at[:, d_t : d_t + d_s], sems.at[3]),
    ]
    for copy in copies:
        copy.start()
    lane = lax.broadcasted_iota(jnp.int32, (images, LANES), 1)
    lane_f = lane.astype(jnp.float32)
    copies[0].wait()
    label = to_column(labels[...].astype(jnp.float32).reshape(1, images), images)
    label = jnp.broadcast_to(label, (images, LANES))
    copies[1].wait()
    found = jnp.zeros((images, LANES), jnp.float32)
    for chunk in range(pl.cdiv(table.shape[0], LANES)):
        entries = table_entries(table, chunk)
        found += jnp.where(lane_f + float(chunk * LANES) == label, entries, 0.0)
    position = jnp.sum(found, axis=1, keepdims=True)
    owner = jnp.floor((position + 0.5) * (1.0 / cls_dev))
    tag = position - owner * cls_dev + 1.0
    owner_row = to_row(owner, images)
    first = lax.broadcasted_iota(jnp.int32, (images, images), 0)
    second = lax.broadcasted_iota(jnp.int32, (images, images), 1)
    before = jnp.logical_and(first < second, owner == owner_row)
    rank = jnp.sum(jnp.where(before, 1.0, 0.0), axis=0, keepdims=True)
    slot = owner_row * float(capacity) + rank
    slot_id = lax.broadcasted_iota(jnp.int32, (slots, images), 0).astype(jnp.float32)
    pick = jnp.where(slot_id == slot, 1.0, 0.0).astype(jnp.bfloat16)
    high = jnp.floor(tag * (1.0 / 32.0))
    tags = jnp.where(lane == 0, high, jnp.where(lane == 1, tag - 32.0 * high, 0.0))
    rows[:, d_t + d_s : d_t + d_s + LANES] = tags.astype(jnp.bfloat16)
    rows[:, d_t + d_s + LANES :] = jnp.zeros(
        (images, rows.shape[1] - d_t - d_s - LANES), jnp.bfloat16
    )
    token[...] = jnp.zeros_like(token)
    copies[2].wait()
    copies[3].wait()
    start = pl.multiple_of(lax.axis_index("feat") * width, LANES)
    out[...] = jnp.dot(
        pick, rows[:, pl.ds(start, width)], preferred_element_type=jnp.float32
    ).astype(jnp.bfloat16)


def load_kernel(head_in, freqs_in, _, head, freqs, sems):
    copies = [
        pltpu.make_async_copy(head_in, head, sems.at[0]),
        pltpu.make_async_copy(freqs_in, freqs, sems.at[1]),
    ]
    for copy in copies:
        copy.start()
    for copy in copies:
        copy.wait()


def carry(norm, lanes):
    row = lax.broadcasted_iota(jnp.int32, (CARRIED, lanes), 0)
    block, index = jnp.zeros((CARRIED, lanes), jnp.float32), 0
    for _ in range(PIECES):
        piece = norm.astype(jnp.bfloat16).astype(jnp.float32)
        norm = norm - piece
        for start in range(0, norm.shape[1], lanes):
            block = jnp.where(row == index, piece[:, start : start + lanes], block)
            index += 1
    return block.astype(jnp.bfloat16)


def carried_norm(block, size):
    lanes = block.shape[1]
    values = block.astype(jnp.float32)
    width = size // lanes
    found = []
    for part in range(width):
        rows = [values[p * width + part : p * width + part + 1, :] for p in range(PIECES)]
        found.append(sum(rows[1:], rows[0]))
    return jnp.concatenate(found, axis=1) if width > 1 else found[0]


def place_of(own, offset, count):
    return lax.rem(own + (count - offset), count)


def project(student, head, others, projected):
    feat = lax.axis_index("feat")
    part = head.shape[1]
    count = projected.shape[1] // part
    for offset in range(count):
        weight = others[offset - 1] if offset else head[...]
        start = pl.multiple_of(place_of(feat, offset, count) * part, LANES)
        projected[:, pl.ds(start, part)] = jnp.dot(
            student, weight, preferred_element_type=jnp.float32
        ).astype(jnp.bfloat16)


def products(inputs, freqs, step):
    return [
        jnp.dot(
            inputs[...], freqs[:, column : column + step], preferred_element_type=jnp.float32
        )
        for column in range(0, freqs.shape[1], step)
    ]


def is_role(role, index):
    return (lax.axis_index("feat") if role is None else role) == index


def first_kernel(role, n_feat, d_s, rows, *refs):
    heads, (freqs, cos, sin, near, inputs, sems) = refs[:n_feat], refs[n_feat:]
    is_student = is_role(role, 1)
    copies = [
        pltpu.make_async_copy(heads[k], near.at[k - 1], sems.at[k - 1]) for k in range(1, n_feat)
    ]
    for copy in copies:
        copy.start()
    part = freqs.shape[0] // n_feat
    own = pl.multiple_of(lax.axis_index("feat") * part, LANES)

    @pl.when(is_student)
    def _():
        inputs[:, pl.ds(own, part)] = jnp.dot(
            rows[:, :d_s], heads[0][...], preferred_element_type=jnp.float32
        ).astype(jnp.bfloat16)

    @pl.when(jnp.logical_not(is_student))
    def _():
        inputs[...] = rows[...]

    step = min(freqs.shape[1], 256)
    blocks = [slice(c, c + step) for c in range(0, freqs.shape[1], step)]
    found = [0.0] * len(blocks)
    for offset in range(n_feat):
        start = pl.multiple_of(place_of(lax.axis_index("feat"), offset, n_feat) * part, LANES)
        if offset:

            @pl.when(is_student)
            def _():
                copies[offset - 1].wait()
                inputs[:, pl.ds(start, part)] = jnp.dot(
                    rows[:, :d_s], near[offset - 1], preferred_element_type=jnp.float32
                ).astype(jnp.bfloat16)

        for index, block in enumerate(blocks):
            found[index] += jnp.dot(
                inputs[:, pl.ds(start, part)],
                freqs[pl.ds(start, part), block],
                preferred_element_type=jnp.float32,
            )
    for index, block in enumerate(blocks):
        cos[:, block], sin[:, block] = cos_sin(found[index])

    @pl.when(jnp.logical_not(is_student))
    def _():
        for copy in copies:
            copy.wait()


def sort_kernel(mine, other, student, tags):
    d_s = student.shape[1]

    def split(rows):
        student[...] = rows[:, :d_s]
        tags[...] = rows[:, d_s : d_s + LANES]

    pl.when(is_role(None, 1))(lambda: split(mine))
    pl.when(is_role(None, 0))(lambda: split(other))


def member_of(group, bit, side):
    low = group * 2 + side
    high = group // 2 * 4 + side * 2 + group % 2
    return jnp.where(bit == 0, low, high)


def class_kernel(
    role, n_feat, n_dp, bits, cls_pad, permuted, other, student, tags_in, cos, sin, *refs
):
    head, others, freqs, refs = refs[0], refs[1], refs[2], refs[3:]
    if permuted:
        weights, refs = refs[0], refs[1:]
    grads, refs = refs[: 2 * n_feat], refs[2 * n_feat :]
    norms, inputs, grad_z, picked = refs
    feat = lax.axis_index("feat")
    holder = lax.axis_index("dp")
    mine_student = is_role(role, 1)
    slots, d_t = inputs.shape
    half = freqs.shape[1]

    tags = tags_in[...].astype(jnp.float32)
    lane = lax.broadcasted_iota(jnp.int32, (slots, LANES), 1)
    tag = jnp.sum(
        tags * jnp.where(lane == 0, 32.0, jnp.where(lane == 1, 1.0, 0.0)), axis=1, keepdims=True
    )
    tag_row = to_row(tag, slots)
    same = jnp.where(jnp.logical_and(tag == tag_row, tag > 0.0), 1.0, 0.0)
    inverse = 1.0 / jnp.maximum(jnp.sum(same, axis=1, keepdims=True), 1.0)
    inverse = jnp.where(mine_student, -inverse, inverse)
    same = same.astype(jnp.bfloat16)

    @pl.when(mine_student)
    def _():
        inputs[...] = other[...]

    @pl.when(jnp.logical_not(mine_student))
    def _():
        project(student[...], head, others, inputs)

    step = min(half, 256)
    norm = jnp.zeros((slots, 1), jnp.float32)
    for index, z in enumerate(products(inputs, freqs, step)):
        block = slice(index * step, (index + 1) * step)
        cos_mine, sin_mine = cos[:, block], sin[:, block]
        cos_other, sin_other = cos_sin(z)
        mean_c = inverse * jnp.dot(
            same, (cos_other - cos_mine).astype(jnp.bfloat16), preferred_element_type=jnp.float32
        )
        mean_s = inverse * jnp.dot(
            same, (sin_other - sin_mine).astype(jnp.bfloat16), preferred_element_type=jnp.float32
        )
        norm += jnp.sum(mean_c * mean_c + mean_s * mean_s, axis=1, keepdims=True)
        cos_s = jnp.where(mine_student, cos_mine, cos_other)
        sin_s = jnp.where(mine_student, sin_mine, sin_other)
        grad_z[:, block] = (cos_s * mean_s - sin_s * mean_c).astype(jnp.bfloat16)
    cls = lax.broadcasted_iota(jnp.int32, (slots, cls_pad), 1).astype(jnp.float32) + 1.0
    total_norm = jnp.sum(jnp.where(cls == tag, norm, 0.0), axis=0, keepdims=True)
    norms[...] = total_norm
    carried = carry(total_norm, slots)
    out_rows = d_t // (n_dp * n_feat)
    block = n_dp // 2 * out_rows
    for offset in range(n_feat):
        target = lax.rem(feat + offset, n_feat)
        bit = lax.rem(target, bits)
        side = jnp.where(bit == 0, lax.rem(holder, 2), lax.rem(holder // 2, 2))
        if permuted:
            picked[...] = weights[offset]
        else:
            for index in range(n_dp):
                across, group = divmod(index, n_dp // 2)
                member = member_of(group, bit, 1 - side if across else side)
                start = pl.multiple_of((member * n_feat + target) * out_rows, out_rows)
                picked[index * out_rows : (index + 1) * out_rows, :] = freqs[
                    pl.ds(start, out_rows), :
                ]
        product = lax.dot_general(
            picked[...], grad_z[...], (((1,), (1,)), ((), ())), preferred_element_type=jnp.float32
        )
        here, there = grads[offset], grads[n_feat + offset]
        here[:block, :] = product[:block].astype(here.dtype)
        there[...] = product[block:].astype(there.dtype)
        if offset:
            here[block:, :] = carried


def summed(refs, size):
    total = refs[0][:size, :].astype(jnp.float32)
    for ref in refs[1:]:
        total += ref[:size, :].astype(jnp.float32)
    return total.astype(jnp.bfloat16)


def fold_kernel(*refs):
    refs[-1][...] = summed(refs[:-1], refs[-1].shape[0])


def own_kernel(scale, divisor, *refs):
    grads, (norms, student, head, loss) = refs[:-4], refs[-4:]
    head[...] = scale * jnp.dot(
        summed(grads, head.shape[0]), student[...], preferred_element_type=jnp.float32
    )
    norm = norms[...]
    for ref in grads[1:]:
        norm += carried_norm(ref[ref.shape[0] - CARRIED :, :], norm.shape[1])
    loss[...] = (norm * (1.0 / divisor))[0, : loss.shape[0]]


def head_kernel(scale, *refs):
    grads, (own, student, head) = refs[:-3], refs[-3:]
    product = jnp.dot(
        summed(grads, head.shape[0]), student[...], preferred_element_type=jnp.float32
    )
    head[...] = (own[...] + product * scale).astype(jnp.bfloat16)


def total_kernel(parts, out):
    out[...] = jnp.sum(parts[...].astype(jnp.float32), axis=0)


def on_device(teacher, student, head, freqs, labels, class_slot):
    n_dp = lax.axis_size("dp")
    n_feat = lax.axis_size("feat")
    images, d_t = teacher.shape
    d_s = student.shape[1]
    half = freqs.shape[1]
    classes = class_slot.shape[0]
    cls_dev = classes // n_dp
    capacity = 2 * images // n_dp
    slots = n_dp * capacity
    cls_pad = up_to(cls_dev, slots)
    width = up_to(d_t + d_s + LANES, LANES * n_feat) // n_feat
    out_rows = d_t // (n_dp * n_feat)
    bits = 2 if n_dp % 4 == 0 else 1
    block = n_dp // 2 * out_rows
    vmem = pltpu.CompilerParams(vmem_limit_bytes=20 * 2**20)
    hbm = pl.BlockSpec(memory_space=pltpu.HBM)
    near = pl.BlockSpec(memory_space=pltpu.VMEM)

    def across(value, offset=0):
        moves = [
            (d * n_feat + f, (d ^ (1 << (f + offset) % n_feat % bits)) * n_feat + (f + offset) % n_feat)
            for d in range(n_dp)
            for f in range(n_feat)
        ]
        return lax.ppermute(value, ("dp", "feat"), moves)

    def shifted(value, offset):
        return lax.ppermute(
            value, "feat", [(f, (f + offset) % n_feat) for f in range(n_feat)]
        )

    sent, token = pl.pallas_call(
        functools.partial(route_kernel, cls_dev, capacity),
        out_shape=(
            jax.ShapeDtypeStruct((slots, width), jnp.bfloat16),
            jax.ShapeDtypeStruct((8, LANES), jnp.float32),
        ),
        in_specs=[hbm] * 4,
        scratch_shapes=[
            pltpu.VMEM((images,), jnp.int32),
            pltpu.VMEM((classes,), jnp.int32),
            pltpu.VMEM((images, width * n_feat), jnp.bfloat16),
            pltpu.SemaphoreType.DMA((4,)),
        ],
        compiler_params=pltpu.CompilerParams(vmem_limit_bytes=60 * 2**20),
        name="route",
    )(labels, class_slot, teacher, student)
    permuted = out_rows % 16 != 0
    weights = []
    if permuted:
        targets = (lax.axis_index("feat") + jnp.arange(n_feat)) % n_feat
        bit = (targets % bits)[:, None]
        group = jnp.tile(jnp.arange(n_dp // 2), 2)[None, :]
        side = (lax.axis_index("dp") >> bit) % 2
        side = jnp.where(jnp.arange(n_dp)[None, :] >= n_dp // 2, 1 - side, side)
        member = member_of(group, bit, side)
        lines = (member * n_feat + targets[:, None])[:, :, None] * out_rows + jnp.arange(out_rows)
        weights = [jnp.take(freqs, lines.reshape(n_feat, 2 * block), axis=0)]
    head_near, freqs_near = pl.pallas_call(
        load_kernel,
        out_shape=(
            jax.ShapeDtypeStruct(head.shape, jnp.bfloat16),
            jax.ShapeDtypeStruct(freqs.shape, jnp.bfloat16),
        ),
        in_specs=[hbm] * 3,
        scratch_shapes=[pltpu.SemaphoreType.DMA((2,))],
        compiler_params=vmem,
        name="load",
    )(head, freqs, token)
    heads = [head_near] + [shifted(head_near, k) for k in range(1, n_feat)]
    mine = lax.all_to_all(
        sent.reshape(n_dp, capacity, width), "dp", split_axis=0, concat_axis=0, tiled=True
    ).reshape(slots, width)
    role = None
    if n_feat == 2 and width == d_t:
        other = shifted(mine, 1)
        student_in, tags_in = pl.pallas_call(
            sort_kernel,
            out_shape=(
                jax.ShapeDtypeStruct((slots, d_s), jnp.bfloat16),
                jax.ShapeDtypeStruct((slots, LANES), jnp.bfloat16),
            ),
            compiler_params=vmem,
            name="sort",
        )(mine, other)
    else:
        role = 0
        everything = lax.all_gather(mine, "feat", axis=1, tiled=True)
        mine, student_in, tags_in = jnp.split(
            everything[:, : d_t + d_s + LANES], [d_t, d_t + d_s], axis=1
        )
        other = mine
    cos, sin, head_others = pl.pallas_call(
        functools.partial(first_kernel, role, n_feat, d_s),
        out_shape=(jax.ShapeDtypeStruct((slots, half), jnp.float32),) * 2
        + (jax.ShapeDtypeStruct((n_feat - 1, *head.shape), jnp.bfloat16),),
        in_specs=[near] * 2 + [hbm] * (n_feat - 1) + [near],
        scratch_shapes=[
            pltpu.VMEM((slots, d_t), jnp.bfloat16),
            pltpu.SemaphoreType.DMA((n_feat - 1,)),
        ],
        compiler_params=vmem,
        name="first",
    )(mine, *heads, freqs_near)
    cos, student_out = lax.optimization_barrier((cos, student_in))
    student_across = across(student_out)
    *grads, norms = pl.pallas_call(
        functools.partial(class_kernel, role, n_feat, n_dp, bits, cls_pad, permuted),
        out_shape=tuple(
            jax.ShapeDtypeStruct((block + CARRIED, slots), jnp.bfloat16)
            if k
            else jax.ShapeDtypeStruct((block, slots), jnp.float32)
            for k in range(n_feat)
        )
        + tuple(
            jax.ShapeDtypeStruct((block, slots), jnp.bfloat16 if k else jnp.float32)
            for k in range(n_feat)
        )
        + (jax.ShapeDtypeStruct((1, cls_pad), jnp.float32),),
        in_specs=[near] * (8 + len(weights)),
        scratch_shapes=[
            pltpu.VMEM((slots, d_t), jnp.bfloat16),
            pltpu.VMEM((slots, half), jnp.bfloat16),
            pltpu.VMEM((2 * block, half), jnp.bfloat16),
        ],
        compiler_params=vmem,
        name="classes",
    )(
        other, student_in, tags_in, cos, sin, heads[0], head_others, freqs_near, *weights
    )
    here = [grads[0]] + [shifted(grads[k], k) for k in range(1, n_feat)]
    there = [grads[n_feat]] + [shifted(grads[n_feat + k], k) for k in range(1, n_feat)]
    folded = pl.pallas_call(
        fold_kernel,
        out_shape=jax.ShapeDtypeStruct((block, slots), jnp.bfloat16),
        compiler_params=vmem,
        name="fold",
    )(*there)
    there = [across(folded)]
    here, student_across = lax.optimization_barrier((here, student_across))
    scale = 1.0 / math.sqrt(images * n_dp)
    own, loss = pl.pallas_call(
        functools.partial(own_kernel, scale, 2.0 * half * n_feat),
        out_shape=(
            jax.ShapeDtypeStruct((block, d_s), jnp.float32),
            jax.ShapeDtypeStruct((cls_dev,), jnp.float32),
        ),
        compiler_params=vmem,
        name="own",
    )(*here, norms, student_in)
    partial_head = pl.pallas_call(
        functools.partial(head_kernel, scale),
        out_shape=jax.ShapeDtypeStruct((block, d_s), jnp.bfloat16),
        compiler_params=vmem,
        name="head",
    )(*there, own, student_across)
    received = lax.all_to_all(
        partial_head.reshape(n_dp // 2, out_rows, d_s),
        ("dp", "feat"),
        split_axis=0,
        concat_axis=0,
        tiled=True,
        axis_index_groups=[
            [d * n_feat + f for d in range(n_dp) if (d >> f % bits) % 2 == side]
            for f in range(n_feat)
            for side in range(2)
        ],
    )
    head_grad = pl.pallas_call(
        total_kernel,
        out_shape=jax.ShapeDtypeStruct((out_rows, d_s), jnp.float32),
        compiler_params=vmem,
        name="total",
    )(received)
    return (head_grad, loss)


def solution(mesh):
    in_specs = (P("dp", None), P("dp", None), P(None, "feat"), P(None, "feat"), P("dp"), P())
    out_specs = (P(("dp", "feat"), None), P("dp"))
    return jax.shard_map(
        on_device, mesh=mesh, in_specs=in_specs, out_specs=out_specs, check_vma=False
    )
```

```python
import functools
import math

import jax
import jax.numpy as jnp
from jax import lax
from jax.experimental import pallas as pl
from jax.experimental.pallas import tpu as pltpu
from jax.sharding import PartitionSpec as P

LANES = 128
CARRIED = 16
PIECES = 3
TURN = 1.0 / (2.0 * math.pi)
SINE = (6.283164044217864, -41.337142357601536, 81.3407683703199, -70.9934277613874)


def up_to(value, multiple):
    return -(-value // multiple) * multiple


def quarter_sine(angle):
    square = angle * angle
    value = jnp.float32(SINE[-1])
    for factor in SINE[-2::-1]:
        value = value * square + factor
    return value * angle


def cos_sin(z):
    turns = z * TURN
    part = turns - lax.round(turns, lax.RoundingMethod.TO_NEAREST_EVEN)
    wave = jnp.minimum(jnp.maximum(part, -0.5 - part), 0.5 - part)
    return quarter_sine(0.25 - jnp.abs(part)), quarter_sine(wave)


def to_row(column, size):
    first = lax.broadcasted_iota(jnp.int32, (size, size), 0)
    second = lax.broadcasted_iota(jnp.int32, (size, size), 1)
    return jnp.sum(jnp.where(first == second, column, 0.0), axis=0, keepdims=True)


def to_column(row, size):
    first = lax.broadcasted_iota(jnp.int32, (size, size), 0)
    second = lax.broadcasted_iota(jnp.int32, (size, size), 1)
    return jnp.sum(jnp.where(first == second, row, 0.0), axis=1, keepdims=True)


def table_entries(table, chunk):
    start = chunk * LANES
    size = min(LANES, table.shape[0] - start)
    entries = table[pl.ds(start, size)].astype(jnp.float32)
    if size < LANES:
        entries = jnp.concatenate([entries, jnp.zeros((LANES - size,), jnp.float32)])
    return entries.reshape(1, LANES)


def route_kernel(
    cls_dev, capacity, labels_in, table_in, teacher, student, out, token, labels, table, rows, sems
):
    images, d_t = teacher.shape
    d_s = student.shape[1]
    slots, width = out.shape
    copies = [
        pltpu.make_async_copy(labels_in, labels, sems.at[0]),
        pltpu.make_async_copy(table_in, table, sems.at[1]),
        pltpu.make_async_copy(teacher, rows.at[:, :d_t], sems.at[2]),
        pltpu.make_async_copy(student, rows.at[:, d_t : d_t + d_s], sems.at[3]),
    ]
    for copy in copies:
        copy.start()
    lane = lax.broadcasted_iota(jnp.int32, (images, LANES), 1)
    lane_f = lane.astype(jnp.float32)
    copies[0].wait()
    label = to_column(labels[...].astype(jnp.float32).reshape(1, images), images)
    label = jnp.broadcast_to(label, (images, LANES))
    copies[1].wait()
    found = jnp.zeros((images, LANES), jnp.float32)
    for chunk in range(pl.cdiv(table.shape[0], LANES)):
        entries = table_entries(table, chunk)
        found += jnp.where(lane_f + float(chunk * LANES) == label, entries, 0.0)
    position = jnp.sum(found, axis=1, keepdims=True)
    owner = jnp.floor((position + 0.5) * (1.0 / cls_dev))
    tag = position - owner * cls_dev + 1.0
    owner_row = to_row(owner, images)
    first = lax.broadcasted_iota(jnp.int32, (images, images), 0)
    second = lax.broadcasted_iota(jnp.int32, (images, images), 1)
    before = jnp.logical_and(first < second, owner == owner_row)
    rank = jnp.sum(jnp.where(before, 1.0, 0.0), axis=0, keepdims=True)
    slot = owner_row * float(capacity) + rank
    slot_id = lax.broadcasted_iota(jnp.int32, (slots, images), 0).astype(jnp.float32)
    pick = jnp.where(slot_id == slot, 1.0, 0.0).astype(jnp.bfloat16)
    high = jnp.floor(tag * (1.0 / 32.0))
    tags = jnp.where(lane == 0, high, jnp.where(lane == 1, tag - 32.0 * high, 0.0))
    rows[:, d_t + d_s : d_t + d_s + LANES] = tags.astype(jnp.bfloat16)
    rows[:, d_t + d_s + LANES :] = jnp.zeros(
        (images, rows.shape[1] - d_t - d_s - LANES), jnp.bfloat16
    )
    token[...] = jnp.zeros_like(token)
    copies[2].wait()
    copies[3].wait()
    start = pl.multiple_of(lax.axis_index("feat") * width, LANES)
    out[...] = jnp.dot(
        pick, rows[:, pl.ds(start, width)], preferred_element_type=jnp.float32
    ).astype(jnp.bfloat16)


def load_kernel(head_in, freqs_in, _, head, freqs, sems):
    copies = [
        pltpu.make_async_copy(head_in, head, sems.at[0]),
        pltpu.make_async_copy(freqs_in, freqs, sems.at[1]),
    ]
    for copy in copies:
        copy.start()
    for copy in copies:
        copy.wait()


def carry(norm, lanes):
    row = lax.broadcasted_iota(jnp.int32, (CARRIED, lanes), 0)
    block, index = jnp.zeros((CARRIED, lanes), jnp.float32), 0
    for _ in range(PIECES):
        piece = norm.astype(jnp.bfloat16).astype(jnp.float32)
        norm = norm - piece
        for start in range(0, norm.shape[1], lanes):
            block = jnp.where(row == index, piece[:, start : start + lanes], block)
            index += 1
    return block.astype(jnp.bfloat16)


def carried_norm(block, size):
    lanes = block.shape[1]
    values = block.astype(jnp.float32)
    width = size // lanes
    found = []
    for part in range(width):
        rows = [values[p * width + part : p * width + part + 1, :] for p in range(PIECES)]
        found.append(sum(rows[1:], rows[0]))
    return jnp.concatenate(found, axis=1) if width > 1 else found[0]


def place_of(own, offset, count):
    return lax.rem(own + (count - offset), count)


def project(student, head, others, projected):
    feat = lax.axis_index("feat")
    part = head.shape[1]
    count = projected.shape[1] // part
    for offset in range(count):
        weight = others[offset - 1] if offset else head[...]
        start = pl.multiple_of(place_of(feat, offset, count) * part, LANES)
        projected[:, pl.ds(start, part)] = jnp.dot(
            student, weight, preferred_element_type=jnp.float32
        ).astype(jnp.bfloat16)


def products(inputs, freqs, step):
    return [
        jnp.dot(
            inputs[...], freqs[:, column : column + step], preferred_element_type=jnp.float32
        )
        for column in range(0, freqs.shape[1], step)
    ]


def is_role(role, index):
    return (lax.axis_index("feat") if role is None else role) == index


def first_kernel(role, n_feat, d_s, rows, *refs):
    heads, (freqs, cos, sin, near, inputs, sems) = refs[:n_feat], refs[n_feat:]
    is_student = is_role(role, 1)
    copies = [
        pltpu.make_async_copy(heads[k], near.at[k - 1], sems.at[k - 1]) for k in range(1, n_feat)
    ]
    for copy in copies:
        copy.start()
    part = freqs.shape[0] // n_feat
    own = pl.multiple_of(lax.axis_index("feat") * part, LANES)

    @pl.when(is_student)
    def _():
        inputs[:, pl.ds(own, part)] = jnp.dot(
            rows[:, :d_s], heads[0][...], preferred_element_type=jnp.float32
        ).astype(jnp.bfloat16)

    @pl.when(jnp.logical_not(is_student))
    def _():
        inputs[...] = rows[...]

    step = min(freqs.shape[1], 256)
    blocks = [slice(c, c + step) for c in range(0, freqs.shape[1], step)]
    found = [0.0] * len(blocks)
    for offset in range(n_feat):
        start = pl.multiple_of(place_of(lax.axis_index("feat"), offset, n_feat) * part, LANES)
        if offset:

            @pl.when(is_student)
            def _():
                copies[offset - 1].wait()
                inputs[:, pl.ds(start, part)] = jnp.dot(
                    rows[:, :d_s], near[offset - 1], preferred_element_type=jnp.float32
                ).astype(jnp.bfloat16)

        for index, block in enumerate(blocks):
            found[index] += jnp.dot(
                inputs[:, pl.ds(start, part)],
                freqs[pl.ds(start, part), block],
                preferred_element_type=jnp.float32,
            )
    for index, block in enumerate(blocks):
        cos[:, block], sin[:, block] = cos_sin(found[index])

    @pl.when(jnp.logical_not(is_student))
    def _():
        for copy in copies:
            copy.wait()


def sort_kernel(mine, other, student, tags):
    d_s = student.shape[1]

    def split(rows):
        student[...] = rows[:, :d_s]
        tags[...] = rows[:, d_s : d_s + LANES]

    pl.when(is_role(None, 1))(lambda: split(mine))
    pl.when(is_role(None, 0))(lambda: split(other))


def member_of(group, bit, side):
    low = group * 2 + side
    high = group // 2 * 4 + side * 2 + group % 2
    return jnp.where(bit == 0, low, high)


def grad_rows(offset, n_feat, n_dp, bits, weight, freqs, grad_z, picked):
    holder = lax.axis_index("dp")
    target = lax.rem(lax.axis_index("feat") + offset, n_feat)
    bit = lax.rem(target, bits)
    side = jnp.where(bit == 0, lax.rem(holder, 2), lax.rem(holder // 2, 2))
    out_rows = picked.shape[0] // n_dp
    if weight is not None:
        picked[...] = weight
    else:
        for index in range(n_dp):
            across, group = divmod(index, n_dp // 2)
            member = member_of(group, bit, 1 - side if across else side)
            start = pl.multiple_of((member * n_feat + target) * out_rows, out_rows)
            picked[index * out_rows : (index + 1) * out_rows, :] = freqs[
                pl.ds(start, out_rows), :
            ]
    return lax.dot_general(
        picked[...], grad_z[...], (((1,), (1,)), ((), ())), preferred_element_type=jnp.float32
    )


def class_kernel(
    role, n_feat, n_dp, bits, cls_pad, permuted, other, student, tags_in, cos, sin, *refs
):
    head, others, freqs, refs = refs[0], refs[1], refs[2], refs[3:]
    if permuted:
        weights, refs = refs[0], refs[1:]
    grads, refs = refs[: 2 * n_feat - 2], refs[2 * n_feat - 2 :]
    norms, grad_z, inputs, picked = refs
    mine_student = is_role(role, 1)
    slots, d_t = inputs.shape
    half = freqs.shape[1]

    tags = tags_in[...].astype(jnp.float32)
    lane = lax.broadcasted_iota(jnp.int32, (slots, LANES), 1)
    tag = jnp.sum(
        tags * jnp.where(lane == 0, 32.0, jnp.where(lane == 1, 1.0, 0.0)), axis=1, keepdims=True
    )
    tag_row = to_row(tag, slots)
    same = jnp.where(jnp.logical_and(tag == tag_row, tag > 0.0), 1.0, 0.0)
    inverse = 1.0 / jnp.maximum(jnp.sum(same, axis=1, keepdims=True), 1.0)
    inverse = jnp.where(mine_student, -inverse, inverse)
    same = same.astype(jnp.bfloat16)

    @pl.when(mine_student)
    def _():
        inputs[...] = other[...]

    @pl.when(jnp.logical_not(mine_student))
    def _():
        project(student[...], head, others, inputs)

    step = min(half, 256)
    norm = jnp.zeros((slots, 1), jnp.float32)
    for index, z in enumerate(products(inputs, freqs, step)):
        block = slice(index * step, (index + 1) * step)
        cos_mine, sin_mine = cos[:, block], sin[:, block]
        cos_other, sin_other = cos_sin(z)
        mean_c = inverse * jnp.dot(
            same, (cos_other - cos_mine).astype(jnp.bfloat16), preferred_element_type=jnp.float32
        )
        mean_s = inverse * jnp.dot(
            same, (sin_other - sin_mine).astype(jnp.bfloat16), preferred_element_type=jnp.float32
        )
        norm += jnp.sum(mean_c * mean_c + mean_s * mean_s, axis=1, keepdims=True)
        cos_s = jnp.where(mine_student, cos_mine, cos_other)
        sin_s = jnp.where(mine_student, sin_mine, sin_other)
        grad_z[:, block] = (cos_s * mean_s - sin_s * mean_c).astype(jnp.bfloat16)
    cls = lax.broadcasted_iota(jnp.int32, (slots, cls_pad), 1).astype(jnp.float32) + 1.0
    total_norm = jnp.sum(jnp.where(cls == tag, norm, 0.0), axis=0, keepdims=True)
    norms[...] = total_norm
    carried = carry(total_norm, slots)
    block = picked.shape[0] // 2
    for offset in range(1, n_feat):
        weight = weights[offset] if permuted else None
        product = grad_rows(offset, n_feat, n_dp, bits, weight, freqs, grad_z, picked)
        here, there = grads[offset - 1], grads[n_feat + offset - 2]
        here[:block, :] = product[:block].astype(here.dtype)
        here[block:, :] = carried
        there[...] = product[block:].astype(there.dtype)


def keep_kernel(n_feat, n_dp, bits, permuted, *refs):
    weights, (freqs, grad_z, here, there, picked) = refs[:-5], refs[-5:]
    weight = weights[0][0] if permuted else None
    product = grad_rows(0, n_feat, n_dp, bits, weight, freqs, grad_z, picked)
    block = picked.shape[0] // 2
    here[...] = product[:block]
    there[...] = product[block:]


def summed(refs, size):
    total = refs[0][:size, :].astype(jnp.float32)
    for ref in refs[1:]:
        total += ref[:size, :].astype(jnp.float32)
    return total.astype(jnp.bfloat16)


def fold_kernel(*refs):
    refs[-1][...] = summed(refs[:-1], refs[-1].shape[0])


def own_kernel(scale, divisor, *refs):
    grads, (norms, student, head, loss) = refs[:-4], refs[-4:]
    head[...] = scale * jnp.dot(
        summed(grads, head.shape[0]), student[...], preferred_element_type=jnp.float32
    )
    norm = norms[...]
    for ref in grads[1:]:
        norm += carried_norm(ref[ref.shape[0] - CARRIED :, :], norm.shape[1])
    loss[...] = (norm * (1.0 / divisor))[0, : loss.shape[0]]


def head_kernel(scale, *refs):
    grads, (own, student, head) = refs[:-3], refs[-3:]
    product = jnp.dot(
        summed(grads, head.shape[0]), student[...], preferred_element_type=jnp.float32
    )
    head[...] = (own[...] + product * scale).astype(jnp.bfloat16)


def total_kernel(parts, out):
    out[...] = jnp.sum(parts[...].astype(jnp.float32), axis=0)


def on_device(teacher, student, head, freqs, labels, class_slot):
    n_dp = lax.axis_size("dp")
    n_feat = lax.axis_size("feat")
    images, d_t = teacher.shape
    d_s = student.shape[1]
    half = freqs.shape[1]
    classes = class_slot.shape[0]
    cls_dev = classes // n_dp
    capacity = 2 * images // n_dp
    slots = n_dp * capacity
    cls_pad = up_to(cls_dev, slots)
    width = up_to(d_t + d_s + LANES, LANES * n_feat) // n_feat
    out_rows = d_t // (n_dp * n_feat)
    bits = 2 if n_dp % 4 == 0 else 1
    block = n_dp // 2 * out_rows
    vmem = pltpu.CompilerParams(vmem_limit_bytes=20 * 2**20)
    hbm = pl.BlockSpec(memory_space=pltpu.HBM)
    near = pl.BlockSpec(memory_space=pltpu.VMEM)

    def across(value, offset=0):
        moves = [
            (d * n_feat + f, (d ^ (1 << (f + offset) % n_feat % bits)) * n_feat + (f + offset) % n_feat)
            for d in range(n_dp)
            for f in range(n_feat)
        ]
        return lax.ppermute(value, ("dp", "feat"), moves)

    def shifted(value, offset):
        return lax.ppermute(
            value, "feat", [(f, (f + offset) % n_feat) for f in range(n_feat)]
        )

    sent, token = pl.pallas_call(
        functools.partial(route_kernel, cls_dev, capacity),
        out_shape=(
            jax.ShapeDtypeStruct((slots, width), jnp.bfloat16),
            jax.ShapeDtypeStruct((8, LANES), jnp.float32),
        ),
        in_specs=[hbm] * 4,
        scratch_shapes=[
            pltpu.VMEM((images,), jnp.int32),
            pltpu.VMEM((classes,), jnp.int32),
            pltpu.VMEM((images, width * n_feat), jnp.bfloat16),
            pltpu.SemaphoreType.DMA((4,)),
        ],
        compiler_params=pltpu.CompilerParams(vmem_limit_bytes=60 * 2**20),
        name="route",
    )(labels, class_slot, teacher, student)
    permuted = out_rows % 16 != 0
    weights = []
    if permuted:
        targets = (lax.axis_index("feat") + jnp.arange(n_feat)) % n_feat
        bit = (targets % bits)[:, None]
        group = jnp.tile(jnp.arange(n_dp // 2), 2)[None, :]
        side = (lax.axis_index("dp") >> bit) % 2
        side = jnp.where(jnp.arange(n_dp)[None, :] >= n_dp // 2, 1 - side, side)
        member = member_of(group, bit, side)
        lines = (member * n_feat + targets[:, None])[:, :, None] * out_rows + jnp.arange(out_rows)
        weights = [jnp.take(freqs, lines.reshape(n_feat, 2 * block), axis=0)]
    head_near, freqs_near = pl.pallas_call(
        load_kernel,
        out_shape=(
            jax.ShapeDtypeStruct(head.shape, jnp.bfloat16),
            jax.ShapeDtypeStruct(freqs.shape, jnp.bfloat16),
        ),
        in_specs=[hbm] * 3,
        scratch_shapes=[pltpu.SemaphoreType.DMA((2,))],
        compiler_params=vmem,
        name="load",
    )(head, freqs, token)
    heads = [head_near] + [shifted(head_near, k) for k in range(1, n_feat)]
    mine = lax.all_to_all(
        sent.reshape(n_dp, capacity, width), "dp", split_axis=0, concat_axis=0, tiled=True
    ).reshape(slots, width)
    role = None
    if n_feat == 2 and width == d_t:
        other = shifted(mine, 1)
        student_in, tags_in = pl.pallas_call(
            sort_kernel,
            out_shape=(
                jax.ShapeDtypeStruct((slots, d_s), jnp.bfloat16),
                jax.ShapeDtypeStruct((slots, LANES), jnp.bfloat16),
            ),
            compiler_params=vmem,
            name="sort",
        )(mine, other)
    else:
        role = 0
        everything = lax.all_gather(mine, "feat", axis=1, tiled=True)
        mine, student_in, tags_in = jnp.split(
            everything[:, : d_t + d_s + LANES], [d_t, d_t + d_s], axis=1
        )
        other = mine
    cos, sin, head_others = pl.pallas_call(
        functools.partial(first_kernel, role, n_feat, d_s),
        out_shape=(jax.ShapeDtypeStruct((slots, half), jnp.float32),) * 2
        + (jax.ShapeDtypeStruct((n_feat - 1, *head.shape), jnp.bfloat16),),
        in_specs=[near] * 2 + [hbm] * (n_feat - 1) + [near],
        scratch_shapes=[
            pltpu.VMEM((slots, d_t), jnp.bfloat16),
            pltpu.SemaphoreType.DMA((n_feat - 1,)),
        ],
        compiler_params=vmem,
        name="first",
    )(mine, *heads, freqs_near)
    cos, student_out = lax.optimization_barrier((cos, student_in))
    student_across = across(student_out)
    *grads, norms, grad_z = pl.pallas_call(
        functools.partial(class_kernel, role, n_feat, n_dp, bits, cls_pad, permuted),
        out_shape=(jax.ShapeDtypeStruct((block + CARRIED, slots), jnp.bfloat16),) * (n_feat - 1)
        + (jax.ShapeDtypeStruct((block, slots), jnp.bfloat16),) * (n_feat - 1)
        + (
            jax.ShapeDtypeStruct((1, cls_pad), jnp.float32),
            jax.ShapeDtypeStruct((slots, half), jnp.bfloat16),
        ),
        in_specs=[near] * (8 + len(weights)),
        scratch_shapes=[
            pltpu.VMEM((slots, d_t), jnp.bfloat16),
            pltpu.VMEM((2 * block, half), jnp.bfloat16),
        ],
        compiler_params=vmem,
        name="classes",
    )(
        other, student_in, tags_in, cos, sin, heads[0], head_others, freqs_near, *weights
    )
    here_own, there_own = pl.pallas_call(
        functools.partial(keep_kernel, n_feat, n_dp, bits, permuted),
        out_shape=(jax.ShapeDtypeStruct((block, slots), jnp.float32),) * 2,
        scratch_shapes=[pltpu.VMEM((2 * block, half), jnp.bfloat16)],
        compiler_params=vmem,
        name="keep",
    )(*weights, freqs_near, grad_z)
    here = [here_own] + [shifted(grads[k - 1], k) for k in range(1, n_feat)]
    there = [there_own] + [shifted(grads[n_feat + k - 2], k) for k in range(1, n_feat)]
    folded = pl.pallas_call(
        fold_kernel,
        out_shape=jax.ShapeDtypeStruct((block, slots), jnp.bfloat16),
        compiler_params=vmem,
        name="fold",
    )(*there)
    there = [across(folded)]
    here, student_across = lax.optimization_barrier((here, student_across))
    scale = 1.0 / math.sqrt(images * n_dp)
    own, loss = pl.pallas_call(
        functools.partial(own_kernel, scale, 2.0 * half * n_feat),
        out_shape=(
            jax.ShapeDtypeStruct((block, d_s), jnp.float32),
            jax.ShapeDtypeStruct((cls_dev,), jnp.float32),
        ),
        compiler_params=vmem,
        name="own",
    )(*here, norms, student_in)
    partial_head = pl.pallas_call(
        functools.partial(head_kernel, scale),
        out_shape=jax.ShapeDtypeStruct((block, d_s), jnp.bfloat16),
        compiler_params=vmem,
        name="head",
    )(*there, own, student_across)
    received = lax.all_to_all(
        partial_head.reshape(n_dp // 2, out_rows, d_s),
        ("dp", "feat"),
        split_axis=0,
        concat_axis=0,
        tiled=True,
        axis_index_groups=[
            [d * n_feat + f for d in range(n_dp) if (d >> f % bits) % 2 == side]
            for f in range(n_feat)
            for side in range(2)
        ],
    )
    head_grad = pl.pallas_call(
        total_kernel,
        out_shape=jax.ShapeDtypeStruct((out_rows, d_s), jnp.float32),
        compiler_params=vmem,
        name="total",
    )(received)
    return (head_grad, loss)


def solution(mesh):
    in_specs = (P("dp", None), P("dp", None), P(None, "feat"), P(None, "feat"), P("dp"), P())
    out_specs = (P(("dp", "feat"), None), P("dp"))
    return jax.shard_map(
        on_device, mesh=mesh, in_specs=in_specs, out_specs=out_specs, check_vma=False
    )
```

```python
import functools
import math

import jax
import jax.numpy as jnp
from jax import lax
from jax.experimental import pallas as pl
from jax.experimental.pallas import tpu as pltpu
from jax.sharding import PartitionSpec as P

LANES = 128
CARRIED = 16
PIECES = 3
TURN = 1.0 / (2.0 * math.pi)
SINE = (6.283164044217864, -41.337142357601536, 81.3407683703199, -70.9934277613874)


def up_to(value, multiple):
    return -(-value // multiple) * multiple


def quarter_sine(angle):
    square = angle * angle
    value = jnp.float32(SINE[-1])
    for factor in SINE[-2::-1]:
        value = value * square + factor
    return value * angle


def cos_sin(z):
    turns = z * TURN
    part = turns - lax.round(turns, lax.RoundingMethod.TO_NEAREST_EVEN)
    wave = jnp.minimum(jnp.maximum(part, -0.5 - part), 0.5 - part)
    return quarter_sine(0.25 - jnp.abs(part)), quarter_sine(wave)


def to_row(column, size):
    first = lax.broadcasted_iota(jnp.int32, (size, size), 0)
    second = lax.broadcasted_iota(jnp.int32, (size, size), 1)
    return jnp.sum(jnp.where(first == second, column, 0.0), axis=0, keepdims=True)


def to_column(row, size):
    first = lax.broadcasted_iota(jnp.int32, (size, size), 0)
    second = lax.broadcasted_iota(jnp.int32, (size, size), 1)
    return jnp.sum(jnp.where(first == second, row, 0.0), axis=1, keepdims=True)


def table_entries(table, chunk):
    start = chunk * LANES
    size = min(LANES, table.shape[0] - start)
    entries = table[pl.ds(start, size)].astype(jnp.float32)
    if size < LANES:
        entries = jnp.concatenate([entries, jnp.zeros((LANES - size,), jnp.float32)])
    return entries.reshape(1, LANES)


def route_kernel(
    cls_dev, capacity, labels_in, table_in, teacher, student, out, token, labels, table, rows, sems
):
    images, d_t = teacher.shape
    d_s = student.shape[1]
    slots, width = out.shape
    copies = [
        pltpu.make_async_copy(labels_in, labels, sems.at[0]),
        pltpu.make_async_copy(table_in, table, sems.at[1]),
        pltpu.make_async_copy(teacher, rows.at[:, :d_t], sems.at[2]),
        pltpu.make_async_copy(student, rows.at[:, d_t : d_t + d_s], sems.at[3]),
    ]
    for copy in copies:
        copy.start()
    lane = lax.broadcasted_iota(jnp.int32, (images, LANES), 1)
    lane_f = lane.astype(jnp.float32)
    copies[0].wait()
    label = to_column(labels[...].astype(jnp.float32).reshape(1, images), images)
    label = jnp.broadcast_to(label, (images, LANES))
    copies[1].wait()
    found = jnp.zeros((images, LANES), jnp.float32)
    for chunk in range(pl.cdiv(table.shape[0], LANES)):
        entries = table_entries(table, chunk)
        found += jnp.where(lane_f + float(chunk * LANES) == label, entries, 0.0)
    position = jnp.sum(found, axis=1, keepdims=True)
    owner = jnp.floor((position + 0.5) * (1.0 / cls_dev))
    tag = position - owner * cls_dev + 1.0
    owner_row = to_row(owner, images)
    first = lax.broadcasted_iota(jnp.int32, (images, images), 0)
    second = lax.broadcasted_iota(jnp.int32, (images, images), 1)
    before = jnp.logical_and(first < second, owner == owner_row)
    rank = jnp.sum(jnp.where(before, 1.0, 0.0), axis=0, keepdims=True)
    slot = owner_row * float(capacity) + rank
    slot_id = lax.broadcasted_iota(jnp.int32, (slots, images), 0).astype(jnp.float32)
    pick = jnp.where(slot_id == slot, 1.0, 0.0).astype(jnp.bfloat16)
    high = jnp.floor(tag * (1.0 / 32.0))
    tags = jnp.where(lane == 0, high, jnp.where(lane == 1, tag - 32.0 * high, 0.0))
    rows[:, d_t + d_s : d_t + d_s + LANES] = tags.astype(jnp.bfloat16)
    rows[:, d_t + d_s + LANES :] = jnp.zeros(
        (images, rows.shape[1] - d_t - d_s - LANES), jnp.bfloat16
    )
    token[...] = jnp.zeros_like(token)
    copies[2].wait()
    copies[3].wait()
    start = pl.multiple_of(lax.axis_index("feat") * width, LANES)
    out[...] = jnp.dot(
        pick, rows[:, pl.ds(start, width)], preferred_element_type=jnp.float32
    ).astype(jnp.bfloat16)


def load_kernel(head_in, freqs_in, _, head, freqs, sems):
    copies = [
        pltpu.make_async_copy(head_in, head, sems.at[0]),
        pltpu.make_async_copy(freqs_in, freqs, sems.at[1]),
    ]
    for copy in copies:
        copy.start()
    for copy in copies:
        copy.wait()


def carry(norm, lanes):
    row = lax.broadcasted_iota(jnp.int32, (CARRIED, lanes), 0)
    block, index = jnp.zeros((CARRIED, lanes), jnp.float32), 0
    for _ in range(PIECES):
        piece = norm.astype(jnp.bfloat16).astype(jnp.float32)
        norm = norm - piece
        for start in range(0, norm.shape[1], lanes):
            block = jnp.where(row == index, piece[:, start : start + lanes], block)
            index += 1
    return block.astype(jnp.bfloat16)


def carried_norm(block, size):
    lanes = block.shape[1]
    values = block.astype(jnp.float32)
    width = size // lanes
    found = []
    for part in range(width):
        rows = [values[p * width + part : p * width + part + 1, :] for p in range(PIECES)]
        found.append(sum(rows[1:], rows[0]))
    return jnp.concatenate(found, axis=1) if width > 1 else found[0]


def place_of(own, offset, count):
    return lax.rem(own + (count - offset), count)


def project(student, head, others, projected):
    feat = lax.axis_index("feat")
    part = head.shape[1]
    count = projected.shape[1] // part
    for offset in range(count):
        weight = others[offset - 1] if offset else head[...]
        start = pl.multiple_of(place_of(feat, offset, count) * part, LANES)
        projected[:, pl.ds(start, part)] = jnp.dot(
            student, weight, preferred_element_type=jnp.float32
        ).astype(jnp.bfloat16)


def products(inputs, freqs, step):
    return [
        jnp.dot(
            inputs[...], freqs[:, column : column + step], preferred_element_type=jnp.float32
        )
        for column in range(0, freqs.shape[1], step)
    ]


def is_role(role, index):
    return (lax.axis_index("feat") if role is None else role) == index


def first_kernel(role, n_feat, d_s, rows, *refs):
    heads, (freqs, cos, sin, near, inputs, sems) = refs[:n_feat], refs[n_feat:]
    is_student = is_role(role, 1)
    copies = [
        pltpu.make_async_copy(heads[k], near.at[k - 1], sems.at[k - 1]) for k in range(1, n_feat)
    ]
    for copy in copies:
        copy.start()
    part = freqs.shape[0] // n_feat
    own = pl.multiple_of(lax.axis_index("feat") * part, LANES)

    @pl.when(is_student)
    def _():
        inputs[:, pl.ds(own, part)] = jnp.dot(
            rows[:, :d_s], heads[0][...], preferred_element_type=jnp.float32
        ).astype(jnp.bfloat16)

    @pl.when(jnp.logical_not(is_student))
    def _():
        inputs[...] = rows[...]

    step = min(freqs.shape[1], 256)
    blocks = [slice(c, c + step) for c in range(0, freqs.shape[1], step)]
    found = [0.0] * len(blocks)
    for offset in range(n_feat):
        start = pl.multiple_of(place_of(lax.axis_index("feat"), offset, n_feat) * part, LANES)
        if offset:

            @pl.when(is_student)
            def _():
                copies[offset - 1].wait()
                inputs[:, pl.ds(start, part)] = jnp.dot(
                    rows[:, :d_s], near[offset - 1], preferred_element_type=jnp.float32
                ).astype(jnp.bfloat16)

        for index, block in enumerate(blocks):
            found[index] += jnp.dot(
                inputs[:, pl.ds(start, part)],
                freqs[pl.ds(start, part), block],
                preferred_element_type=jnp.float32,
            )
    for index, block in enumerate(blocks):
        cos[:, block], sin[:, block] = cos_sin(found[index])

    @pl.when(jnp.logical_not(is_student))
    def _():
        for copy in copies:
            copy.wait()


def sort_kernel(mine, other, student, tags):
    d_s = student.shape[1]

    def split(rows):
        student[...] = rows[:, :d_s]
        tags[...] = rows[:, d_s : d_s + LANES]

    pl.when(is_role(None, 1))(lambda: split(mine))
    pl.when(is_role(None, 0))(lambda: split(other))


def member_of(group, bit, side):
    low = group * 2 + side
    high = group // 2 * 4 + side * 2 + group % 2
    return jnp.where(bit == 0, low, high)


def grad_rows(offset, n_feat, n_dp, bits, weight, freqs, grad_z, picked):
    holder = lax.axis_index("dp")
    target = lax.rem(lax.axis_index("feat") + offset, n_feat)
    bit = lax.rem(target, bits)
    side = jnp.where(bit == 0, lax.rem(holder, 2), lax.rem(holder // 2, 2))
    out_rows = picked.shape[0] // n_dp
    if weight is not None:
        picked[...] = weight
    else:
        for index in range(n_dp):
            across, group = divmod(index, n_dp // 2)
            member = member_of(group, bit, 1 - side if across else side)
            start = pl.multiple_of((member * n_feat + target) * out_rows, out_rows)
            picked[index * out_rows : (index + 1) * out_rows, :] = freqs[
                pl.ds(start, out_rows), :
            ]
    return lax.dot_general(
        picked[...], grad_z[...], (((1,), (1,)), ((), ())), preferred_element_type=jnp.float32
    )


def class_kernel(
    role, n_feat, n_dp, bits, cls_pad, permuted, other, student, tags_in, cos, sin, *refs
):
    head, others, freqs, refs = refs[0], refs[1], refs[2], refs[3:]
    if permuted:
        weights, refs = refs[0], refs[1:]
    grads, refs = refs[: 2 * n_feat - 2], refs[2 * n_feat - 2 :]
    norms, grad_z, inputs, picked = refs
    mine_student = is_role(role, 1)
    slots, d_t = inputs.shape
    half = freqs.shape[1]

    @pl.when(mine_student)
    def _():
        inputs[...] = other[...]

    @pl.when(jnp.logical_not(mine_student))
    def _():
        project(student[...], head, others, inputs)

    tags = tags_in[...].astype(jnp.float32)
    lane = lax.broadcasted_iota(jnp.int32, (slots, LANES), 1)
    tag = jnp.sum(
        tags * jnp.where(lane == 0, 32.0, jnp.where(lane == 1, 1.0, 0.0)), axis=1, keepdims=True
    )
    tag_row = to_row(tag, slots)
    same = jnp.where(jnp.logical_and(tag == tag_row, tag > 0.0), 1.0, 0.0)
    inverse = 1.0 / jnp.maximum(jnp.sum(same, axis=1, keepdims=True), 1.0)
    inverse = jnp.where(mine_student, -inverse, inverse)
    same = same.astype(jnp.bfloat16)
    step = min(half, 256)
    norm = jnp.zeros((slots, 1), jnp.float32)
    for index, z in enumerate(products(inputs, freqs, step)):
        block = slice(index * step, (index + 1) * step)
        cos_mine, sin_mine = cos[:, block], sin[:, block]
        cos_other, sin_other = cos_sin(z)
        mean_c = inverse * jnp.dot(
            same, (cos_other - cos_mine).astype(jnp.bfloat16), preferred_element_type=jnp.float32
        )
        mean_s = inverse * jnp.dot(
            same, (sin_other - sin_mine).astype(jnp.bfloat16), preferred_element_type=jnp.float32
        )
        norm += jnp.sum(mean_c * mean_c + mean_s * mean_s, axis=1, keepdims=True)
        cos_s = jnp.where(mine_student, cos_mine, cos_other)
        sin_s = jnp.where(mine_student, sin_mine, sin_other)
        grad_z[:, block] = (cos_s * mean_s - sin_s * mean_c).astype(jnp.bfloat16)
    cls = lax.broadcasted_iota(jnp.int32, (slots, cls_pad), 1).astype(jnp.float32) + 1.0
    total_norm = jnp.sum(jnp.where(cls == tag, norm, 0.0), axis=0, keepdims=True)
    norms[...] = total_norm
    carried = carry(total_norm, slots)
    block = picked.shape[0] // 2
    for offset in range(1, n_feat):
        weight = weights[offset] if permuted else None
        product = grad_rows(offset, n_feat, n_dp, bits, weight, freqs, grad_z, picked)
        here, there = grads[offset - 1], grads[n_feat + offset - 2]
        here[:block, :] = product[:block].astype(here.dtype)
        here[block:, :] = carried
        there[...] = product[block:].astype(there.dtype)


def keep_kernel(n_feat, n_dp, bits, permuted, *refs):
    weights, (freqs, grad_z, here, there, picked) = refs[:-5], refs[-5:]
    weight = weights[0][0] if permuted else None
    product = grad_rows(0, n_feat, n_dp, bits, weight, freqs, grad_z, picked)
    block = picked.shape[0] // 2
    here[...] = product[:block]
    there[...] = product[block:]


def summed(refs, size):
    total = refs[0][:size, :].astype(jnp.float32)
    for ref in refs[1:]:
        total += ref[:size, :].astype(jnp.float32)
    return total.astype(jnp.bfloat16)


def fold_kernel(*refs):
    refs[-1][...] = summed(refs[:-1], refs[-1].shape[0])


def own_kernel(scale, divisor, *refs):
    grads, (norms, student, head, loss) = refs[:-4], refs[-4:]
    head[...] = scale * jnp.dot(
        summed(grads, head.shape[0]), student[...], preferred_element_type=jnp.float32
    )
    norm = norms[...]
    for ref in grads[1:]:
        norm += carried_norm(ref[ref.shape[0] - CARRIED :, :], norm.shape[1])
    loss[...] = (norm * (1.0 / divisor))[0, : loss.shape[0]]


def head_kernel(scale, *refs):
    grads, (own, student, head) = refs[:-3], refs[-3:]
    product = jnp.dot(
        summed(grads, head.shape[0]), student[...], preferred_element_type=jnp.float32
    )
    head[...] = (own[...] + product * scale).astype(jnp.bfloat16)


def total_kernel(parts, out):
    out[...] = jnp.sum(parts[...].astype(jnp.float32), axis=0)


def on_device(teacher, student, head, freqs, labels, class_slot):
    n_dp = lax.axis_size("dp")
    n_feat = lax.axis_size("feat")
    images, d_t = teacher.shape
    d_s = student.shape[1]
    half = freqs.shape[1]
    classes = class_slot.shape[0]
    cls_dev = classes // n_dp
    capacity = 2 * images // n_dp
    slots = n_dp * capacity
    cls_pad = up_to(cls_dev, slots)
    width = up_to(d_t + d_s + LANES, LANES * n_feat) // n_feat
    out_rows = d_t // (n_dp * n_feat)
    bits = 2 if n_dp % 4 == 0 else 1
    block = n_dp // 2 * out_rows
    vmem = pltpu.CompilerParams(vmem_limit_bytes=20 * 2**20)
    hbm = pl.BlockSpec(memory_space=pltpu.HBM)
    near = pl.BlockSpec(memory_space=pltpu.VMEM)

    def across(value, offset=0):
        moves = [
            (d * n_feat + f, (d ^ (1 << (f + offset) % n_feat % bits)) * n_feat + (f + offset) % n_feat)
            for d in range(n_dp)
            for f in range(n_feat)
        ]
        return lax.ppermute(value, ("dp", "feat"), moves)

    def shifted(value, offset):
        return lax.ppermute(
            value, "feat", [(f, (f + offset) % n_feat) for f in range(n_feat)]
        )

    sent, token = pl.pallas_call(
        functools.partial(route_kernel, cls_dev, capacity),
        out_shape=(
            jax.ShapeDtypeStruct((slots, width), jnp.bfloat16),
            jax.ShapeDtypeStruct((8, LANES), jnp.float32),
        ),
        in_specs=[hbm] * 4,
        scratch_shapes=[
            pltpu.VMEM((images,), jnp.int32),
            pltpu.VMEM((classes,), jnp.int32),
            pltpu.VMEM((images, width * n_feat), jnp.bfloat16),
            pltpu.SemaphoreType.DMA((4,)),
        ],
        compiler_params=pltpu.CompilerParams(vmem_limit_bytes=60 * 2**20),
        name="route",
    )(labels, class_slot, teacher, student)
    permuted = out_rows % 16 != 0
    weights = []
    if permuted:
        targets = (lax.axis_index("feat") + jnp.arange(n_feat)) % n_feat
        bit = (targets % bits)[:, None]
        group = jnp.tile(jnp.arange(n_dp // 2), 2)[None, :]
        side = (lax.axis_index("dp") >> bit) % 2
        side = jnp.where(jnp.arange(n_dp)[None, :] >= n_dp // 2, 1 - side, side)
        member = member_of(group, bit, side)
        lines = (member * n_feat + targets[:, None])[:, :, None] * out_rows + jnp.arange(out_rows)
        weights = [jnp.take(freqs, lines.reshape(n_feat, 2 * block), axis=0)]
    head_near, freqs_near = pl.pallas_call(
        load_kernel,
        out_shape=(
            jax.ShapeDtypeStruct(head.shape, jnp.bfloat16),
            jax.ShapeDtypeStruct(freqs.shape, jnp.bfloat16),
        ),
        in_specs=[hbm] * 3,
        scratch_shapes=[pltpu.SemaphoreType.DMA((2,))],
        compiler_params=vmem,
        name="load",
    )(head, freqs, token)
    heads = [head_near] + [shifted(head_near, k) for k in range(1, n_feat)]
    mine = lax.all_to_all(
        sent.reshape(n_dp, capacity, width), "dp", split_axis=0, concat_axis=0, tiled=True
    ).reshape(slots, width)
    role = None
    if n_feat == 2 and width == d_t:
        other = shifted(mine, 1)
        student_in, tags_in = pl.pallas_call(
            sort_kernel,
            out_shape=(
                jax.ShapeDtypeStruct((slots, d_s), jnp.bfloat16),
                jax.ShapeDtypeStruct((slots, LANES), jnp.bfloat16),
            ),
            compiler_params=vmem,
            name="sort",
        )(mine, other)
    else:
        role = 0
        everything = lax.all_gather(mine, "feat", axis=1, tiled=True)
        mine, student_in, tags_in = jnp.split(
            everything[:, : d_t + d_s + LANES], [d_t, d_t + d_s], axis=1
        )
        other = mine
    cos, sin, head_others = pl.pallas_call(
        functools.partial(first_kernel, role, n_feat, d_s),
        out_shape=(jax.ShapeDtypeStruct((slots, half), jnp.float32),) * 2
        + (jax.ShapeDtypeStruct((n_feat - 1, *head.shape), jnp.bfloat16),),
        in_specs=[near] * 2 + [hbm] * (n_feat - 1) + [near],
        scratch_shapes=[
            pltpu.VMEM((slots, d_t), jnp.bfloat16),
            pltpu.SemaphoreType.DMA((n_feat - 1,)),
        ],
        compiler_params=vmem,
        name="first",
    )(mine, *heads, freqs_near)
    cos, student_out = lax.optimization_barrier((cos, student_in))
    student_across = across(student_out)
    *grads, norms, grad_z = pl.pallas_call(
        functools.partial(class_kernel, role, n_feat, n_dp, bits, cls_pad, permuted),
        out_shape=(jax.ShapeDtypeStruct((block + CARRIED, slots), jnp.bfloat16),) * (n_feat - 1)
        + (jax.ShapeDtypeStruct((block, slots), jnp.bfloat16),) * (n_feat - 1)
        + (
            jax.ShapeDtypeStruct((1, cls_pad), jnp.float32),
            jax.ShapeDtypeStruct((slots, half), jnp.bfloat16),
        ),
        in_specs=[near] * (8 + len(weights)),
        scratch_shapes=[
            pltpu.VMEM((slots, d_t), jnp.bfloat16),
            pltpu.VMEM((2 * block, half), jnp.bfloat16),
        ],
        compiler_params=vmem,
        name="classes",
    )(
        other, student_in, tags_in, cos, sin, heads[0], head_others, freqs_near, *weights
    )
    here_own, there_own = pl.pallas_call(
        functools.partial(keep_kernel, n_feat, n_dp, bits, permuted),
        out_shape=(jax.ShapeDtypeStruct((block, slots), jnp.float32),) * 2,
        scratch_shapes=[pltpu.VMEM((2 * block, half), jnp.bfloat16)],
        compiler_params=vmem,
        name="keep",
    )(*weights, freqs_near, grad_z)
    here = [here_own] + [shifted(grads[k - 1], k) for k in range(1, n_feat)]
    there = [there_own] + [shifted(grads[n_feat + k - 2], k) for k in range(1, n_feat)]
    folded = pl.pallas_call(
        fold_kernel,
        out_shape=jax.ShapeDtypeStruct((block, slots), jnp.bfloat16),
        compiler_params=vmem,
        name="fold",
    )(*there)
    there = [across(folded)]
    here, student_across = lax.optimization_barrier((here, student_across))
    scale = 1.0 / math.sqrt(images * n_dp)
    own, loss = pl.pallas_call(
        functools.partial(own_kernel, scale, 2.0 * half * n_feat),
        out_shape=(
            jax.ShapeDtypeStruct((block, d_s), jnp.float32),
            jax.ShapeDtypeStruct((cls_dev,), jnp.float32),
        ),
        compiler_params=vmem,
        name="own",
    )(*here, norms, student_in)
    partial_head = pl.pallas_call(
        functools.partial(head_kernel, scale),
        out_shape=jax.ShapeDtypeStruct((block, d_s), jnp.bfloat16),
        compiler_params=vmem,
        name="head",
    )(*there, own, student_across)
    received = lax.all_to_all(
        partial_head.reshape(n_dp // 2, out_rows, d_s),
        ("dp", "feat"),
        split_axis=0,
        concat_axis=0,
        tiled=True,
        axis_index_groups=[
            [d * n_feat + f for d in range(n_dp) if (d >> f % bits) % 2 == side]
            for f in range(n_feat)
            for side in range(2)
        ],
    )
    head_grad = pl.pallas_call(
        total_kernel,
        out_shape=jax.ShapeDtypeStruct((out_rows, d_s), jnp.float32),
        compiler_params=vmem,
        name="total",
    )(received)
    return (head_grad, loss)


def solution(mesh):
    in_specs = (P("dp", None), P("dp", None), P(None, "feat"), P(None, "feat"), P("dp"), P())
    out_specs = (P(("dp", "feat"), None), P("dp"))
    return jax.shard_map(
        on_device, mesh=mesh, in_specs=in_specs, out_specs=out_specs, check_vma=False
    )
```

```python
import functools
import math

import jax
import jax.numpy as jnp
from jax import lax
from jax.experimental import pallas as pl
from jax.experimental.pallas import tpu as pltpu
from jax.sharding import PartitionSpec as P

LANES = 128
CARRIED = 16
PIECES = 3
TURN = 1.0 / (2.0 * math.pi)
SINE = (6.283164044217864, -41.337142357601536, 81.3407683703199, -70.9934277613874)


def up_to(value, multiple):
    return -(-value // multiple) * multiple


def quarter_sine(angle):
    square = angle * angle
    value = jnp.float32(SINE[-1])
    for factor in SINE[-2::-1]:
        value = value * square + factor
    return value * angle


def cos_sin(z):
    turns = z * TURN
    part = turns - lax.round(turns, lax.RoundingMethod.TO_NEAREST_EVEN)
    wave = jnp.minimum(jnp.maximum(part, -0.5 - part), 0.5 - part)
    return quarter_sine(0.25 - jnp.abs(part)), quarter_sine(wave)


def to_row(column, size):
    first = lax.broadcasted_iota(jnp.int32, (size, size), 0)
    second = lax.broadcasted_iota(jnp.int32, (size, size), 1)
    return jnp.sum(jnp.where(first == second, column, 0.0), axis=0, keepdims=True)


def to_column(row, size):
    first = lax.broadcasted_iota(jnp.int32, (size, size), 0)
    second = lax.broadcasted_iota(jnp.int32, (size, size), 1)
    return jnp.sum(jnp.where(first == second, row, 0.0), axis=1, keepdims=True)


def table_entries(table, chunk):
    start = chunk * LANES
    size = min(LANES, table.shape[0] - start)
    entries = table[pl.ds(start, size)].astype(jnp.float32)
    if size < LANES:
        entries = jnp.concatenate([entries, jnp.zeros((LANES - size,), jnp.float32)])
    return entries.reshape(1, LANES)


def route_kernel(
    cls_dev, capacity, labels_in, table_in, teacher, student, out, token, labels, table, rows, sems
):
    images, d_t = teacher.shape
    d_s = student.shape[1]
    slots, width = out.shape
    copies = [
        pltpu.make_async_copy(labels_in, labels, sems.at[0]),
        pltpu.make_async_copy(table_in, table, sems.at[1]),
        pltpu.make_async_copy(teacher, rows.at[:, :d_t], sems.at[2]),
        pltpu.make_async_copy(student, rows.at[:, d_t : d_t + d_s], sems.at[3]),
    ]
    for copy in copies:
        copy.start()
    lane = lax.broadcasted_iota(jnp.int32, (images, LANES), 1)
    lane_f = lane.astype(jnp.float32)
    copies[0].wait()
    label = to_column(labels[...].astype(jnp.float32).reshape(1, images), images)
    label = jnp.broadcast_to(label, (images, LANES))
    copies[1].wait()
    found = jnp.zeros((images, LANES), jnp.float32)
    for chunk in range(pl.cdiv(table.shape[0], LANES)):
        entries = table_entries(table, chunk)
        found += jnp.where(lane_f + float(chunk * LANES) == label, entries, 0.0)
    position = jnp.sum(found, axis=1, keepdims=True)
    owner = jnp.floor((position + 0.5) * (1.0 / cls_dev))
    tag = position - owner * cls_dev + 1.0
    owner_row = to_row(owner, images)
    first = lax.broadcasted_iota(jnp.int32, (images, images), 0)
    second = lax.broadcasted_iota(jnp.int32, (images, images), 1)
    before = jnp.logical_and(first < second, owner == owner_row)
    rank = jnp.sum(jnp.where(before, 1.0, 0.0), axis=0, keepdims=True)
    slot = owner_row * float(capacity) + rank
    slot_id = lax.broadcasted_iota(jnp.int32, (slots, images), 0).astype(jnp.float32)
    pick = jnp.where(slot_id == slot, 1.0, 0.0).astype(jnp.bfloat16)
    high = jnp.floor(tag * (1.0 / 32.0))
    tags = jnp.where(lane == 0, high, jnp.where(lane == 1, tag - 32.0 * high, 0.0))
    rows[:, d_t + d_s : d_t + d_s + LANES] = tags.astype(jnp.bfloat16)
    rows[:, d_t + d_s + LANES :] = jnp.zeros(
        (images, rows.shape[1] - d_t - d_s - LANES), jnp.bfloat16
    )
    token[...] = jnp.zeros_like(token)
    copies[2].wait()
    copies[3].wait()
    start = pl.multiple_of(lax.axis_index("feat") * width, LANES)
    out[...] = jnp.dot(
        pick, rows[:, pl.ds(start, width)], preferred_element_type=jnp.float32
    ).astype(jnp.bfloat16)


def load_kernel(head_in, freqs_in, _, head, freqs, sems):
    copies = [
        pltpu.make_async_copy(head_in, head, sems.at[0]),
        pltpu.make_async_copy(freqs_in, freqs, sems.at[1]),
    ]
    for copy in copies:
        copy.start()
    for copy in copies:
        copy.wait()


def carry(norm, lanes):
    row = lax.broadcasted_iota(jnp.int32, (CARRIED, lanes), 0)
    block, index = jnp.zeros((CARRIED, lanes), jnp.float32), 0
    for _ in range(PIECES):
        piece = norm.astype(jnp.bfloat16).astype(jnp.float32)
        norm = norm - piece
        for start in range(0, norm.shape[1], lanes):
            block = jnp.where(row == index, piece[:, start : start + lanes], block)
            index += 1
    return block.astype(jnp.bfloat16)


def carried_norm(block, size):
    lanes = block.shape[1]
    values = block.astype(jnp.float32)
    width = size // lanes
    found = []
    for part in range(width):
        rows = [values[p * width + part : p * width + part + 1, :] for p in range(PIECES)]
        found.append(sum(rows[1:], rows[0]))
    return jnp.concatenate(found, axis=1) if width > 1 else found[0]


def lane_start(own, offset, count, part):
    if isinstance(own, int):
        return (own - offset) % count * part
    return pl.multiple_of(lax.rem(own + (count - offset), count) * part, LANES)


def holder_of(role, index):
    return index if role is None else lax.axis_index("feat")


def project(feat, student, head, others, projected):
    part = head.shape[1]
    count = projected.shape[1] // part
    for offset in range(count):
        weight = others[offset - 1] if offset else head[...]
        start = lane_start(feat, offset, count, part)
        projected[:, pl.ds(start, part)] = jnp.dot(
            student, weight, preferred_element_type=jnp.float32
        ).astype(jnp.bfloat16)


def products(inputs, freqs, step):
    return [
        jnp.dot(
            inputs[...], freqs[:, column : column + step], preferred_element_type=jnp.float32
        )
        for column in range(0, freqs.shape[1], step)
    ]


def is_role(role, index):
    return (lax.axis_index("feat") if role is None else role) == index


def first_kernel(role, n_feat, d_s, rows, *refs):
    heads, (freqs, cos, sin, near, inputs, sems) = refs[:n_feat], refs[n_feat:]
    is_student = is_role(role, 1)
    rows_each = d_s // PIECES
    copies = [
        [
            pltpu.make_async_copy(
                heads[k].at[pl.ds(piece * rows_each, rows_each)],
                near.at[k - 1, pl.ds(piece * rows_each, rows_each)],
                sems.at[k - 1, piece],
            )
            for piece in range(PIECES)
        ]
        for k in range(1, n_feat)
    ]
    for group in copies:
        for copy in group:
            copy.start()
    part = freqs.shape[0] // n_feat
    feat = holder_of(role, 1)
    own = lane_start(feat, 0, n_feat, part)

    @pl.when(is_student)
    def _():
        inputs[:, pl.ds(own, part)] = jnp.dot(
            rows[:, :d_s], heads[0][...], preferred_element_type=jnp.float32
        ).astype(jnp.bfloat16)

    @pl.when(jnp.logical_not(is_student))
    def _():
        inputs[...] = rows[...]

    step = min(freqs.shape[1], 256)
    blocks = [slice(c, c + step) for c in range(0, freqs.shape[1], step)]
    found = [0.0] * len(blocks)
    for offset in range(n_feat):
        start = lane_start(feat, offset, n_feat, part)
        if offset:

            @pl.when(is_student)
            def _():
                for copy in copies[offset - 1]:
                    copy.wait()
                inputs[:, pl.ds(start, part)] = jnp.dot(
                    rows[:, :d_s], near[offset - 1], preferred_element_type=jnp.float32
                ).astype(jnp.bfloat16)

        for index, block in enumerate(blocks):
            found[index] += jnp.dot(
                inputs[:, pl.ds(start, part)],
                freqs[pl.ds(start, part), block],
                preferred_element_type=jnp.float32,
            )
    for index, block in enumerate(blocks):
        cos[:, block], sin[:, block] = cos_sin(found[index])

    @pl.when(jnp.logical_not(is_student))
    def _():
        for group in copies:
            for copy in group:
                copy.wait()


def sort_kernel(mine, other, student, tags):
    d_s = student.shape[1]

    def split(rows):
        student[...] = rows[:, :d_s]
        tags[...] = rows[:, d_s : d_s + LANES]

    pl.when(is_role(None, 1))(lambda: split(mine))
    pl.when(is_role(None, 0))(lambda: split(other))


def member_of(group, bit, side):
    low = group * 2 + side
    high = group // 2 * 4 + side * 2 + group % 2
    return jnp.where(bit == 0, low, high)


def grad_rows(offset, n_feat, n_dp, bits, weight, freqs, grad_z, picked):
    holder = lax.axis_index("dp")
    target = lax.rem(lax.axis_index("feat") + offset, n_feat)
    bit = lax.rem(target, bits)
    side = jnp.where(bit == 0, lax.rem(holder, 2), lax.rem(holder // 2, 2))
    out_rows = picked.shape[0] // n_dp
    if weight is not None:
        picked[...] = weight
    else:
        for index in range(n_dp):
            across, group = divmod(index, n_dp // 2)
            member = member_of(group, bit, 1 - side if across else side)
            start = pl.multiple_of((member * n_feat + target) * out_rows, out_rows)
            picked[index * out_rows : (index + 1) * out_rows, :] = freqs[
                pl.ds(start, out_rows), :
            ]
    return lax.dot_general(
        picked[...], grad_z[...], (((1,), (1,)), ((), ())), preferred_element_type=jnp.float32
    )


def class_kernel(
    role, n_feat, n_dp, bits, cls_pad, permuted, other, student, tags_in, cos, sin, *refs
):
    head, others, freqs, refs = refs[0], refs[1], refs[2], refs[3:]
    if permuted:
        weights, refs = refs[0], refs[1:]
    grads, refs = refs[: 2 * n_feat - 2], refs[2 * n_feat - 2 :]
    norms, grad_z, inputs, picked = refs
    mine_student = is_role(role, 1)
    slots, d_t = inputs.shape
    half = freqs.shape[1]

    @pl.when(mine_student)
    def _():
        inputs[...] = other[...]

    @pl.when(jnp.logical_not(mine_student))
    def _():
        project(holder_of(role, 0), student[...], head, others, inputs)

    tags = tags_in[...].astype(jnp.float32)
    lane = lax.broadcasted_iota(jnp.int32, (slots, LANES), 1)
    tag = jnp.sum(
        tags * jnp.where(lane == 0, 32.0, jnp.where(lane == 1, 1.0, 0.0)), axis=1, keepdims=True
    )
    tag_row = to_row(tag, slots)
    same = jnp.where(jnp.logical_and(tag == tag_row, tag > 0.0), 1.0, 0.0)
    inverse = 1.0 / jnp.maximum(jnp.sum(same, axis=1, keepdims=True), 1.0)
    inverse = jnp.where(mine_student, -inverse, inverse)
    same = same.astype(jnp.bfloat16)
    step = min(half, 256)
    norm = jnp.zeros((slots, 1), jnp.float32)
    for index, z in enumerate(products(inputs, freqs, step)):
        block = slice(index * step, (index + 1) * step)
        cos_mine, sin_mine = cos[:, block], sin[:, block]
        cos_other, sin_other = cos_sin(z)
        mean_c = inverse * jnp.dot(
            same, (cos_other - cos_mine).astype(jnp.bfloat16), preferred_element_type=jnp.float32
        )
        mean_s = inverse * jnp.dot(
            same, (sin_other - sin_mine).astype(jnp.bfloat16), preferred_element_type=jnp.float32
        )
        norm += jnp.sum(mean_c * mean_c + mean_s * mean_s, axis=1, keepdims=True)
        cos_s = jnp.where(mine_student, cos_mine, cos_other)
        sin_s = jnp.where(mine_student, sin_mine, sin_other)
        grad_z[:, block] = (cos_s * mean_s - sin_s * mean_c).astype(jnp.bfloat16)
    cls = lax.broadcasted_iota(jnp.int32, (slots, cls_pad), 1).astype(jnp.float32) + 1.0
    total_norm = jnp.sum(jnp.where(cls == tag, norm, 0.0), axis=0, keepdims=True)
    norms[...] = total_norm
    carried = carry(total_norm, slots)
    block = picked.shape[0] // 2
    for offset in range(1, n_feat):
        weight = weights[offset] if permuted else None
        product = grad_rows(offset, n_feat, n_dp, bits, weight, freqs, grad_z, picked)
        here, there = grads[offset - 1], grads[n_feat + offset - 2]
        here[:block, :] = product[:block].astype(here.dtype)
        here[block:, :] = carried
        there[...] = product[block:].astype(there.dtype)


def keep_kernel(n_feat, n_dp, bits, permuted, *refs):
    weights, (freqs, grad_z, here, there, picked) = refs[:-5], refs[-5:]
    weight = weights[0][0] if permuted else None
    product = grad_rows(0, n_feat, n_dp, bits, weight, freqs, grad_z, picked)
    block = picked.shape[0] // 2
    here[...] = product[:block]
    there[...] = product[block:]


def summed(refs, size):
    total = refs[0][:size, :].astype(jnp.float32)
    for ref in refs[1:]:
        total += ref[:size, :].astype(jnp.float32)
    return total.astype(jnp.bfloat16)


def fold_kernel(*refs):
    refs[-1][...] = summed(refs[:-1], refs[-1].shape[0])


def own_kernel(scale, divisor, *refs):
    grads, (norms, student, head, loss) = refs[:-4], refs[-4:]
    head[...] = scale * jnp.dot(
        summed(grads, head.shape[0]), student[...], preferred_element_type=jnp.float32
    )
    norm = norms[...]
    for ref in grads[1:]:
        norm += carried_norm(ref[ref.shape[0] - CARRIED :, :], norm.shape[1])
    loss[...] = (norm * (1.0 / divisor))[0, : loss.shape[0]]


def head_kernel(scale, *refs):
    grads, (own, student, head) = refs[:-3], refs[-3:]
    product = jnp.dot(
        summed(grads, head.shape[0]), student[...], preferred_element_type=jnp.float32
    )
    head[...] = (own[...] + product * scale).astype(jnp.bfloat16)


def total_kernel(parts, out):
    out[...] = jnp.sum(parts[...].astype(jnp.float32), axis=0)


def on_device(teacher, student, head, freqs, labels, class_slot):
    n_dp = lax.axis_size("dp")
    n_feat = lax.axis_size("feat")
    images, d_t = teacher.shape
    d_s = student.shape[1]
    half = freqs.shape[1]
    classes = class_slot.shape[0]
    cls_dev = classes // n_dp
    capacity = 2 * images // n_dp
    slots = n_dp * capacity
    cls_pad = up_to(cls_dev, slots)
    width = up_to(d_t + d_s + LANES, LANES * n_feat) // n_feat
    out_rows = d_t // (n_dp * n_feat)
    bits = 2 if n_dp % 4 == 0 else 1
    block = n_dp // 2 * out_rows
    vmem = pltpu.CompilerParams(vmem_limit_bytes=20 * 2**20)
    hbm = pl.BlockSpec(memory_space=pltpu.HBM)
    near = pl.BlockSpec(memory_space=pltpu.VMEM)

    def across(value, offset=0):
        moves = [
            (d * n_feat + f, (d ^ (1 << (f + offset) % n_feat % bits)) * n_feat + (f + offset) % n_feat)
            for d in range(n_dp)
            for f in range(n_feat)
        ]
        return lax.ppermute(value, ("dp", "feat"), moves)

    def shifted(value, offset):
        return lax.ppermute(
            value, "feat", [(f, (f + offset) % n_feat) for f in range(n_feat)]
        )

    sent, token = pl.pallas_call(
        functools.partial(route_kernel, cls_dev, capacity),
        out_shape=(
            jax.ShapeDtypeStruct((slots, width), jnp.bfloat16),
            jax.ShapeDtypeStruct((8, LANES), jnp.float32),
        ),
        in_specs=[hbm] * 4,
        scratch_shapes=[
            pltpu.VMEM((images,), jnp.int32),
            pltpu.VMEM((classes,), jnp.int32),
            pltpu.VMEM((images, width * n_feat), jnp.bfloat16),
            pltpu.SemaphoreType.DMA((4,)),
        ],
        compiler_params=pltpu.CompilerParams(vmem_limit_bytes=60 * 2**20),
        name="route",
    )(labels, class_slot, teacher, student)
    permuted = out_rows % 16 != 0
    weights = []
    if permuted:
        targets = (lax.axis_index("feat") + jnp.arange(n_feat)) % n_feat
        bit = (targets % bits)[:, None]
        group = jnp.tile(jnp.arange(n_dp // 2), 2)[None, :]
        side = (lax.axis_index("dp") >> bit) % 2
        side = jnp.where(jnp.arange(n_dp)[None, :] >= n_dp // 2, 1 - side, side)
        member = member_of(group, bit, side)
        lines = (member * n_feat + targets[:, None])[:, :, None] * out_rows + jnp.arange(out_rows)
        weights = [jnp.take(freqs, lines.reshape(n_feat, 2 * block), axis=0)]
    head_near, freqs_near = pl.pallas_call(
        load_kernel,
        out_shape=(
            jax.ShapeDtypeStruct(head.shape, jnp.bfloat16),
            jax.ShapeDtypeStruct(freqs.shape, jnp.bfloat16),
        ),
        in_specs=[hbm] * 3,
        scratch_shapes=[pltpu.SemaphoreType.DMA((2,))],
        compiler_params=vmem,
        name="load",
    )(head, freqs, token)
    heads = [head_near] + [shifted(head_near, k) for k in range(1, n_feat)]
    mine = lax.all_to_all(
        sent.reshape(n_dp, capacity, width), "dp", split_axis=0, concat_axis=0, tiled=True
    ).reshape(slots, width)
    role = None
    if n_feat == 2 and width == d_t:
        other = shifted(mine, 1)
        student_in, tags_in = pl.pallas_call(
            sort_kernel,
            out_shape=(
                jax.ShapeDtypeStruct((slots, d_s), jnp.bfloat16),
                jax.ShapeDtypeStruct((slots, LANES), jnp.bfloat16),
            ),
            compiler_params=vmem,
            name="sort",
        )(mine, other)
    else:
        role = 0
        everything = lax.all_gather(mine, "feat", axis=1, tiled=True)
        mine, student_in, tags_in = jnp.split(
            everything[:, : d_t + d_s + LANES], [d_t, d_t + d_s], axis=1
        )
        other = mine
    cos, sin, head_others = pl.pallas_call(
        functools.partial(first_kernel, role, n_feat, d_s),
        out_shape=(jax.ShapeDtypeStruct((slots, half), jnp.float32),) * 2
        + (jax.ShapeDtypeStruct((n_feat - 1, *head.shape), jnp.bfloat16),),
        in_specs=[near] * 2 + [hbm] * (n_feat - 1) + [near],
        scratch_shapes=[
            pltpu.VMEM((slots, d_t), jnp.bfloat16),
            pltpu.SemaphoreType.DMA((n_feat - 1, PIECES)),
        ],
        compiler_params=vmem,
        name="first",
    )(mine, *heads, freqs_near)
    cos, student_out = lax.optimization_barrier((cos, student_in))
    student_across = across(student_out)
    *grads, norms, grad_z = pl.pallas_call(
        functools.partial(class_kernel, role, n_feat, n_dp, bits, cls_pad, permuted),
        out_shape=(jax.ShapeDtypeStruct((block + CARRIED, slots), jnp.bfloat16),) * (n_feat - 1)
        + (jax.ShapeDtypeStruct((block, slots), jnp.bfloat16),) * (n_feat - 1)
        + (
            jax.ShapeDtypeStruct((1, cls_pad), jnp.float32),
            jax.ShapeDtypeStruct((slots, half), jnp.bfloat16),
        ),
        in_specs=[near] * (8 + len(weights)),
        scratch_shapes=[
            pltpu.VMEM((slots, d_t), jnp.bfloat16),
            pltpu.VMEM((2 * block, half), jnp.bfloat16),
        ],
        compiler_params=vmem,
        name="classes",
    )(
        other, student_in, tags_in, cos, sin, heads[0], head_others, freqs_near, *weights
    )
    here_own, there_own = pl.pallas_call(
        functools.partial(keep_kernel, n_feat, n_dp, bits, permuted),
        out_shape=(jax.ShapeDtypeStruct((block, slots), jnp.float32),) * 2,
        scratch_shapes=[pltpu.VMEM((2 * block, half), jnp.bfloat16)],
        compiler_params=vmem,
        name="keep",
    )(*weights, freqs_near, grad_z)
    here = [here_own] + [shifted(grads[k - 1], k) for k in range(1, n_feat)]
    there = [there_own] + [shifted(grads[n_feat + k - 2], k) for k in range(1, n_feat)]
    folded = pl.pallas_call(
        fold_kernel,
        out_shape=jax.ShapeDtypeStruct((block, slots), jnp.bfloat16),
        compiler_params=vmem,
        name="fold",
    )(*there)
    there = [across(folded)]
    here, student_across = lax.optimization_barrier((here, student_across))
    scale = 1.0 / math.sqrt(images * n_dp)
    own, loss = pl.pallas_call(
        functools.partial(own_kernel, scale, 2.0 * half * n_feat),
        out_shape=(
            jax.ShapeDtypeStruct((block, d_s), jnp.float32),
            jax.ShapeDtypeStruct((cls_dev,), jnp.float32),
        ),
        compiler_params=vmem,
        name="own",
    )(*here, norms, student_in)
    partial_head = pl.pallas_call(
        functools.partial(head_kernel, scale),
        out_shape=jax.ShapeDtypeStruct((block, d_s), jnp.bfloat16),
        compiler_params=vmem,
        name="head",
    )(*there, own, student_across)
    received = lax.all_to_all(
        partial_head.reshape(n_dp // 2, out_rows, d_s),
        ("dp", "feat"),
        split_axis=0,
        concat_axis=0,
        tiled=True,
        axis_index_groups=[
            [d * n_feat + f for d in range(n_dp) if (d >> f % bits) % 2 == side]
            for f in range(n_feat)
            for side in range(2)
        ],
    )
    head_grad = pl.pallas_call(
        total_kernel,
        out_shape=jax.ShapeDtypeStruct((out_rows, d_s), jnp.float32),
        compiler_params=vmem,
        name="total",
    )(received)
    return (head_grad, loss)


def solution(mesh):
    in_specs = (P("dp", None), P("dp", None), P(None, "feat"), P(None, "feat"), P("dp"), P())
    out_specs = (P(("dp", "feat"), None), P("dp"))
    return jax.shard_map(
        on_device, mesh=mesh, in_specs=in_specs, out_specs=out_specs, check_vma=False
    )
```

```python
import functools
import math

import jax
import jax.numpy as jnp
from jax import lax
from jax.experimental import pallas as pl
from jax.experimental.pallas import tpu as pltpu
from jax.sharding import PartitionSpec as P

LANES = 128
CARRIED = 16
PIECES = 3
TURN = 1.0 / (2.0 * math.pi)
SINE = (6.283164044217864, -41.337142357601536, 81.3407683703199, -70.9934277613874)


def up_to(value, multiple):
    return -(-value // multiple) * multiple


def quarter_sine(angle):
    square = angle * angle
    value = jnp.float32(SINE[-1])
    for factor in SINE[-2::-1]:
        value = value * square + factor
    return value * angle


def cos_sin(z):
    turns = z * TURN
    part = turns - lax.round(turns, lax.RoundingMethod.TO_NEAREST_EVEN)
    wave = jnp.minimum(jnp.maximum(part, -0.5 - part), 0.5 - part)
    return quarter_sine(0.25 - jnp.abs(part)), quarter_sine(wave)


def to_row(column, size):
    first = lax.broadcasted_iota(jnp.int32, (size, size), 0)
    second = lax.broadcasted_iota(jnp.int32, (size, size), 1)
    return jnp.sum(jnp.where(first == second, column, 0.0), axis=0, keepdims=True)


def to_column(row, size):
    first = lax.broadcasted_iota(jnp.int32, (size, size), 0)
    second = lax.broadcasted_iota(jnp.int32, (size, size), 1)
    return jnp.sum(jnp.where(first == second, row, 0.0), axis=1, keepdims=True)


def table_entries(table, chunk):
    start = chunk * LANES
    size = min(LANES, table.shape[0] - start)
    entries = table[pl.ds(start, size)].astype(jnp.float32)
    if size < LANES:
        entries = jnp.concatenate([entries, jnp.zeros((LANES - size,), jnp.float32)])
    return entries.reshape(1, LANES)


def route_kernel(
    cls_dev, capacity, labels_in, table_in, teacher, student, out, token, labels, table, rows, sems
):
    images, d_t = teacher.shape
    d_s = student.shape[1]
    slots, width = out.shape
    copies = [
        pltpu.make_async_copy(labels_in, labels, sems.at[0]),
        pltpu.make_async_copy(table_in, table, sems.at[1]),
        pltpu.make_async_copy(teacher, rows.at[:, :d_t], sems.at[2]),
        pltpu.make_async_copy(student, rows.at[:, d_t : d_t + d_s], sems.at[3]),
    ]
    for copy in copies:
        copy.start()
    lane = lax.broadcasted_iota(jnp.int32, (images, LANES), 1)
    lane_f = lane.astype(jnp.float32)
    copies[0].wait()
    label = to_column(labels[...].astype(jnp.float32).reshape(1, images), images)
    label = jnp.broadcast_to(label, (images, LANES))
    copies[1].wait()
    found = jnp.zeros((images, LANES), jnp.float32)
    for chunk in range(pl.cdiv(table.shape[0], LANES)):
        entries = table_entries(table, chunk)
        found += jnp.where(lane_f + float(chunk * LANES) == label, entries, 0.0)
    position = jnp.sum(found, axis=1, keepdims=True)
    owner = jnp.floor((position + 0.5) * (1.0 / cls_dev))
    tag = position - owner * cls_dev + 1.0
    owner_row = to_row(owner, images)
    first = lax.broadcasted_iota(jnp.int32, (images, images), 0)
    second = lax.broadcasted_iota(jnp.int32, (images, images), 1)
    before = jnp.logical_and(first < second, owner == owner_row)
    rank = jnp.sum(jnp.where(before, 1.0, 0.0), axis=0, keepdims=True)
    slot = owner_row * float(capacity) + rank
    slot_id = lax.broadcasted_iota(jnp.int32, (slots, images), 0).astype(jnp.float32)
    pick = jnp.where(slot_id == slot, 1.0, 0.0).astype(jnp.bfloat16)
    high = jnp.floor(tag * (1.0 / 32.0))
    tags = jnp.where(lane == 0, high, jnp.where(lane == 1, tag - 32.0 * high, 0.0))
    rows[:, d_t + d_s : d_t + d_s + LANES] = tags.astype(jnp.bfloat16)
    rows[:, d_t + d_s + LANES :] = jnp.zeros(
        (images, rows.shape[1] - d_t - d_s - LANES), jnp.bfloat16
    )
    token[...] = jnp.zeros_like(token)
    copies[2].wait()
    copies[3].wait()
    start = pl.multiple_of(lax.axis_index("feat") * width, LANES)
    out[...] = jnp.dot(
        pick, rows[:, pl.ds(start, width)], preferred_element_type=jnp.float32
    ).astype(jnp.bfloat16)


def load_kernel(head_in, freqs_in, _, head, freqs, sems):
    copies = [
        pltpu.make_async_copy(head_in, head, sems.at[0]),
        pltpu.make_async_copy(freqs_in, freqs, sems.at[1]),
    ]
    for copy in copies:
        copy.start()
    for copy in copies:
        copy.wait()


def carry(norm, lanes):
    row = lax.broadcasted_iota(jnp.int32, (CARRIED, lanes), 0)
    block, index = jnp.zeros((CARRIED, lanes), jnp.float32), 0
    for _ in range(PIECES):
        piece = norm.astype(jnp.bfloat16).astype(jnp.float32)
        norm = norm - piece
        for start in range(0, norm.shape[1], lanes):
            block = jnp.where(row == index, piece[:, start : start + lanes], block)
            index += 1
    return block.astype(jnp.bfloat16)


def carried_norm(block, size):
    lanes = block.shape[1]
    values = block.astype(jnp.float32)
    width = size // lanes
    found = []
    for part in range(width):
        rows = [values[p * width + part : p * width + part + 1, :] for p in range(PIECES)]
        found.append(sum(rows[1:], rows[0]))
    return jnp.concatenate(found, axis=1) if width > 1 else found[0]


def lane_start(own, offset, count, part):
    if isinstance(own, int):
        return (own - offset) % count * part
    return pl.multiple_of(lax.rem(own + (count - offset), count) * part, LANES)


def holder_of(role, index):
    return index if role is None else lax.axis_index("feat")


def project(feat, student, head, others, projected):
    part = head.shape[1]
    count = projected.shape[1] // part
    for offset in range(count):
        weight = others[offset - 1] if offset else head[...]
        start = lane_start(feat, offset, count, part)
        projected[:, pl.ds(start, part)] = jnp.dot(
            student, weight, preferred_element_type=jnp.float32
        ).astype(jnp.bfloat16)


def products(inputs, freqs, step):
    return [
        jnp.dot(
            inputs[...], freqs[:, column : column + step], preferred_element_type=jnp.float32
        )
        for column in range(0, freqs.shape[1], step)
    ]


def is_role(role, index):
    return (lax.axis_index("feat") if role is None else role) == index


def first_kernel(role, n_feat, d_s, rows, *refs):
    heads, (freqs, cos, sin, near, inputs, sems) = refs[:n_feat], refs[n_feat:]
    is_student = is_role(role, 1)
    rows_each = d_s // PIECES
    copies = [
        [
            pltpu.make_async_copy(
                heads[k].at[pl.ds(piece * rows_each, rows_each)],
                near.at[k - 1, pl.ds(piece * rows_each, rows_each)],
                sems.at[k - 1, piece],
            )
            for piece in range(PIECES)
        ]
        for k in range(1, n_feat)
    ]
    for group in copies:
        for copy in group:
            copy.start()
    part = freqs.shape[0] // n_feat
    feat = holder_of(role, 1)
    own = lane_start(feat, 0, n_feat, part)

    @pl.when(is_student)
    def _():
        inputs[:, pl.ds(own, part)] = jnp.dot(
            rows[:, :d_s], heads[0][...], preferred_element_type=jnp.float32
        ).astype(jnp.bfloat16)

    @pl.when(jnp.logical_not(is_student))
    def _():
        inputs[...] = rows[...]

    step = min(freqs.shape[1], 256)
    blocks = [slice(c, c + step) for c in range(0, freqs.shape[1], step)]
    found = [0.0] * len(blocks)
    for offset in range(n_feat):
        start = lane_start(feat, offset, n_feat, part)
        if offset:

            @pl.when(is_student)
            def _():
                for copy in copies[offset - 1]:
                    copy.wait()
                inputs[:, pl.ds(start, part)] = jnp.dot(
                    rows[:, :d_s], near[offset - 1], preferred_element_type=jnp.float32
                ).astype(jnp.bfloat16)

        for index, block in enumerate(blocks):
            found[index] += jnp.dot(
                inputs[:, pl.ds(start, part)],
                freqs[pl.ds(start, part), block],
                preferred_element_type=jnp.float32,
            )
    for index, block in enumerate(blocks):
        cos[:, block], sin[:, block] = cos_sin(found[index])

    @pl.when(jnp.logical_not(is_student))
    def _():
        for group in copies:
            for copy in group:
                copy.wait()


def sort_kernel(mine, other, student, tags):
    d_s = student.shape[1]

    def split(rows):
        student[...] = rows[:, :d_s]
        tags[...] = rows[:, d_s : d_s + LANES]

    pl.when(is_role(None, 1))(lambda: split(mine))
    pl.when(is_role(None, 0))(lambda: split(other))


def member_of(group, bit, side):
    low = group * 2 + side
    high = group // 2 * 4 + side * 2 + group % 2
    return jnp.where(bit == 0, low, high)


def grad_rows(offset, sides, n_feat, n_dp, bits, weight, freqs, grad_z, picked):
    holder = lax.axis_index("dp")
    target = lax.rem(lax.axis_index("feat") + offset, n_feat)
    bit = lax.rem(target, bits)
    side = jnp.where(bit == 0, lax.rem(holder, 2), lax.rem(holder // 2, 2))
    half = n_dp // 2
    out_rows = picked.shape[0] // n_dp
    span = slice(sides[0] * half * out_rows, (sides[-1] + 1) * half * out_rows)
    if weight is not None:
        picked[span, :] = weight[span]
    else:
        for index in range(sides[0] * half, (sides[-1] + 1) * half):
            across, group = divmod(index, half)
            member = member_of(group, bit, 1 - side if across else side)
            start = pl.multiple_of((member * n_feat + target) * out_rows, out_rows)
            picked[index * out_rows : (index + 1) * out_rows, :] = freqs[
                pl.ds(start, out_rows), :
            ]
    return lax.dot_general(
        picked[span, :], grad_z[...], (((1,), (1,)), ((), ())), preferred_element_type=jnp.float32
    )


def class_kernel(
    role, n_feat, n_dp, bits, cls_pad, permuted, other, student, tags_in, cos, sin, *refs
):
    head, others, freqs, refs = refs[0], refs[1], refs[2], refs[3:]
    if permuted:
        weights, refs = refs[0], refs[1:]
    grads, refs = refs[: n_feat - 1], refs[n_feat - 1 :]
    norms, grad_z, inputs, picked = refs
    mine_student = is_role(role, 1)
    slots, d_t = inputs.shape
    half = freqs.shape[1]

    @pl.when(mine_student)
    def _():
        inputs[...] = other[...]

    @pl.when(jnp.logical_not(mine_student))
    def _():
        project(holder_of(role, 0), student[...], head, others, inputs)

    tags = tags_in[...].astype(jnp.float32)
    lane = lax.broadcasted_iota(jnp.int32, (slots, LANES), 1)
    tag = jnp.sum(
        tags * jnp.where(lane == 0, 32.0, jnp.where(lane == 1, 1.0, 0.0)), axis=1, keepdims=True
    )
    tag_row = to_row(tag, slots)
    same = jnp.where(jnp.logical_and(tag == tag_row, tag > 0.0), 1.0, 0.0)
    inverse = 1.0 / jnp.maximum(jnp.sum(same, axis=1, keepdims=True), 1.0)
    inverse = jnp.where(mine_student, -inverse, inverse)
    same = same.astype(jnp.bfloat16)
    step = min(half, 256)
    norm = jnp.zeros((slots, 1), jnp.float32)
    for index, z in enumerate(products(inputs, freqs, step)):
        block = slice(index * step, (index + 1) * step)
        cos_mine, sin_mine = cos[:, block], sin[:, block]
        cos_other, sin_other = cos_sin(z)
        mean_c = inverse * jnp.dot(
            same, (cos_other - cos_mine).astype(jnp.bfloat16), preferred_element_type=jnp.float32
        )
        mean_s = inverse * jnp.dot(
            same, (sin_other - sin_mine).astype(jnp.bfloat16), preferred_element_type=jnp.float32
        )
        norm += jnp.sum(mean_c * mean_c + mean_s * mean_s, axis=1, keepdims=True)
        cos_s = jnp.where(mine_student, cos_mine, cos_other)
        sin_s = jnp.where(mine_student, sin_mine, sin_other)
        grad_z[:, block] = (cos_s * mean_s - sin_s * mean_c).astype(jnp.bfloat16)
    cls = lax.broadcasted_iota(jnp.int32, (slots, cls_pad), 1).astype(jnp.float32) + 1.0
    total_norm = jnp.sum(jnp.where(cls == tag, norm, 0.0), axis=0, keepdims=True)
    norms[...] = total_norm
    for offset in range(1, n_feat):
        weight = weights[offset] if permuted else None
        product = grad_rows(offset, (1,), n_feat, n_dp, bits, weight, freqs, grad_z, picked)
        grads[offset - 1][...] = product.astype(jnp.bfloat16)


def keep_kernel(n_feat, n_dp, bits, permuted, *refs):
    weights, (freqs, grad_z, norms, *heres, there, picked) = refs[:permuted], refs[permuted:]
    block = picked.shape[0] // 2
    for offset in range(n_feat):
        weight = weights[0][offset] if permuted else None
        sides = (0,) if offset else (0, 1)
        product = grad_rows(offset, sides, n_feat, n_dp, bits, weight, freqs, grad_z, picked)
        here = heres[offset]
        here[:block, :] = product[:block].astype(here.dtype)
        if offset:
            here[block:, :] = carry(norms[...], here.shape[1])
        else:
            there[...] = product[block:]


def summed(refs, size):
    total = refs[0][:size, :].astype(jnp.float32)
    for ref in refs[1:]:
        total += ref[:size, :].astype(jnp.float32)
    return total.astype(jnp.bfloat16)


def fold_kernel(*refs):
    refs[-1][...] = summed(refs[:-1], refs[-1].shape[0])


def own_kernel(scale, divisor, *refs):
    grads, (norms, student, head, loss) = refs[:-4], refs[-4:]
    head[...] = scale * jnp.dot(
        summed(grads, head.shape[0]), student[...], preferred_element_type=jnp.float32
    )
    norm = norms[...]
    for ref in grads[1:]:
        norm += carried_norm(ref[ref.shape[0] - CARRIED :, :], norm.shape[1])
    loss[...] = (norm * (1.0 / divisor))[0, : loss.shape[0]]


def head_kernel(scale, *refs):
    grads, (own, student, head) = refs[:-3], refs[-3:]
    product = jnp.dot(
        summed(grads, head.shape[0]), student[...], preferred_element_type=jnp.float32
    )
    head[...] = (own[...] + product * scale).astype(jnp.bfloat16)


def total_kernel(parts, out):
    out[...] = jnp.sum(parts[...].astype(jnp.float32), axis=0)


def on_device(teacher, student, head, freqs, labels, class_slot):
    n_dp = lax.axis_size("dp")
    n_feat = lax.axis_size("feat")
    images, d_t = teacher.shape
    d_s = student.shape[1]
    half = freqs.shape[1]
    classes = class_slot.shape[0]
    cls_dev = classes // n_dp
    capacity = 2 * images // n_dp
    slots = n_dp * capacity
    cls_pad = up_to(cls_dev, slots)
    width = up_to(d_t + d_s + LANES, LANES * n_feat) // n_feat
    out_rows = d_t // (n_dp * n_feat)
    bits = 2 if n_dp % 4 == 0 else 1
    block = n_dp // 2 * out_rows
    vmem = pltpu.CompilerParams(vmem_limit_bytes=20 * 2**20)
    hbm = pl.BlockSpec(memory_space=pltpu.HBM)
    near = pl.BlockSpec(memory_space=pltpu.VMEM)

    def across(value, offset=0):
        moves = [
            (d * n_feat + f, (d ^ (1 << (f + offset) % n_feat % bits)) * n_feat + (f + offset) % n_feat)
            for d in range(n_dp)
            for f in range(n_feat)
        ]
        return lax.ppermute(value, ("dp", "feat"), moves)

    def shifted(value, offset):
        return lax.ppermute(
            value, "feat", [(f, (f + offset) % n_feat) for f in range(n_feat)]
        )

    sent, token = pl.pallas_call(
        functools.partial(route_kernel, cls_dev, capacity),
        out_shape=(
            jax.ShapeDtypeStruct((slots, width), jnp.bfloat16),
            jax.ShapeDtypeStruct((8, LANES), jnp.float32),
        ),
        in_specs=[hbm] * 4,
        scratch_shapes=[
            pltpu.VMEM((images,), jnp.int32),
            pltpu.VMEM((classes,), jnp.int32),
            pltpu.VMEM((images, width * n_feat), jnp.bfloat16),
            pltpu.SemaphoreType.DMA((4,)),
        ],
        compiler_params=pltpu.CompilerParams(vmem_limit_bytes=60 * 2**20),
        name="route",
    )(labels, class_slot, teacher, student)
    permuted = out_rows % 16 != 0
    weights = []
    if permuted:
        targets = (lax.axis_index("feat") + jnp.arange(n_feat)) % n_feat
        bit = (targets % bits)[:, None]
        group = jnp.tile(jnp.arange(n_dp // 2), 2)[None, :]
        side = (lax.axis_index("dp") >> bit) % 2
        side = jnp.where(jnp.arange(n_dp)[None, :] >= n_dp // 2, 1 - side, side)
        member = member_of(group, bit, side)
        lines = (member * n_feat + targets[:, None])[:, :, None] * out_rows + jnp.arange(out_rows)
        weights = [jnp.take(freqs, lines.reshape(n_feat, 2 * block), axis=0)]
    head_near, freqs_near = pl.pallas_call(
        load_kernel,
        out_shape=(
            jax.ShapeDtypeStruct(head.shape, jnp.bfloat16),
            jax.ShapeDtypeStruct(freqs.shape, jnp.bfloat16),
        ),
        in_specs=[hbm] * 3,
        scratch_shapes=[pltpu.SemaphoreType.DMA((2,))],
        compiler_params=vmem,
        name="load",
    )(head, freqs, token)
    heads = [head_near] + [shifted(head_near, k) for k in range(1, n_feat)]
    mine = lax.all_to_all(
        sent.reshape(n_dp, capacity, width), "dp", split_axis=0, concat_axis=0, tiled=True
    ).reshape(slots, width)
    role = None
    if n_feat == 2 and width == d_t:
        other = shifted(mine, 1)
        student_in, tags_in = pl.pallas_call(
            sort_kernel,
            out_shape=(
                jax.ShapeDtypeStruct((slots, d_s), jnp.bfloat16),
                jax.ShapeDtypeStruct((slots, LANES), jnp.bfloat16),
            ),
            compiler_params=vmem,
            name="sort",
        )(mine, other)
    else:
        role = 0
        everything = lax.all_gather(mine, "feat", axis=1, tiled=True)
        mine, student_in, tags_in = jnp.split(
            everything[:, : d_t + d_s + LANES], [d_t, d_t + d_s], axis=1
        )
        other = mine
    cos, sin, head_others = pl.pallas_call(
        functools.partial(first_kernel, role, n_feat, d_s),
        out_shape=(jax.ShapeDtypeStruct((slots, half), jnp.float32),) * 2
        + (jax.ShapeDtypeStruct((n_feat - 1, *head.shape), jnp.bfloat16),),
        in_specs=[near] * 2 + [hbm] * (n_feat - 1) + [near],
        scratch_shapes=[
            pltpu.VMEM((slots, d_t), jnp.bfloat16),
            pltpu.SemaphoreType.DMA((n_feat - 1, PIECES)),
        ],
        compiler_params=vmem,
        name="first",
    )(mine, *heads, freqs_near)
    cos, student_out = lax.optimization_barrier((cos, student_in))
    student_across = across(student_out)
    *grads, norms, grad_z = pl.pallas_call(
        functools.partial(class_kernel, role, n_feat, n_dp, bits, cls_pad, permuted),
        out_shape=(jax.ShapeDtypeStruct((block, slots), jnp.bfloat16),) * (n_feat - 1)
        + (
            jax.ShapeDtypeStruct((1, cls_pad), jnp.float32),
            jax.ShapeDtypeStruct((slots, half), jnp.bfloat16),
        ),
        in_specs=[near] * (8 + len(weights)),
        scratch_shapes=[
            pltpu.VMEM((slots, d_t), jnp.bfloat16),
            pltpu.VMEM((2 * block, half), jnp.bfloat16),
        ],
        compiler_params=vmem,
        name="classes",
    )(
        other, student_in, tags_in, cos, sin, heads[0], head_others, freqs_near, *weights
    )
    own_block = jax.ShapeDtypeStruct((block, slots), jnp.float32)
    sent_block = jax.ShapeDtypeStruct((block + CARRIED, slots), jnp.bfloat16)
    here_own, *here_others, there_own = pl.pallas_call(
        functools.partial(keep_kernel, n_feat, n_dp, bits, int(permuted)),
        out_shape=(own_block,) + (sent_block,) * (n_feat - 1) + (own_block,),
        scratch_shapes=[pltpu.VMEM((2 * block, half), jnp.bfloat16)],
        compiler_params=vmem,
        name="keep",
    )(*weights, freqs_near, grad_z, norms)
    here = [here_own] + [shifted(here_others[k - 1], k) for k in range(1, n_feat)]
    there = [there_own] + [shifted(grads[k - 1], k) for k in range(1, n_feat)]
    folded = pl.pallas_call(
        fold_kernel,
        out_shape=jax.ShapeDtypeStruct((block, slots), jnp.bfloat16),
        compiler_params=vmem,
        name="fold",
    )(*there)
    there = [across(folded)]
    here, student_across = lax.optimization_barrier((here, student_across))
    scale = 1.0 / math.sqrt(images * n_dp)
    own, loss = pl.pallas_call(
        functools.partial(own_kernel, scale, 2.0 * half * n_feat),
        out_shape=(
            jax.ShapeDtypeStruct((block, d_s), jnp.float32),
            jax.ShapeDtypeStruct((cls_dev,), jnp.float32),
        ),
        compiler_params=vmem,
        name="own",
    )(*here, norms, student_in)
    partial_head = pl.pallas_call(
        functools.partial(head_kernel, scale),
        out_shape=jax.ShapeDtypeStruct((block, d_s), jnp.bfloat16),
        compiler_params=vmem,
        name="head",
    )(*there, own, student_across)
    received = lax.all_to_all(
        partial_head.reshape(n_dp // 2, out_rows, d_s),
        ("dp", "feat"),
        split_axis=0,
        concat_axis=0,
        tiled=True,
        axis_index_groups=[
            [d * n_feat + f for d in range(n_dp) if (d >> f % bits) % 2 == side]
            for f in range(n_feat)
            for side in range(2)
        ],
    )
    head_grad = pl.pallas_call(
        total_kernel,
        out_shape=jax.ShapeDtypeStruct((out_rows, d_s), jnp.float32),
        compiler_params=vmem,
        name="total",
    )(received)
    return (head_grad, loss)


def solution(mesh):
    in_specs = (P("dp", None), P("dp", None), P(None, "feat"), P(None, "feat"), P("dp"), P())
    out_specs = (P(("dp", "feat"), None), P("dp"))
    return jax.shard_map(
        on_device, mesh=mesh, in_specs=in_specs, out_specs=out_specs, check_vma=False
    )
```
